256 devices in a mesh: section: 8 (over z_lo, core), dp: 32 (over z_hi, y, x).
Axes of the slice: x: 4, y: 4, z: 8 (z_hi: 2, z_lo: 4; z = z_hi * 4 + z_lo), core: 2. Of those that a mesh axis runs over, the one named last changes fastest.
Arguments:
- tokens: bfloat16 [2, 32, 256, 2048], P(None, 'dp'), may hold values from -0.14941406 to 0.14941406
- cotangent: bfloat16 [2, 32, 256, 2048], P(None, 'dp'), may hold values from -6 to 6
- inflow: bfloat16 [8, 32, 256, 2048], P('section', 'dp'), may hold values from -0.14941406 to 0.14941406
- backflow: bfloat16 [8, 32, 256, 2048], P('section', 'dp'), may hold values from -6 to 6
- norm_gain: float32 [8, 2048], P('section'), may hold values from 0.5 to 1.5
- slot_scale: float32 [8], P('section'), may hold values from 20 to 60
- router_weight: bfloat16 [8, 2048, 128], P('section', None, 'dp'), may hold values from -6 to 6
- expert_in: bfloat16 [8, 2048, 8192], P('section', None, 'dp'), may hold values from -2 to 2
- expert_back: bfloat16 [8, 8192, 2048], P('section', 'dp'), may hold values from -0.0625 to 0.0625
Outputs:
- section_grads: bfloat16 [8, 2, 32, 256, 2048], P('section', None, 'dp')
- slot_out: bfloat16 [8, 2, 32, 2048], P('section', None, 'dp')
- slot_grad: bfloat16 [8, 2, 32, 2048], P('section', None, 'dp')
- expert_in_grad: bfloat16 [8, 2048, 8192], P('section', None, 'dp')
- expert_back_grad: bfloat16 [8, 8192, 2048], P('section', 'dp')
- router_grad: bfloat16 [8, 2048, 128], P('section', None, 'dp')
- gain_grad: float32 [8, 2048], P('section')
The draws below stay inside these ranges and needn't reach their ends.
All inputs are finite; a program needn't handle non-finite values.
Results may differ from the reference program's by a relative error of at most 0.039.
Values may be sent and summed in bfloat16 or wider, within the bound.
No kernel may reach another device: no remote copies, remote signals or barrier semaphores. Data moves between devices by JAX's collectives and lax.ppermute only.
A program may use at most 64 MiB of HBM per device.

```python
import math
import jax
import jax.numpy as jnp
from jax import lax

D = 2048
FF = 8192
EXPERTS = 128
PATCHES = 256
MICRO = 2
LAYERS = 8
IMAGES = 32


def shard_levels(stream_key, shape, pieces, least, high):
    def one(position, blocks):
        heights = jax.random.uniform(jax.random.fold_in(jax.random.fold_in(stream_key, 6), position), (blocks,), jnp.float32, least / len(pieces), high / len(pieces))
        return jnp.repeat(jnp.exp(heights), shape[position] // blocks).reshape((-1,) + (1,) * (len(shape) - position - 1))

    level = one(*pieces[0])
    for cut in pieces[1:]:
        level = level * one(*cut)
    return level


def gaussian(stream_key, dims, scale, most, split=(), kind=jnp.bfloat16):
    factor_of = shard_levels(stream_key, dims, split, -0.22, 0.18) if split else 1.0
    drawn = jax.random.normal(stream_key, dims, jnp.float32) * scale * factor_of
    return jnp.minimum(jnp.maximum(drawn, -most), most).astype(kind)


def setup_inputs(seed: int = 0) -> dict:
    key_list = jax.random.split(jax.random.key(seed), 10)
    return {
        "tokens": gaussian(key_list[0], (MICRO, IMAGES, PATCHES, D), 0.025, 0.14941406, ((1, 32),)),
        "cotangent": gaussian(key_list[1], (MICRO, IMAGES, PATCHES, D), 1.0, 6.0, ((1, 32),)),
        "inflow": gaussian(key_list[2], (LAYERS, IMAGES, PATCHES, D), 0.025, 0.14941406, ((0, 8), (1, 32))),
        "backflow": gaussian(key_list[3], (LAYERS, IMAGES, PATCHES, D), 1.0, 6.0, ((0, 8), (1, 32))),
        "norm_gain": jnp.clip(1.0 + 0.1 * jax.random.normal(key_list[4], (LAYERS, D), jnp.float32), 0.5, 1.5),
        "slot_scale": jnp.clip(jnp.exp(math.log(60.0) - 1.0986123 * jax.random.uniform(key_list[5], (LAYERS,), jnp.float32) ** shard_levels(key_list[5], (LAYERS,), ((0, 8),), -0.2, 0.2)), 20.0, 60.0),
        "router_weight": gaussian(key_list[6], (LAYERS, D, EXPERTS), 1.0, 6.0, ((0, 8), (2, 32))),
        "expert_in": gaussian(key_list[7], (LAYERS, D, FF), (D // PATCHES) ** -0.5, 2.0, ((0, 8), (2, 32))),
        "expert_back": gaussian(key_list[8], (LAYERS, FF, D), FF ** -0.5, 0.0625, ((0, 8), (1, 32))),
    }


EPSILON = 1e-06
precise = lax.Precision.HIGHEST

def norm_tokens(act_in, gain_row):
    meansq = lax.optimization_barrier(jnp.mean(act_in * act_in, axis=-1, keepdims=True))
    return act_in * lax.rsqrt(meansq + EPSILON) * gain_row

def normalize_cols(weights):
    wide = weights.astype(jnp.float32)
    return wide * lax.rsqrt(lax.optimization_barrier(jnp.sum(wide * wide, axis=0, keepdims=True)) + EPSILON)

def mix_slots(hidden, scores, scale_val):
    sumsq = lax.optimization_barrier(jnp.sum(hidden * hidden, axis=-1, keepdims=True))
    logits = scale_val * scores * lax.rsqrt(sumsq + EPSILON)
    expo = jnp.exp(logits)
    first_col = expo[..., 0]
    combine = first_col / lax.optimization_barrier(jnp.sum(expo, axis=-1))
    dispatch = (first_col / lax.optimization_barrier(jnp.sum(first_col, axis=-1, keepdims=True))).astype(jnp.bfloat16)
    slot_rows = jnp.einsum('ip,ipd->id', dispatch.astype(jnp.float32), hidden, precision=precise)
    return (slot_rows.astype(jnp.bfloat16), combine)

def dot_last(left_side, right_side):
    return lax.dot_general(left_side, right_side, (((1,), (1,)), ((), ())), preferred_element_type=jnp.float32)

def dot_rows(left_side, right_side):
    return lax.dot_general(left_side, right_side, (((0,), (0,)), ((), ())), preferred_element_type=jnp.float32)

def front_parts(section_in, gain_row, columns):
    normed, pull_norm = jax.vjp(norm_tokens, section_in.astype(jnp.float32), gain_row)
    hidden_bf = normed.astype(jnp.bfloat16)
    model_width = hidden_bf.shape[-1]
    scores = jnp.dot(hidden_bf.reshape(-1, model_width), columns, preferred_element_type=jnp.float32)
    scores = scores.reshape(hidden_bf.shape[:-1] + (columns.shape[1],))
    return (hidden_bf, hidden_bf.astype(jnp.float32), scores, pull_norm)

def reference(tokens, cotangent, inflow, backflow, norm_gain, slot_scale, router_weight, expert_in, expert_back):
    layer_count = norm_gain.shape[0]
    micro_count = tokens.shape[0]
    model_width = tokens.shape[3]
    columns = [normalize_cols(router_weight[index]).astype(jnp.bfloat16) for index in range(layer_count)]
    first_acc = [jnp.zeros(expert_in.shape[1:], jnp.float32) for index in range(layer_count)]
    second_acc = [jnp.zeros(expert_back.shape[1:], jnp.float32) for index in range(layer_count)]
    router_acc = [jnp.zeros(router_weight.shape[1:], jnp.float32) for index in range(layer_count)]
    gain_acc = [jnp.zeros(norm_gain.shape[1:], jnp.float32) for index in range(layer_count)]
    grads_rows = [[None for index in range(micro_count)] for other in range(layer_count)]
    outs_rows = [[None for index in range(micro_count)] for other in range(layer_count)]
    slot_rows_grad = [[None for index in range(micro_count)] for other in range(layer_count)]
    saved_all = [[None for index in range(micro_count)] for other in range(layer_count)]
    layer_outs = [[None for index in range(micro_count)] for other in range(layer_count)]
    for round_index in range(micro_count):
        for layer_index in range(layer_count):
            if layer_index == 0:
                current = tokens[round_index]
            elif round_index == 0:
                current = inflow[layer_index]
            else:
                current = layer_outs[layer_index - 1][round_index - 1]
            hidden_bf, hidden, scores, pull_norm = front_parts(current, norm_gain[layer_index], columns[layer_index])
            slot_rows, combine = mix_slots(hidden, scores, slot_scale[layer_index])
            pre_act = jnp.dot(slot_rows, expert_in[layer_index], preferred_element_type=jnp.float32)
            activation = jax.nn.gelu(pre_act).astype(jnp.bfloat16)
            mixed_out = jnp.dot(activation, expert_back[layer_index], preferred_element_type=jnp.float32).astype(jnp.bfloat16)
            saved_all[layer_index][round_index] = (current, slot_rows, pre_act, activation, mixed_out, combine)
            outs_rows[layer_index][round_index] = mixed_out
            layer_outs[layer_index][round_index] = (current.astype(jnp.float32) + combine[..., None] * mixed_out.astype(jnp.float32)[:, None, :]).astype(jnp.bfloat16)
    for round_index in reversed(range(micro_count)):
        for layer_index in reversed(range(layer_count)):
            if layer_index == layer_count - 1:
                upstream = cotangent[round_index]
            elif round_index == micro_count - 1:
                upstream = backflow[layer_index]
            else:
                upstream = grads_rows[layer_index + 1][round_index + 1]
            section_in, slot_rows, pre_act, activation, mixed_out, combine = saved_all[layer_index][round_index]
            upstream_f = upstream.astype(jnp.float32)
            dmixed = jnp.einsum('ip,ipd->id', combine, upstream_f, precision=precise).astype(jnp.bfloat16)
            back_hidden = dot_last(dmixed, expert_back[layer_index])
            gelu_pull = jax.vjp(jax.nn.gelu, pre_act)[1]
            pre_grad = gelu_pull(back_hidden)[0].astype(jnp.bfloat16)
            slot_back = dot_last(pre_grad, expert_in[layer_index]).astype(jnp.bfloat16)
            dcombine = jnp.einsum('ipd,id->ip', upstream_f, mixed_out.astype(jnp.float32), precision=precise)
            hidden_bf, hidden, scores, pull_norm = front_parts(section_in, norm_gain[layer_index], columns[layer_index])
            scale_val = slot_scale[layer_index]
            pull_mix = jax.vjp(lambda left_side, right_side: mix_slots(left_side, right_side, scale_val), hidden, scores)[1]
            dhidden, dscores = pull_mix((slot_back, dcombine))
            dscores_bf = dscores.astype(jnp.bfloat16).reshape(-1, dscores.shape[-1])
            dhidden = dhidden + dot_last(dscores_bf, columns[layer_index]).reshape(dhidden.shape)
            router_acc[layer_index] = router_acc[layer_index] + dot_rows(hidden_bf.reshape(-1, model_width), dscores_bf)
            dinput, dgain = pull_norm(dhidden)
            gain_acc[layer_index] = gain_acc[layer_index] + dgain
            first_acc[layer_index] = first_acc[layer_index] + dot_rows(slot_rows, pre_grad)
            second_acc[layer_index] = second_acc[layer_index] + dot_rows(activation, dmixed)
            grads_rows[layer_index][round_index] = (upstream_f + dinput).astype(jnp.bfloat16)
            slot_rows_grad[layer_index][round_index] = slot_back
    router_out = []
    for layer_index in range(layer_count):
        pull_cols = jax.vjp(normalize_cols, router_weight[layer_index])[1]
        router_out.append(pull_cols(router_acc[layer_index])[0].astype(jnp.bfloat16))
    section_grads = jnp.stack([jnp.stack(row) for row in grads_rows])
    slot_out = jnp.stack([jnp.stack(row) for row in outs_rows])
    slot_grad = jnp.stack([jnp.stack(row) for row in slot_rows_grad])
    expert_in_grad = jnp.stack(first_acc).astype(jnp.bfloat16)
    expert_back_grad = jnp.stack(second_acc).astype(jnp.bfloat16)
    router_grad = jnp.stack(router_out)
    gain_grad = jnp.stack(gain_acc)
    return (section_grads, slot_out, slot_grad, expert_in_grad, expert_back_grad, router_grad, gain_grad)
```

```python
import jax
import jax.numpy as jnp
from jax import lax
from jax.sharding import Mesh
from jax.sharding import PartitionSpec as P

EPSILON = 1e-06
BF = jnp.bfloat16
F32 = jnp.float32
AXES = ("section", "zh", "y", "x")
DP = ("zh", "y", "x")


def dot_last(left_side, right_side):
    return lax.dot_general(
        left_side, right_side, (((1,), (1,)), ((), ())), preferred_element_type=F32
    )


def dot_rows(left_side, right_side):
    return lax.dot_general(
        left_side, right_side, (((0,), (0,)), ((), ())), preferred_element_type=F32
    )


def dot_plain(left_side, right_side):
    return jnp.dot(left_side, right_side, preferred_element_type=F32)


def split_wide(value):
    high = lax.reduce_precision(value, 8, 7)
    return high.astype(BF), (value - high).astype(BF)


def exchange(chunks, axes):
    return lax.all_to_all(chunks, axes, 0, 0, tiled=True)


def gather(rows, axes):
    count = lax.axis_size(axes)
    return exchange(jnp.broadcast_to(rows[None], (count,) + rows.shape), axes)


def section_shift(block, distance):
    sections = lax.axis_size("section")
    route = [(i, i + distance) for i in range(sections) if 0 <= i + distance < sections]
    return lax.ppermute(block, "section", route)


def front(section_in, gain_row, columns, scale_val):
    wide = section_in.astype(F32)
    inverse = lax.rsqrt(jnp.mean(wide * wide, axis=-1, keepdims=True) + EPSILON)
    hidden = (wide * inverse * gain_row).astype(BF)
    hidden_f = hidden.astype(F32)
    product = dot_last(hidden, columns)
    inv_len = lax.rsqrt(jnp.sum(hidden_f * hidden_f, axis=-1, keepdims=True) + EPSILON)
    logits = scale_val * product * inv_len
    expo = jnp.exp(logits)
    first = expo[:, :1]
    norm = jnp.sum(expo, axis=-1, keepdims=True)
    spread = first / jnp.sum(first, axis=0, keepdims=True)
    slot = dot_rows(spread.astype(BF), hidden).astype(BF)
    return dict(
        wide=wide,
        inverse=inverse,
        hidden=hidden,
        inv_len=inv_len,
        logits=logits,
        prob=expo / norm,
        combine=first / norm,
        spread=spread,
        slot=slot,
    )


def mix_upstream(combine, upstream):
    high, low = split_wide(combine)
    pair = dot_rows(jnp.concatenate([high, low], axis=1), upstream)
    return (pair[:1] + pair[1:]).astype(BF)


def back(saved, gain_row, columns, scale_val, upstream, slot_out, slot_grad):
    combine = saved["combine"]
    spread = saved["spread"]
    hidden = saved["hidden"]
    dcombine = dot_last(upstream, slot_out)
    dspread = dot_last(hidden, slot_grad).astype(BF).astype(F32)
    first_term = spread * (dspread - jnp.sum(dspread * spread, axis=0, keepdims=True))
    mixed = combine * dcombine
    is_first = lax.broadcasted_iota(jnp.int32, saved["prob"].shape, 1) == 0
    dlogits = jnp.where(is_first, mixed + first_term, 0.0) - saved["prob"] * mixed
    dproduct = (dlogits * scale_val * saved["inv_len"]).astype(BF)
    pull = jnp.sum(dlogits * saved["logits"], axis=-1, keepdims=True)
    pull = pull * saved["inv_len"] * saved["inv_len"]
    spread_bf = spread.astype(BF).astype(F32)
    dhidden = (
        spread_bf * slot_grad.astype(F32)
        - hidden.astype(F32) * pull
        + dot_plain(dproduct, columns)
    )
    scaled = saved["wide"] * saved["inverse"]
    gain_part = jnp.sum(dhidden * scaled, axis=0, keepdims=True)
    through = dhidden * gain_row
    mean_term = jnp.mean(through * scaled, axis=-1, keepdims=True)
    dinput = saved["inverse"] * (through - scaled * mean_term)
    grads = (upstream.astype(F32) + dinput).astype(BF)
    router_part = dot_rows(dproduct, hidden)
    return grads, router_part, gain_part


def shards(
    tokens,
    cotangent,
    inflow,
    backflow,
    norm_gain,
    slot_scale,
    router_weight,
    expert_in,
    expert_back,
):
    section_index = lax.axis_index("section")
    is_first = section_index == 0
    is_last = section_index == lax.axis_size("section") - 1
    group = lax.axis_size(DP)
    width = tokens.shape[3]
    gain_row = norm_gain
    scale_val = slot_scale[0]
    first_weight = expert_in[0]
    second_weight = expert_back[0]
    weights = router_weight[0].T.astype(F32)
    weight_inv = lax.rsqrt(jnp.sum(weights * weights, axis=1, keepdims=True) + EPSILON)
    local_cols = (weights * weight_inv).astype(BF)

    start_in = jnp.where(is_first, tokens[0, 0], inflow[0, 0])
    sent_in = section_shift(start_in, 1)
    columns = gather(local_cols, DP).reshape(-1, width)

    early = front(start_in, gain_row, columns, scale_val)
    slot_early = gather(early["slot"], DP).reshape(group, width)
    pre_early = dot_plain(slot_early, first_weight)
    act_early, pull_early = jax.vjp(jax.nn.gelu, pre_early)
    act_early = act_early.astype(BF)
    part = dot_plain(act_early, second_weight)

    sums_early = exchange(part.reshape(group, 1, width), DP).reshape(group, width).sum(0)
    out_early = sums_early[None].astype(BF)
    flat_comb = early["combine"].reshape(1, -1)
    moved = section_shift(jnp.concatenate([out_early.astype(F32), flat_comb], axis=1), 1)
    out_before = moved[:, :width].astype(BF)
    comb_before = moved[:, width:].reshape(-1, 1)

    relayed = (sent_in.astype(F32) + comb_before * out_before.astype(F32)).astype(BF)
    late_in = jnp.where(is_first, tokens[1, 0], relayed)
    late = front(late_in, gain_row, columns, scale_val)
    late_up = jnp.where(is_last, cotangent[1, 0], backflow[0, 0])
    dmixed_late = mix_upstream(late["combine"], late_up)
    pair = jnp.concatenate([late["slot"], dmixed_late], axis=0)
    pairs = gather(pair, DP).reshape(group, 2, width)
    slot_late = pairs[:, 0]
    dmixed_late_all = pairs[:, 1]
    pre_late = dot_plain(slot_late, first_weight)
    act_late, pull_late = jax.vjp(jax.nn.gelu, pre_late)
    act_late = act_late.astype(BF)
    pre_grad_late = pull_late(dot_last(dmixed_late_all, second_weight))[0].astype(BF)
    part_out = dot_plain(act_late, second_weight)
    part_grad = dot_last(pre_grad_late, first_weight)
    parts = jnp.stack([part_out, part_grad], axis=1)
    sums = exchange(parts, DP).reshape(group, 2, width).sum(0)
    out_late = sums[:1].astype(BF)
    slot_grad_late = sums[1:].astype(BF)
    grads_late, router_late, gain_late = back(
        late, gain_row, columns, scale_val, late_up, out_late, slot_grad_late
    )

    dmixed_last = mix_upstream(early["combine"], cotangent[0, 0])
    dmixed_before = mix_upstream(comb_before, grads_late)
    moved_back = section_shift(dmixed_before, -1)
    sent_grads = section_shift(grads_late, -1)
    dmixed_early = jnp.where(is_last, dmixed_last, moved_back)
    dmixed_early_all = gather(dmixed_early, DP).reshape(group, width)
    pre_grad_early = pull_early(dot_last(dmixed_early_all, second_weight))[0].astype(BF)
    part_early = dot_last(pre_grad_early, first_weight)
    slot_grad_early = (
        exchange(part_early.reshape(group, 1, width), DP).reshape(group, width).sum(0)
    ).astype(BF)[None]
    early_up = jnp.where(is_last, cotangent[0, 0], sent_grads)
    grads_early, router_early, gain_early = back(
        early, gain_row, columns, scale_val, early_up, out_early, slot_grad_early
    )

    router_sum = (router_late + router_early).astype(BF).reshape(group, -1, width)
    gain_high, gain_low = split_wide(gain_late + gain_early)
    gain_pair = jnp.broadcast_to(
        jnp.concatenate([gain_high, gain_low], axis=0)[None], (group, 2, width)
    )
    finals = exchange(jnp.concatenate([router_sum, gain_pair], axis=1), DP)
    finals = finals.reshape(group, -1, width).astype(F32).sum(0)
    local = router_weight.shape[2]
    gain_total = finals[local : local + 1] + finals[local + 1 :]
    pulled = finals[:local]
    dots = jnp.sum(pulled * weights, axis=1, keepdims=True)
    router_grad = weight_inv * (pulled - weights * (dots * weight_inv * weight_inv))

    first_grad = dot_rows(
        jnp.concatenate([slot_early, slot_late], axis=0),
        jnp.concatenate([pre_grad_early, pre_grad_late], axis=0),
    )
    second_grad = dot_rows(
        jnp.concatenate([act_early, act_late], axis=0),
        jnp.concatenate([dmixed_early_all, dmixed_late_all], axis=0),
    )
    return (
        jnp.stack([grads_early, grads_late])[None, :, None],
        jnp.stack([out_early, out_late])[None],
        jnp.stack([slot_grad_early, slot_grad_late])[None],
        first_grad.astype(BF)[None],
        second_grad.astype(BF)[None],
        router_grad.astype(BF).T[None],
        gain_total,
    )


def solution(mesh):
    fine = Mesh(mesh.devices.reshape(mesh.shape["section"], 2, 4, 4), AXES)
    in_specs = (
        P(None, DP, None, None),
        P(None, DP, None, None),
        P("section", DP, None, None),
        P("section", DP, None, None),
        P("section", None),
        P("section"),
        P("section", None, DP),
        P("section", None, DP),
        P("section", DP, None),
    )
    out_specs = (
        P("section", None, DP, None, None),
        P("section", None, DP, None),
        P("section", None, DP, None),
        P("section", None, DP),
        P("section", DP, None),
        P("section", None, DP),
        P("section", None),
    )
    return jax.shard_map(shards, mesh=fine, in_specs=in_specs, out_specs=out_specs, check_vma=False)
```

```python
import jax
import jax.numpy as jnp
from jax import lax
from jax.experimental import pallas as pl
from jax.experimental.pallas import tpu as pltpu
from jax.sharding import Mesh
from jax.sharding import PartitionSpec as P

EPSILON = 1e-06
BF = jnp.bfloat16
F32 = jnp.float32
AXES = ("section", "zh", "y", "x")
DP = ("zh", "y", "x")
LANES = 128
STEP = 16
VMEM_BYTES = 32 * 1024 * 1024


def dot_dims(left_side, right_side, left_dim, right_dim):
    return lax.dot_general(
        left_side,
        right_side,
        (((left_dim,), (right_dim,)), ((), ())),
        preferred_element_type=F32,
    )


def split_wide(value):
    high = lax.reduce_precision(value, 8, 7)
    return high.astype(BF), (value - high).astype(BF)


def exchange(chunks, axes):
    return lax.all_to_all(chunks, axes, 0, 0, tiled=True)


def gather(rows, axes):
    count = lax.axis_size(axes)
    return exchange(jnp.broadcast_to(rows[None], (count,) + rows.shape), axes)


def section_shift(block, distance):
    sections = lax.axis_size("section")
    route = [(i, i + distance) for i in range(sections) if 0 <= i + distance < sections]
    return lax.ppermute(block, "section", route)


def run(body, outs, scratch, flops, *operands):
    return pl.pallas_call(
        body,
        out_shape=[jax.ShapeDtypeStruct(shape, kind) for shape, kind in outs],
        in_specs=[
            pl.BlockSpec(memory_space=pltpu.SMEM if item.ndim == 1 else pltpu.VMEM)
            for item in operands
        ],
        out_specs=[pl.BlockSpec(memory_space=pltpu.VMEM) for _ in outs],
        scratch_shapes=[pltpu.VMEM(shape, kind) for shape, kind in scratch],
        compiler_params=pltpu.CompilerParams(vmem_limit_bytes=VMEM_BYTES),
        cost_estimate=pl.CostEstimate(flops=flops, bytes_accessed=4000000, transcendentals=0),
    )(*operands)


def to_chunk(row):
    count = row.shape[1] // LANES
    return jnp.concatenate([row[:, k * LANES : (k + 1) * LANES] for k in range(count)], axis=0)


def to_row(chunk):
    return jnp.concatenate([chunk[k : k + 1, :] for k in range(chunk.shape[0])], axis=1)


def to_column(row):
    return jnp.transpose(jnp.broadcast_to(row, (LANES, row.shape[1])))


def stack_rows(rows, count, kind):
    filler = jnp.zeros((count - len(rows), rows[0].shape[1]), F32)
    return jnp.concatenate(list(rows) + [filler], axis=0).astype(kind)


def first_rows(rows):
    return stack_rows(rows, STEP, BF)


def wide_rows(ref, offset, count):
    return jnp.concatenate([ref[:, offset + k, :] for k in range(count)], axis=1)


def put_rows(ref, offset, value):
    for k in range(value.shape[1] // LANES):
        ref[:, offset + k, :] = value[:, k * LANES : (k + 1) * LANES]


def two_parts(row):
    high = row.astype(BF).astype(F32)
    return high, row - high


def norm_step(wide, gain, window, hidden_ref, inverse_ref, length_ref):
    inverse = lax.rsqrt(jnp.mean(wide * wide, axis=-1, keepdims=True) + EPSILON)
    hidden = (wide * inverse * gain).astype(BF)
    hidden_ref[window, :] = hidden
    hidden_f = hidden.astype(F32)
    length = lax.rsqrt(jnp.sum(hidden_f * hidden_f, axis=-1, keepdims=True) + EPSILON)
    inverse_ref[window, :] = jnp.broadcast_to(inverse, (STEP, LANES))
    length_ref[window, :] = jnp.broadcast_to(length, (STEP, LANES))


def norm_kernel(in_ref, gain_ref, hidden_ref, inverse_ref, length_out, length_ref):
    gain = gain_ref[...]

    @pl.loop(0, in_ref.shape[0] // STEP)
    def _(index):
        window = pl.ds(index * STEP, STEP)
        wide = in_ref[window, :].astype(F32)
        norm_step(wide, gain, window, hidden_ref, inverse_ref, length_ref)

    length_out[...] = jnp.transpose(length_ref[...])[:8]


def slot_front(scale, columns_ref, hidden_ref, length, logits_ref, prob_ref, rows_ref):
    product = dot_dims(columns_ref[...], hidden_ref[...], 1, 1)
    logits = scale * product * length
    expo = jnp.exp(logits)
    first = expo[:1]
    norm = jnp.sum(expo, axis=0, keepdims=True)
    combine = first / norm
    spread = first / jnp.sum(first, axis=1, keepdims=True)
    logits_ref[...] = logits
    prob_ref[...] = expo / norm
    rows_ref[...] = stack_rows([length, combine, spread], 8, F32)
    slot = jnp.dot(first_rows([spread]), hidden_ref[...], preferred_element_type=F32)
    return combine, slot[:1].astype(BF).astype(F32)


def mix_rows(combine, upstream):
    mixed = jnp.dot(first_rows(two_parts(combine)), upstream, preferred_element_type=F32)
    return (mixed[:1] + mixed[1:2]).astype(BF).astype(F32)


def early_kernel(
    scale_ref, hidden_ref, length_ref, columns_ref, up_ref,
    send_ref, logits_ref, prob_ref, rows_ref, mixed_ref,
):
    length = length_ref[:1]
    combine, slot = slot_front(
        scale_ref[0], columns_ref, hidden_ref, length, logits_ref, prob_ref, rows_ref
    )
    send_ref[...] = jnp.broadcast_to(to_chunk(slot)[None], send_ref.shape)
    mixed_ref[...] = to_chunk(mix_rows(combine, up_ref[...]))


def pack_kernel(sums_ref, rows_ref, out_ref):
    total = jnp.sum(sums_ref[...], axis=0).astype(BF).astype(F32)
    combine = to_chunk(rows_ref[1:2])
    count = total.shape[0]
    out_ref[:count] = total
    out_ref[count:] = jnp.concatenate(
        [combine, jnp.zeros((out_ref.shape[0] - count - combine.shape[0], LANES), F32)], axis=0
    )


def late_kernel(
    scale_ref, base_ref, moved_ref, up_ref, columns_ref, gain_ref,
    send_ref, in_ref, hidden_ref, inverse_ref, logits_ref, prob_ref, rows_ref,
    length_ref, comb_ref,
):
    gain = gain_ref[...]
    chunk = gain.shape[1] // LANES
    out_row = to_row(moved_ref[:chunk])
    comb_ref[...] = to_column(to_row(moved_ref[chunk : chunk + 2]))

    @pl.loop(0, in_ref.shape[0] // STEP)
    def _(index):
        window = pl.ds(index * STEP, STEP)
        base = base_ref[window, :].astype(F32)
        value = (base + comb_ref[window, :1] * out_row).astype(BF)
        in_ref[window, :] = value
        norm_step(value.astype(F32), gain, window, hidden_ref, inverse_ref, length_ref)

    length = jnp.transpose(length_ref[...])[:1]
    combine, slot = slot_front(
        scale_ref[0], columns_ref, hidden_ref, length, logits_ref, prob_ref, rows_ref
    )
    mixed = mix_rows(combine, up_ref[...])
    both = jnp.concatenate([to_chunk(slot), to_chunk(mixed)], axis=0)
    send_ref[...] = jnp.broadcast_to(both[None], send_ref.shape)


def gelu_parts(value):
    rate = 0.7978845608028654
    cube = 0.044715
    bent = jnp.tanh(rate * (value + cube * value * value * value))
    half = 0.5 * (1.0 + bent)
    slope = half + 0.5 * value * (1.0 - bent * bent) * rate * (1.0 + 3.0 * cube * value * value)
    return value * half, slope


def expert_early_kernel(slots_ref, first_ref, second_ref, send_ref, slot_ref, act_ref, slope_ref):
    chunk = slots_ref.shape[1]
    slots = wide_rows(slots_ref, 0, chunk).astype(BF)
    slot_ref[...] = slots
    value, slope = gelu_parts(jnp.dot(slots, first_ref[...], preferred_element_type=F32))
    act = value.astype(BF)
    act_ref[...] = act
    slope_ref[...] = slope
    put_rows(send_ref, 0, jnp.dot(act, second_ref[...], preferred_element_type=F32))


def expert_late_kernel(
    pairs_ref, first_ref, second_ref, send_ref, slot_ref, mixed_ref, act_ref, grad_ref
):
    chunk = pairs_ref.shape[1] // 2
    slots = wide_rows(pairs_ref, 0, chunk).astype(BF)
    mixed = wide_rows(pairs_ref, chunk, chunk).astype(BF)
    slot_ref[...] = slots
    mixed_ref[...] = mixed
    value, slope = gelu_parts(jnp.dot(slots, first_ref[...], preferred_element_type=F32))
    act = value.astype(BF)
    act_ref[...] = act
    grad = (dot_dims(mixed, second_ref[...], 1, 1) * slope).astype(BF)
    grad_ref[...] = grad
    put_rows(send_ref, 0, jnp.dot(act, second_ref[...], preferred_element_type=F32))
    put_rows(send_ref, chunk, dot_dims(grad, first_ref[...], 1, 1))


def expert_back_kernel(
    mixed_in_ref, slope_ref, first_ref, second_ref, send_ref, mixed_ref, grad_ref
):
    mixed = wide_rows(mixed_in_ref, 0, mixed_in_ref.shape[1]).astype(BF)
    mixed_ref[...] = mixed
    grad = (dot_dims(mixed, second_ref[...], 1, 1) * slope_ref[...]).astype(BF)
    grad_ref[...] = grad
    put_rows(send_ref, 0, dot_dims(grad, first_ref[...], 1, 1))


def back_body(
    scale, out_row, grad_row, in_ref, hidden_ref, inverse_ref, logits_ref, prob_ref, rows_ref,
    up_ref, columns_ref, gain_ref, grads_ref, gain_out, hold_ref, pull_ref,
):
    gain = gain_ref[...]
    length = rows_ref[0:1]
    combine = rows_ref[1:2]
    spread = rows_ref[2:3]
    grad_rows = first_rows([grad_row])
    dcombine = dot_dims(first_rows([out_row]), up_ref[...], 1, 1)[:1]
    dspread = dot_dims(grad_rows, hidden_ref[...], 1, 1)[:1].astype(BF).astype(F32)
    first_term = spread * (dspread - jnp.sum(dspread * spread, axis=1, keepdims=True))
    mixed = combine * dcombine
    prob = prob_ref[...]
    top = lax.broadcasted_iota(jnp.int32, prob.shape, 0) == 0
    dlogits = jnp.where(top, mixed + first_term, 0.0) - prob * mixed
    dproduct = dlogits * scale * length
    pull = jnp.sum(dlogits * logits_ref[...], axis=0, keepdims=True) * length * length
    pull_ref[...] = to_column(pull)
    dproduct_bf = dproduct.astype(BF)
    hold_ref[...] = dot_dims(dproduct_bf, columns_ref[...], 0, 0) + dot_dims(
        first_rows([spread]), grad_rows, 0, 0
    )
    router = jnp.dot(dproduct_bf, hidden_ref[...], preferred_element_type=F32)
    gain_out[...] = jnp.zeros_like(gain_out)

    @pl.loop(0, in_ref.shape[0] // STEP)
    def _(index):
        window = pl.ds(index * STEP, STEP)
        inverse = inverse_ref[window, :1]
        dhidden = hold_ref[window, :] - hidden_ref[window, :].astype(F32) * pull_ref[window, :1]
        scaled = in_ref[window, :].astype(F32) * inverse
        product = dhidden * scaled
        gain_out[...] += product[:8] + product[8:]
        through = dhidden * gain
        mean_term = jnp.mean(product * gain, axis=-1, keepdims=True)
        dinput = inverse * (through - scaled * mean_term)
        grads_ref[window, :] = (up_ref[window, :].astype(F32) + dinput).astype(BF)

    return router


def back_late_kernel(
    scale_ref, sums_ref, in_ref, hidden_ref, inverse_ref, logits_ref, prob_ref, rows_ref,
    up_ref, columns_ref, gain_ref, moved_ref,
    grads_ref, mixed_ref, outs_ref, router_ref, gain_out, hold_ref, pull_ref,
):
    chunk = sums_ref.shape[1] // 2
    total = jnp.sum(sums_ref[...], axis=0).astype(BF).astype(F32)
    outs_ref[...] = total
    router = back_body(
        scale_ref[0], to_row(total[:chunk]), to_row(total[chunk:]), in_ref, hidden_ref,
        inverse_ref, logits_ref, prob_ref, rows_ref, up_ref, columns_ref, gain_ref, grads_ref,
        gain_out, hold_ref, pull_ref,
    )
    router_ref[...] = router
    combine = to_row(moved_ref[chunk : chunk + 2])
    mixed_ref[...] = to_chunk(mix_rows(combine, grads_ref[...]))


def back_early_kernel(
    scale_ref, sums_ref, packed_ref, in_ref, hidden_ref, inverse_ref, logits_ref, prob_ref,
    rows_ref, up_ref, columns_ref, gain_ref, router_in_ref, gain_in_ref,
    grads_ref, outs_ref, router_ref, gain_ref_out, gain_out, hold_ref, pull_ref,
):
    chunk = sums_ref.shape[1]
    total = jnp.sum(sums_ref[...], axis=0).astype(BF).astype(F32)
    outs_ref[...] = total
    router = back_body(
        scale_ref[0], to_row(packed_ref[:chunk]), to_row(total), in_ref, hidden_ref,
        inverse_ref, logits_ref, prob_ref, rows_ref, up_ref, columns_ref, gain_ref, grads_ref,
        gain_out, hold_ref, pull_ref,
    )
    router_ref[...] = (router + router_in_ref[...]).astype(BF)
    gain_sum = jnp.sum(gain_out[...] + gain_in_ref[...], axis=0, keepdims=True)
    gain_ref_out[...] = stack_rows(two_parts(gain_sum), 8, F32)


def shards(
    tokens,
    cotangent,
    inflow,
    backflow,
    norm_gain,
    slot_scale,
    router_weight,
    expert_in,
    expert_back,
):
    section_index = lax.axis_index("section")
    is_first = section_index == 0
    is_last = section_index == lax.axis_size("section") - 1
    group = lax.axis_size(DP)
    patches = tokens.shape[2]
    width = tokens.shape[3]
    chunk = width // LANES
    local = router_weight.shape[2]
    slots = local * group
    hidden_units = expert_in.shape[2]
    first_weight = expert_in[0]
    second_weight = expert_back[0]
    token_block = (patches, width)
    table = ((slots, patches), F32)
    weights = router_weight[0].T.astype(F32)
    weight_inv = lax.rsqrt(jnp.sum(weights * weights, axis=1, keepdims=True) + EPSILON)
    local_cols = (weights * weight_inv).astype(BF)

    start_in = jnp.where(is_first, tokens[0, 0], inflow[0, 0])
    sent_in = section_shift(start_in, 1)
    columns = gather(local_cols, DP).reshape(-1, width)

    hidden_early, inverse_early, length_early = run(
        norm_kernel,
        [(token_block, BF), ((patches, LANES), F32), ((8, patches), F32)],
        [((patches, LANES), F32)],
        10000000,
        start_in,
        norm_gain,
    )
    send, logits_early, prob_early, rows_early, mixed_last = run(
        early_kernel,
        [((group, chunk, LANES), F32), table, table, ((8, patches), F32), ((chunk, LANES), F32)],
        [],
        300000000,
        slot_scale,
        hidden_early,
        length_early,
        columns,
        cotangent[0, 0],
    )
    part, slot_early, act_early, slope_early = run(
        expert_early_kernel,
        [
            ((group, chunk, LANES), F32),
            ((group, width), BF),
            ((group, hidden_units), BF),
            ((group, hidden_units), F32),
        ],
        [],
        70000000,
        exchange(send, DP),
        first_weight,
        second_weight,
    )
    packed = run(
        pack_kernel,
        [((chunk + 8, LANES), F32)],
        [],
        1000000,
        exchange(part, DP),
        rows_early,
    )[0]
    moved = section_shift(packed, 1)

    base = jnp.where(is_first, tokens[1, 0], sent_in)
    late_up = jnp.where(is_last, cotangent[1, 0], backflow[0, 0])
    send, late_in, hidden_late, inverse_late, logits_late, prob_late, rows_late = run(
        late_kernel,
        [
            ((group, 2 * chunk, LANES), F32),
            (token_block, BF),
            (token_block, BF),
            ((patches, LANES), F32),
            table,
            table,
            ((8, patches), F32),
        ],
        [((patches, LANES), F32), ((patches, LANES), F32)],
        400000000,
        slot_scale,
        base,
        moved,
        late_up,
        columns,
        norm_gain,
    )
    parts, slot_late, mixed_late, act_late, pre_grad_late = run(
        expert_late_kernel,
        [
            ((group, 2 * chunk, LANES), F32),
            ((group, width), BF),
            ((group, width), BF),
            ((group, hidden_units), BF),
            ((group, hidden_units), BF),
        ],
        [],
        140000000,
        exchange(send, DP),
        first_weight,
        second_weight,
    )
    back_scratch = [(token_block, F32), ((patches, LANES), F32)]
    grads_late, mixed_before, outs_late, router_late, gain_late = run(
        back_late_kernel,
        [
            (token_block, BF),
            ((chunk, LANES), F32),
            ((2 * chunk, LANES), F32),
            ((slots, width), F32),
            ((8, width), F32),
        ],
        back_scratch,
        600000000,
        slot_scale,
        exchange(parts, DP),
        late_in,
        hidden_late,
        inverse_late,
        logits_late,
        prob_late,
        rows_late,
        late_up,
        columns,
        norm_gain,
        moved,
    )
    moved_back = section_shift(mixed_before, -1)
    sent_grads = section_shift(grads_late, -1)
    mixed_early = jnp.where(is_last, mixed_last, moved_back)
    part, mixed_early_all, pre_grad_early = run(
        expert_back_kernel,
        [
            ((group, chunk, LANES), F32),
            ((group, width), BF),
            ((group, hidden_units), BF),
        ],
        [],
        70000000,
        gather(mixed_early, DP),
        slope_early,
        first_weight,
        second_weight,
    )
    early_up = jnp.where(is_last, cotangent[0, 0], sent_grads)
    grads_early, outs_early, router_sum, gain_pair = run(
        back_early_kernel,
        [
            (token_block, BF),
            ((chunk, LANES), F32),
            ((slots, width), BF),
            ((8, width), F32),
        ],
        [((8, width), F32)] + back_scratch,
        600000000,
        slot_scale,
        exchange(part, DP),
        packed,
        start_in,
        hidden_early,
        inverse_early,
        logits_early,
        prob_early,
        rows_early,
        early_up,
        columns,
        norm_gain,
        router_late,
        gain_late,
    )

    gain_rows = jnp.broadcast_to(gain_pair[:2].astype(BF)[None], (group, 2, width))
    finals = exchange(
        jnp.concatenate([router_sum.reshape(group, local, width), gain_rows], axis=1), DP
    )
    finals = finals.reshape(group, -1, width).astype(F32).sum(0)
    gain_total = finals[local : local + 1] + finals[local + 1 :]
    pulled = finals[:local]
    dots = jnp.sum(pulled * weights, axis=1, keepdims=True)
    router_grad = weight_inv * (pulled - weights * (dots * weight_inv * weight_inv))

    first_grad = dot_dims(
        jnp.concatenate([slot_early, slot_late], axis=0),
        jnp.concatenate([pre_grad_early, pre_grad_late], axis=0),
        0,
        0,
    )
    second_grad = dot_dims(
        jnp.concatenate([act_early, act_late], axis=0),
        jnp.concatenate([mixed_early_all, mixed_late], axis=0),
        0,
        0,
    )
    slot_out = jnp.stack([packed[:chunk].reshape(1, width), outs_late[:chunk].reshape(1, width)])
    slot_grad = jnp.stack([outs_early.reshape(1, width), outs_late[chunk:].reshape(1, width)])
    return (
        jnp.stack([grads_early, grads_late])[None, :, None],
        slot_out.astype(BF)[None],
        slot_grad.astype(BF)[None],
        first_grad.astype(BF)[None],
        second_grad.astype(BF)[None],
        router_grad.astype(BF).T[None],
        gain_total,
    )


def solution(mesh):
    fine = Mesh(mesh.devices.reshape(mesh.shape["section"], 2, 4, 4), AXES)
    in_specs = (
        P(None, DP, None, None),
        P(None, DP, None, None),
        P("section", DP, None, None),
        P("section", DP, None, None),
        P("section", None),
        P("section"),
        P("section", None, DP),
        P("section", None, DP),
        P("section", DP, None),
    )
    out_specs = (
        P("section", None, DP, None, None),
        P("section", None, DP, None),
        P("section", None, DP, None),
        P("section", None, DP),
        P("section", DP, None),
        P("section", None, DP),
        P("section", None),
    )
    return jax.shard_map(shards, mesh=fine, in_specs=in_specs, out_specs=out_specs, check_vma=False)
```

```python
import jax
import jax.numpy as jnp
from jax import lax
from jax.experimental import pallas as pl
from jax.experimental.pallas import tpu as pltpu
from jax.sharding import Mesh
from jax.sharding import PartitionSpec as P

EPSILON = 1e-06
BF = jnp.bfloat16
F32 = jnp.float32
AXES = ("section", "zh", "y", "x")
DP = ("zh", "y", "x")
LANES = 128
STEP = 16
VMEM_BYTES = 24 * 1024 * 1024


def dot_dims(left_side, right_side, left_dim, right_dim):
    return lax.dot_general(
        left_side,
        right_side,
        (((left_dim,), (right_dim,)), ((), ())),
        preferred_element_type=F32,
    )


def exchange(chunks, axes):
    return lax.all_to_all(chunks, axes, 0, 0, tiled=True)


def section_shift(block, distance):
    sections = lax.axis_size("section")
    route = [(i, i + distance) for i in range(sections) if 0 <= i + distance < sections]
    return lax.ppermute(block, "section", route)


def run(body, outs, scratch, flops, near, *operands):
    def place(index, item):
        if item.ndim == 1:
            return pltpu.SMEM
        return pltpu.VMEM if index < near else pl.ANY

    return pl.pallas_call(
        body,
        out_shape=[jax.ShapeDtypeStruct(shape, kind) for shape, kind in outs],
        in_specs=[
            pl.BlockSpec(memory_space=place(index, item)) for index, item in enumerate(operands)
        ],
        out_specs=[pl.BlockSpec(memory_space=pltpu.VMEM) for _ in outs],
        scratch_shapes=[
            pltpu.VMEM(*item) if isinstance(item, tuple) else item for item in scratch
        ],
        compiler_params=pltpu.CompilerParams(vmem_limit_bytes=VMEM_BYTES),
        cost_estimate=pl.CostEstimate(flops=flops, bytes_accessed=4000000, transcendentals=0),
    )(*operands)


def to_chunk(row):
    count = row.shape[1] // LANES
    return jnp.concatenate([row[:, k * LANES : (k + 1) * LANES] for k in range(count)], axis=0)


def to_row(chunk):
    return jnp.concatenate([chunk[k : k + 1, :] for k in range(chunk.shape[0])], axis=1)


def to_column(row):
    return jnp.transpose(jnp.broadcast_to(row, (LANES, row.shape[1])))


def stack_rows(rows, count, kind):
    filler = jnp.zeros((count - len(rows), rows[0].shape[1]), F32)
    return jnp.concatenate(list(rows) + [filler], axis=0).astype(kind)


def first_rows(rows):
    return stack_rows(rows, STEP, BF)


def wide_rows(ref, offset, count):
    return jnp.concatenate([ref[:, offset + k, :] for k in range(count)], axis=1)


def put_rows(ref, offset, value):
    for k in range(value.shape[1] // LANES):
        ref[:, offset + k, :] = value[:, k * LANES : (k + 1) * LANES]


def two_parts(row):
    high = row.astype(BF).astype(F32)
    return high, row - high


def lane_sums(value):
    parts = [value[:, k * LANES : (k + 1) * LANES] for k in range(value.shape[1] // LANES)]
    while len(parts) > 1:
        parts = [x + y for x, y in zip(parts[::2], parts[1::2])]
    return parts[0]


def summed(chunks_ref):
    return jnp.sum(chunks_ref[...].astype(F32), axis=0).astype(BF).astype(F32)


def passes(ref, body):
    @pl.loop(0, ref.shape[0] // STEP)
    def _(index):
        body(pl.ds(index * STEP, STEP))


def begin_copy(flag, yes, no, target, sem):
    @pl.when(flag != 0)
    def _():
        pltpu.make_async_copy(yes, target, sem).start()

    @pl.when(flag == 0)
    def _():
        pltpu.make_async_copy(no, target, sem).start()


def end_copy(source, target, sem):
    pltpu.make_async_copy(source, target, sem).wait()


def scaled_weights(weights_ref):
    weights = weights_ref[...].astype(F32)
    total = jnp.sum(weights * weights, axis=1, keepdims=True)
    return weights, lax.rsqrt(total + EPSILON)


def columns_kernel(weights_ref, send_ref):
    weights, inverse = scaled_weights(weights_ref)
    columns = weights * inverse
    rows = [to_chunk(columns[k : k + 1]) for k in range(columns.shape[0])]
    block = jnp.concatenate(rows, axis=0).astype(BF)
    send_ref[...] = jnp.broadcast_to(block[None], send_ref.shape)


def norm_passes(in_ref, gain, hidden_ref, inverse_ref, sums_ref):
    rate = 1.0 / in_ref.shape[1]
    inverse = lax.rsqrt(jnp.sum(sums_ref[...], axis=1, keepdims=True) * rate + EPSILON)
    inverse_ref[...] = jnp.broadcast_to(inverse, inverse_ref.shape)

    def scale_rows(window):
        wide = in_ref[window, :].astype(F32)
        hidden = (wide * inverse_ref[window, :1] * gain).astype(BF)
        hidden_ref[window, :] = hidden
        hidden_f = hidden.astype(F32)
        sums_ref[window, :] = lane_sums(hidden_f * hidden_f)

    passes(in_ref, scale_rows)
    total = jnp.sum(jnp.transpose(sums_ref[...]), axis=0, keepdims=True)
    return lax.rsqrt(total + EPSILON)


def slot_front(scale, columns_ref, hidden_ref, length, logits_ref, prob_ref, rows_ref):
    product = dot_dims(columns_ref[...], hidden_ref[...], 1, 1)
    logits = scale * product * length
    expo = jnp.exp(logits)
    first = expo[:1]
    norm = jnp.sum(expo, axis=0, keepdims=True)
    combine = first / norm
    spread = first / jnp.sum(first, axis=1, keepdims=True)
    logits_ref[...] = logits
    prob_ref[...] = expo / norm
    rows_ref[...] = stack_rows([length, combine, spread], 8, F32)
    slot = jnp.dot(first_rows([spread]), hidden_ref[...], preferred_element_type=F32)
    return combine, slot[:1]


def mix_rows(combine, upstream):
    mixed = jnp.dot(first_rows(two_parts(combine)), upstream, preferred_element_type=F32)
    return mixed[:1] + mixed[1:2]


def early_kernel(
    scale_ref, flags_ref, chunks_ref, gain_ref, tokens_ref, inflow_ref, cotangent_ref,
    send_ref, in_ref, columns_ref, hidden_ref, inverse_ref, logits_ref, prob_ref, rows_ref,
    mixed_ref, up_ref, wide_ref, sums_ref, in_sem, up_sem,
):
    begin_copy(flags_ref[0], tokens_ref.at[0, 0], inflow_ref.at[0, 0], in_ref, in_sem)
    last = flags_ref[1] != 0

    @pl.when(last)
    def _():
        pltpu.make_async_copy(cotangent_ref.at[0, 0], up_ref, up_sem).start()

    peers = chunks_ref.shape[0]
    chunk = gain_ref.shape[1] // LANES
    wide_ref[...] = chunks_ref[...].astype(F32)
    for k in range(chunks_ref.shape[1] // chunk):
        columns_ref[k * peers : (k + 1) * peers] = wide_rows(wide_ref, k * chunk, chunk).astype(BF)
    end_copy(inflow_ref.at[0, 0], in_ref, in_sem)

    def square_rows(window):
        wide = in_ref[window, :].astype(F32)
        sums_ref[window, :] = lane_sums(wide * wide)

    passes(in_ref, square_rows)
    length = norm_passes(in_ref, gain_ref[...], hidden_ref, inverse_ref, sums_ref)
    combine, slot = slot_front(
        scale_ref[0], columns_ref, hidden_ref, length, logits_ref, prob_ref, rows_ref
    )
    send_ref[...] = jnp.broadcast_to(to_chunk(slot).astype(BF)[None], send_ref.shape)
    mixed_ref[...] = jnp.zeros_like(mixed_ref)

    @pl.when(last)
    def _():
        end_copy(cotangent_ref.at[0, 0], up_ref, up_sem)
        mixed_ref[...] = to_chunk(mix_rows(combine, up_ref[...])).astype(BF)


def pack_kernel(sums_ref, rows_ref, out_ref):
    total = summed(sums_ref)
    combine = to_chunk(rows_ref[1:2])
    count = total.shape[0]
    out_ref[:count] = total
    out_ref[count:] = jnp.concatenate(
        [combine, jnp.zeros((out_ref.shape[0] - count - combine.shape[0], LANES), F32)], axis=0
    )


def late_kernel(
    scale_ref, flags_ref, base_ref, moved_ref, columns_ref, gain_ref, cotangent_ref, backflow_ref,
    send_ref, in_ref, hidden_ref, inverse_ref, logits_ref, prob_ref, rows_ref, up_ref,
    sums_ref, comb_ref, up_sem,
):
    begin_copy(flags_ref[1], cotangent_ref.at[1, 0], backflow_ref.at[0, 0], up_ref, up_sem)
    chunk = gain_ref.shape[1] // LANES
    out_row = to_row(moved_ref[:chunk])
    comb_ref[...] = to_column(to_row(moved_ref[chunk : chunk + 2]))

    def add_rows(window):
        base = base_ref[window, :].astype(F32)
        value = (base + comb_ref[window, :1] * out_row).astype(BF)
        in_ref[window, :] = value
        wide = value.astype(F32)
        sums_ref[window, :] = lane_sums(wide * wide)

    passes(in_ref, add_rows)
    length = norm_passes(in_ref, gain_ref[...], hidden_ref, inverse_ref, sums_ref)
    combine, slot = slot_front(
        scale_ref[0], columns_ref, hidden_ref, length, logits_ref, prob_ref, rows_ref
    )
    end_copy(backflow_ref.at[0, 0], up_ref, up_sem)
    mixed = mix_rows(combine, up_ref[...])
    both = jnp.concatenate([to_chunk(slot), to_chunk(mixed)], axis=0).astype(BF)
    send_ref[...] = jnp.broadcast_to(both[None], send_ref.shape)


def gelu_parts(value):
    rate = 0.7978845608028654
    cube = 0.044715
    bent = jnp.tanh(rate * (value + cube * value * value * value))
    half = 0.5 * (1.0 + bent)
    slope = half + 0.5 * value * (1.0 - bent * bent) * rate * (1.0 + 3.0 * cube * value * value)
    return value * half, slope


def expert_early_kernel(
    slots_ref, first_ref, second_ref, send_ref, slot_ref, act_ref, slope_ref, wide_ref
):
    wide_ref[...] = slots_ref[...].astype(F32)
    slots = wide_rows(wide_ref, 0, slots_ref.shape[1]).astype(BF)
    slot_ref[...] = slots
    value, slope = gelu_parts(jnp.dot(slots, first_ref[...], preferred_element_type=F32))
    act = value.astype(BF)
    act_ref[...] = act
    slope_ref[...] = slope
    put_rows(wide_ref, 0, jnp.dot(act, second_ref[...], preferred_element_type=F32))
    send_ref[...] = wide_ref[...].astype(BF)


def expert_late_kernel(
    pairs_ref, first_ref, second_ref, send_ref, slot_ref, mixed_ref, act_ref, grad_ref, wide_ref
):
    chunk = pairs_ref.shape[1] // 2
    wide_ref[...] = pairs_ref[...].astype(F32)
    slots = wide_rows(wide_ref, 0, chunk).astype(BF)
    mixed = wide_rows(wide_ref, chunk, chunk).astype(BF)
    slot_ref[...] = slots
    mixed_ref[...] = mixed
    value, slope = gelu_parts(jnp.dot(slots, first_ref[...], preferred_element_type=F32))
    act = value.astype(BF)
    act_ref[...] = act
    grad = (dot_dims(mixed, second_ref[...], 1, 1) * slope).astype(BF)
    grad_ref[...] = grad
    put_rows(wide_ref, 0, jnp.dot(act, second_ref[...], preferred_element_type=F32))
    put_rows(wide_ref, chunk, dot_dims(grad, first_ref[...], 1, 1))
    send_ref[...] = wide_ref[...].astype(BF)


def expert_back_kernel(
    mixed_in_ref, slope_ref, first_ref, second_ref, send_ref, mixed_ref, grad_ref, wide_ref
):
    wide_ref[...] = mixed_in_ref[...].astype(F32)
    mixed = wide_rows(wide_ref, 0, mixed_in_ref.shape[1]).astype(BF)
    mixed_ref[...] = mixed
    grad = (dot_dims(mixed, second_ref[...], 1, 1) * slope_ref[...]).astype(BF)
    grad_ref[...] = grad
    put_rows(wide_ref, 0, dot_dims(grad, first_ref[...], 1, 1))
    send_ref[...] = wide_ref[...].astype(BF)


def spread_kernel(moved_ref, own_ref, send_ref):
    block = (moved_ref[...].astype(F32) + own_ref[...].astype(F32)).astype(BF)
    send_ref[...] = jnp.broadcast_to(block[None], send_ref.shape)


def back_body(
    scale, out_row, grad_row, in_ref, hidden_ref, inverse_ref, logits_ref, prob_ref, rows_ref,
    up_ref, columns_ref, gain_ref, grads_ref, hold_ref, pull_ref, mean_ref,
):
    gain = gain_ref[...]
    length = rows_ref[0:1]
    combine = rows_ref[1:2]
    spread = rows_ref[2:3]
    grad_rows = first_rows([grad_row])
    dcombine = dot_dims(first_rows([out_row]), up_ref[...], 1, 1)[:1]
    dspread = dot_dims(grad_rows, hidden_ref[...], 1, 1)[:1].astype(BF).astype(F32)
    first_term = spread * (dspread - jnp.sum(dspread * spread, axis=1, keepdims=True))
    mixed = combine * dcombine
    prob = prob_ref[...]
    top = lax.broadcasted_iota(jnp.int32, prob.shape, 0) == 0
    dlogits = jnp.where(top, mixed + first_term, 0.0) - prob * mixed
    dproduct = dlogits * scale * length
    pull = jnp.sum(dlogits * logits_ref[...], axis=0, keepdims=True) * length * length
    pull_ref[...] = to_column(pull)
    dproduct_bf = dproduct.astype(BF)
    hold_ref[...] = dot_dims(dproduct_bf, columns_ref[...], 0, 0) + dot_dims(
        first_rows([spread]), grad_rows, 0, 0
    )
    router = jnp.dot(dproduct_bf, hidden_ref[...], preferred_element_type=F32)

    def product_rows(index, total):
        window = pl.ds(index * STEP, STEP)
        dhidden = hold_ref[window, :] - hidden_ref[window, :].astype(F32) * pull_ref[window, :1]
        hold_ref[window, :] = dhidden
        product = dhidden * (in_ref[window, :].astype(F32) * inverse_ref[window, :1])
        mean_ref[window, :] = lane_sums(product * gain)
        return total + product[:8] + product[8:]

    gain_sum = lax.fori_loop(
        0, in_ref.shape[0] // STEP, product_rows, jnp.zeros((8, in_ref.shape[1]), F32)
    )
    mean = jnp.sum(mean_ref[...], axis=1, keepdims=True) * (1.0 / in_ref.shape[1])
    mean_ref[...] = jnp.broadcast_to(mean * inverse_ref[...], mean_ref.shape)

    def grad_rows_pass(window):
        inverse = inverse_ref[window, :1]
        through = hold_ref[window, :] * gain
        wide = in_ref[window, :].astype(F32)
        dinput = inverse * (through - wide * mean_ref[window, :1])
        grads_ref[window, :] = (up_ref[window, :].astype(F32) + dinput).astype(BF)

    passes(in_ref, grad_rows_pass)
    return router, gain_sum


def back_late_kernel(
    scale_ref, sums_ref, in_ref, hidden_ref, inverse_ref, logits_ref, prob_ref, rows_ref,
    up_ref, columns_ref, gain_ref, moved_ref,
    grads_ref, mixed_ref, outs_ref, router_ref, gain_out, hold_ref, pull_ref, mean_ref,
):
    chunk = sums_ref.shape[1] // 2
    total = summed(sums_ref)
    outs_ref[...] = total
    router, gain_sum = back_body(
        scale_ref[0], to_row(total[:chunk]), to_row(total[chunk:]), in_ref, hidden_ref,
        inverse_ref, logits_ref, prob_ref, rows_ref, up_ref, columns_ref, gain_ref, grads_ref,
        hold_ref, pull_ref, mean_ref,
    )
    router_ref[...] = router
    gain_out[...] = gain_sum
    combine = to_row(moved_ref[chunk : chunk + 2])
    mixed_ref[...] = to_chunk(mix_rows(combine, grads_ref[...])).astype(BF)


def back_early_kernel(
    scale_ref, flags_ref, sums_ref, packed_ref, in_ref, hidden_ref, inverse_ref, logits_ref,
    prob_ref, rows_ref, columns_ref, gain_ref, router_in_ref, gain_in_ref, cotangent_ref, sent_ref,
    grads_ref, outs_ref, send_ref, up_ref, hold_ref, pull_ref, mean_ref, wide_ref, up_sem,
):
    begin_copy(flags_ref[1], cotangent_ref.at[0, 0], sent_ref, up_ref, up_sem)
    chunk = sums_ref.shape[1]
    total = summed(sums_ref)
    outs_ref[...] = total
    end_copy(sent_ref, up_ref, up_sem)
    router, gain_sum = back_body(
        scale_ref[0], to_row(packed_ref[:chunk]), to_row(total), in_ref, hidden_ref,
        inverse_ref, logits_ref, prob_ref, rows_ref, up_ref, columns_ref, gain_ref, grads_ref,
        hold_ref, pull_ref, mean_ref,
    )
    router = router + router_in_ref[...]
    peers = send_ref.shape[0]
    count = router.shape[0] // peers
    for k in range(count):
        put_rows(wide_ref, k * chunk, router[k * peers : (k + 1) * peers])
    gain_row = jnp.sum(gain_sum + gain_in_ref[...], axis=0, keepdims=True)
    wide_ref[:, count * chunk :, :] = jnp.broadcast_to(
        to_chunk(gain_row)[None], (peers, chunk, LANES)
    )
    send_ref[...] = wide_ref[...].astype(BF)


def final_kernel(chunks_ref, weights_ref, router_ref, gain_ref):
    weights, inverse = scaled_weights(weights_ref)
    total = jnp.sum(chunks_ref[...].astype(F32), axis=0)
    count = weights.shape[0]
    chunk = weights.shape[1] // LANES
    rows = [to_row(total[k * chunk : (k + 1) * chunk]) for k in range(count)]
    pulled = jnp.concatenate(rows, axis=0)
    dots = jnp.sum(pulled * weights, axis=1, keepdims=True)
    router_ref[...] = (inverse * (pulled - weights * (dots * inverse * inverse))).astype(BF)
    gain_ref[...] = to_row(total[count * chunk :])


def shards(
    tokens,
    cotangent,
    inflow,
    backflow,
    norm_gain,
    slot_scale,
    router_weight,
    expert_in,
    expert_back,
):
    section_index = lax.axis_index("section")
    is_first = section_index == 0
    is_last = section_index == lax.axis_size("section") - 1
    flags = jnp.stack([is_first, is_last]).astype(jnp.int32)
    group = lax.axis_size(DP)
    patches = tokens.shape[2]
    width = tokens.shape[3]
    chunk = width // LANES
    local = router_weight.shape[2]
    slots = local * group
    hidden_units = expert_in.shape[2]
    first_weight = expert_in[0]
    second_weight = expert_back[0]
    weights = router_weight[0].T
    token_block = ((patches, width), BF)
    column = ((patches, LANES), F32)
    table = ((slots, patches), F32)
    rows = ((8, patches), F32)
    single = ((group, chunk, LANES), BF)
    double = ((group, 2 * chunk, LANES), BF)
    every_slot = ((group, width), BF)
    every_hidden = ((group, hidden_units), BF)
    copy_sem = pltpu.SemaphoreType.DMA

    columns_block = run(
        columns_kernel, [((group, local * chunk, LANES), BF)], [], 1000000, 1, weights
    )[0]
    (
        send, start_in, columns, hidden_early, inverse_early, logits_early, prob_early,
        rows_early, mixed_last,
    ) = run(
        early_kernel,
        [
            single, token_block, ((slots, width), BF), token_block, column, table, table, rows,
            ((chunk, LANES), BF),
        ],
        [token_block, ((group, local * chunk, LANES), F32), column, copy_sem, copy_sem],
        300000000,
        4,
        slot_scale,
        flags,
        exchange(columns_block, DP),
        norm_gain,
        tokens,
        inflow,
        cotangent,
    )
    sent_in = section_shift(start_in, 1)
    part, slot_early, act_early, slope_early = run(
        expert_early_kernel,
        [single, every_slot, every_hidden, ((group, hidden_units), F32)],
        [((group, chunk, LANES), F32)],
        70000000,
        3,
        exchange(send, DP),
        first_weight,
        second_weight,
    )
    packed = run(
        pack_kernel, [((chunk + 8, LANES), F32)], [], 1000000, 2, exchange(part, DP), rows_early
    )[0]
    moved = section_shift(packed, 1)

    base = jnp.where(is_first, tokens[1, 0], sent_in)
    (
        send, late_in, hidden_late, inverse_late, logits_late, prob_late, rows_late, late_up,
    ) = run(
        late_kernel,
        [double, token_block, token_block, column, table, table, rows, token_block],
        [column, column, copy_sem],
        400000000,
        6,
        slot_scale,
        flags,
        base,
        moved,
        columns,
        norm_gain,
        cotangent,
        backflow,
    )
    parts, slot_late, mixed_late, act_late, pre_grad_late = run(
        expert_late_kernel,
        [double, every_slot, every_slot, every_hidden, every_hidden],
        [((group, 2 * chunk, LANES), F32)],
        140000000,
        3,
        exchange(send, DP),
        first_weight,
        second_weight,
    )
    back_scratch = [((patches, width), F32), column, column]
    grads_late, mixed_before, outs_late, router_late, gain_late = run(
        back_late_kernel,
        [
            token_block, ((chunk, LANES), BF), ((2 * chunk, LANES), F32), ((slots, width), F32),
            ((8, width), F32),
        ],
        back_scratch,
        600000000,
        12,
        slot_scale,
        exchange(parts, DP),
        late_in,
        hidden_late,
        inverse_late,
        logits_late,
        prob_late,
        rows_late,
        late_up,
        columns,
        norm_gain,
        moved,
    )
    moved_back, held_grads = lax.optimization_barrier(
        (section_shift(mixed_before, -1), grads_late)
    )
    sent_grads = section_shift(held_grads, -1)
    send = run(spread_kernel, [single], [], 1000000, 2, moved_back, mixed_last)[0]
    part, mixed_early_all, pre_grad_early = run(
        expert_back_kernel,
        [single, every_slot, every_hidden],
        [((group, chunk, LANES), F32)],
        70000000,
        4,
        exchange(send, DP),
        slope_early,
        first_weight,
        second_weight,
    )
    last_rows = (local + 1) * chunk
    grads_early, outs_early, finals = run(
        back_early_kernel,
        [token_block, ((chunk, LANES), F32), ((group, last_rows, LANES), BF)],
        [token_block] + back_scratch + [((group, last_rows, LANES), F32), copy_sem],
        600000000,
        14,
        slot_scale,
        flags,
        exchange(part, DP),
        packed,
        start_in,
        hidden_early,
        inverse_early,
        logits_early,
        prob_early,
        rows_early,
        columns,
        norm_gain,
        router_late,
        gain_late,
        cotangent,
        sent_grads,
    )
    router_grad, gain_total = run(
        final_kernel,
        [((local, width), BF), ((1, width), F32)],
        [],
        1000000,
        2,
        exchange(finals, DP),
        weights,
    )

    first_grad = dot_dims(
        jnp.concatenate([slot_early, slot_late], axis=0),
        jnp.concatenate([pre_grad_early, pre_grad_late], axis=0),
        0,
        0,
    )
    second_grad = dot_dims(
        jnp.concatenate([act_early, act_late], axis=0),
        jnp.concatenate([mixed_early_all, mixed_late], axis=0),
        0,
        0,
    )
    slot_out = jnp.stack([packed[:chunk].reshape(1, width), outs_late[:chunk].reshape(1, width)])
    slot_grad = jnp.stack([outs_early.reshape(1, width), outs_late[chunk:].reshape(1, width)])
    return (
        jnp.stack([grads_early, grads_late])[None, :, None],
        slot_out.astype(BF)[None],
        slot_grad.astype(BF)[None],
        first_grad.astype(BF)[None],
        second_grad.astype(BF)[None],
        router_grad.T[None],
        gain_total,
    )


def solution(mesh):
    fine = Mesh(mesh.devices.reshape(mesh.shape["section"], 2, 4, 4), AXES)
    in_specs = (
        P(None, DP, None, None),
        P(None, DP, None, None),
        P("section", DP, None, None),
        P("section", DP, None, None),
        P("section", None),
        P("section"),
        P("section", None, DP),
        P("section", None, DP),
        P("section", DP, None),
    )
    out_specs = (
        P("section", None, DP, None, None),
        P("section", None, DP, None),
        P("section", None, DP, None),
        P("section", None, DP),
        P("section", DP, None),
        P("section", None, DP),
        P("section", None),
    )
    return jax.shard_map(shards, mesh=fine, in_specs=in_specs, out_specs=out_specs, check_vma=False)
```

```python
import jax
import jax.numpy as jnp
from jax import lax
from jax.experimental import pallas as pl
from jax.experimental.pallas import tpu as pltpu
from jax.sharding import Mesh
from jax.sharding import PartitionSpec as P

EPSILON = 1e-06
BF = jnp.bfloat16
F32 = jnp.float32
AXES = ("section", "zh", "y", "x")
DP = ("zh", "y", "x")
LANES = 128
STEP = 16
VMEM_BYTES = 24 * 1024 * 1024


def dot_dims(left_side, right_side, left_dim, right_dim):
    return lax.dot_general(
        left_side,
        right_side,
        (((left_dim,), (right_dim,)), ((), ())),
        preferred_element_type=F32,
    )


def exchange(chunks, axes):
    return lax.all_to_all(chunks, axes, 0, 0, tiled=True)


def section_ring(block, distance):
    sections = lax.axis_size("section")
    return lax.ppermute(block, "section", [(i, (i + distance) % sections) for i in range(sections)])


def run(body, outs, scratch, flops, near, *operands):
    def place(index, item):
        if item.ndim == 1:
            return pltpu.SMEM
        return pltpu.VMEM if index < near else pl.ANY

    return pl.pallas_call(
        body,
        out_shape=[jax.ShapeDtypeStruct(item[0], item[1]) for item in outs],
        in_specs=[
            pl.BlockSpec(memory_space=place(index, item)) for index, item in enumerate(operands)
        ],
        out_specs=[
            pl.BlockSpec(memory_space=pltpu.VMEM if len(item) == 2 else pl.ANY) for item in outs
        ],
        scratch_shapes=[
            pltpu.VMEM(*item) if isinstance(item, tuple) else item for item in scratch
        ],
        compiler_params=pltpu.CompilerParams(vmem_limit_bytes=VMEM_BYTES),
        cost_estimate=pl.CostEstimate(flops=flops, bytes_accessed=4000000, transcendentals=0),
    )(*operands)


def to_chunk(row):
    count = row.shape[1] // LANES
    return jnp.concatenate([row[:, k * LANES : (k + 1) * LANES] for k in range(count)], axis=0)


def to_row(chunk):
    return jnp.concatenate([chunk[k : k + 1, :] for k in range(chunk.shape[0])], axis=1)


def to_column(row):
    return jnp.transpose(jnp.broadcast_to(row, (LANES, row.shape[1])))


def stack_rows(rows, count, kind):
    filler = jnp.zeros((count - len(rows), rows[0].shape[1]), F32)
    return jnp.concatenate(list(rows) + [filler], axis=0).astype(kind)


def first_rows(rows):
    return stack_rows(rows, STEP, BF)


def wide_rows(ref, offset, count):
    return jnp.concatenate([ref[:, offset + k, :] for k in range(count)], axis=1)


def put_rows(ref, offset, value):
    for k in range(value.shape[1] // LANES):
        ref[:, offset + k, :] = value[:, k * LANES : (k + 1) * LANES]


def two_parts(row):
    high = row.astype(BF).astype(F32)
    return high, row - high


def lane_sums(value):
    parts = [value[:, k * LANES : (k + 1) * LANES] for k in range(value.shape[1] // LANES)]
    while len(parts) > 1:
        parts = [x + y for x, y in zip(parts[::2], parts[1::2])]
    return parts[0]


def summed(chunks_ref):
    return jnp.sum(chunks_ref[...].astype(F32), axis=0).astype(BF).astype(F32)


def passes(ref, body):
    @pl.loop(0, ref.shape[0] // STEP)
    def _(index):
        body(pl.ds(index * STEP, STEP))


def begin_copy(flag, yes, no, target, sem):
    @pl.when(flag != 0)
    def _():
        pltpu.make_async_copy(yes, target, sem).start()

    @pl.when(flag == 0)
    def _():
        pltpu.make_async_copy(no, target, sem).start()


def end_copy(source, target, sem):
    pltpu.make_async_copy(source, target, sem).wait()


def scaled_weights(weights_ref):
    weights = weights_ref[...].astype(F32)
    total = jnp.sum(weights * weights, axis=1, keepdims=True)
    return weights, lax.rsqrt(total + EPSILON)


def columns_kernel(weights_ref, send_ref):
    weights, inverse = scaled_weights(weights_ref)
    columns = weights * inverse
    rows = [to_chunk(columns[k : k + 1]) for k in range(columns.shape[0])]
    block = jnp.concatenate(rows, axis=0).astype(BF)
    send_ref[...] = jnp.broadcast_to(block[None], send_ref.shape)


def norm_passes(in_ref, gain, hidden_ref, inverse_ref, sums_ref):
    rate = 1.0 / in_ref.shape[1]
    inverse = lax.rsqrt(jnp.sum(sums_ref[...], axis=1, keepdims=True) * rate + EPSILON)
    inverse_ref[...] = jnp.broadcast_to(inverse, inverse_ref.shape)

    def scale_rows(window):
        wide = in_ref[window, :].astype(F32)
        hidden = (wide * inverse_ref[window, :1] * gain).astype(BF)
        hidden_ref[window, :] = hidden
        hidden_f = hidden.astype(F32)
        sums_ref[window, :] = lane_sums(hidden_f * hidden_f)

    passes(in_ref, scale_rows)
    total = jnp.sum(jnp.transpose(sums_ref[...]), axis=0, keepdims=True)
    return lax.rsqrt(total + EPSILON)


def slot_front(scale, columns_ref, hidden_ref, length, logits_ref, prob_ref, rows_ref):
    product = dot_dims(columns_ref[...], hidden_ref[...], 1, 1)
    logits = scale * product * length
    expo = jnp.exp(logits)
    first = expo[:1]
    norm = jnp.sum(expo, axis=0, keepdims=True)
    combine = first / norm
    spread = first / jnp.sum(first, axis=1, keepdims=True)
    logits_ref[...] = logits
    prob_ref[...] = expo / norm
    rows_ref[...] = stack_rows([length, combine, spread], 8, F32)
    slot = jnp.dot(first_rows([spread]), hidden_ref[...], preferred_element_type=F32)
    return combine, slot[:1]


def mix_rows(combine, upstream):
    mixed = jnp.dot(first_rows(two_parts(combine)), upstream, preferred_element_type=F32)
    return mixed[:1] + mixed[1:2]


def norm_kernel(
    flags_ref, aux_ref, tokens_ref, inflow_ref,
    start_ref, hidden_out, inverse_ref, length_ref,
    in_ref, hidden_ref, sums_ref, in_sem, out_sem, hidden_sem,
):
    begin_copy(flags_ref[0], tokens_ref.at[0, 0], inflow_ref.at[0, 0], in_ref, in_sem)
    end_copy(inflow_ref.at[0, 0], in_ref, in_sem)
    pltpu.make_async_copy(in_ref, start_ref, out_sem).start()

    def square_rows(window):
        wide = in_ref[window, :].astype(F32)
        sums_ref[window, :] = lane_sums(wide * wide)

    passes(in_ref, square_rows)
    length = norm_passes(in_ref, aux_ref[:1], hidden_ref, inverse_ref, sums_ref)
    length_ref[...] = jnp.broadcast_to(length, length_ref.shape)
    pltpu.make_async_copy(hidden_ref, hidden_out, hidden_sem).start()
    end_copy(in_ref, start_ref, out_sem)
    end_copy(hidden_ref, hidden_out, hidden_sem)


def early_kernel(
    flags_ref, chunks_ref, length_ref, aux_ref, hidden_in, start_in, tokens_ref,
    send_ref, columns_ref, logits_ref, prob_ref, rows_ref, base_ref,
    hidden_ref, wide_ref, hidden_sem, base_sem,
):
    pltpu.make_async_copy(hidden_in, hidden_ref, hidden_sem).start()
    begin_copy(flags_ref[1], tokens_ref.at[1, 0], start_in, base_ref, base_sem)
    peers = chunks_ref.shape[0]
    chunk = aux_ref.shape[1] // LANES
    wide_ref[...] = chunks_ref[...].astype(F32)
    for k in range(chunks_ref.shape[1] // chunk):
        columns_ref[k * peers : (k + 1) * peers] = wide_rows(wide_ref, k * chunk, chunk).astype(BF)
    end_copy(hidden_in, hidden_ref, hidden_sem)
    _, slot = slot_front(
        aux_ref[1:2, :1], columns_ref, hidden_ref, length_ref[:1], logits_ref, prob_ref, rows_ref
    )
    send_ref[...] = jnp.broadcast_to(to_chunk(slot).astype(BF)[None], send_ref.shape)
    end_copy(start_in, base_ref, base_sem)


def late_kernel(
    flags_ref, sums_in, rows_in, base_ref, columns_ref, aux_ref, backflow_ref, cotangent_ref,
    send_ref, in_ref, hidden_ref, inverse_ref, logits_ref, prob_ref, rows_ref, up_ref, out_ref,
    sums_ref, comb_ref, up_sem,
):
    begin_copy(flags_ref[2], cotangent_ref.at[1, 0], backflow_ref, up_ref, up_sem)
    total = summed(sums_in)
    out_ref[...] = total
    out_row = to_row(total)
    before = rows_in[1:2]
    comb_ref[...] = to_column(jnp.where(flags_ref[1] != 0, jnp.zeros_like(before), before))

    def add_rows(window):
        base = base_ref[window, :].astype(F32)
        value = (base + comb_ref[window, :1] * out_row).astype(BF)
        in_ref[window, :] = value
        wide = value.astype(F32)
        sums_ref[window, :] = lane_sums(wide * wide)

    passes(in_ref, add_rows)
    length = norm_passes(in_ref, aux_ref[:1], hidden_ref, inverse_ref, sums_ref)
    combine, slot = slot_front(
        aux_ref[1:2, :1], columns_ref, hidden_ref, length, logits_ref, prob_ref, rows_ref
    )
    end_copy(backflow_ref, up_ref, up_sem)
    mixed = mix_rows(combine, up_ref[...])
    both = jnp.concatenate([to_chunk(slot), to_chunk(mixed)], axis=0).astype(BF)
    send_ref[...] = jnp.broadcast_to(both[None], send_ref.shape)


def gelu_parts(value):
    rate = 0.7978845608028654
    cube = 0.044715
    bent = jnp.tanh(rate * (value + cube * value * value * value))
    half = 0.5 * (1.0 + bent)
    slope = half + 0.5 * value * (1.0 - bent * bent) * rate * (1.0 + 3.0 * cube * value * value)
    return value * half, slope


def expert_early_kernel(
    slots_ref, first_ref, second_ref, send_ref, slot_ref, act_ref, slope_ref, wide_ref
):
    wide_ref[...] = slots_ref[...].astype(F32)
    slots = wide_rows(wide_ref, 0, slots_ref.shape[1]).astype(BF)
    slot_ref[...] = slots
    value, slope = gelu_parts(jnp.dot(slots, first_ref[...], preferred_element_type=F32))
    act = value.astype(BF)
    act_ref[...] = act
    slope_ref[...] = slope
    put_rows(wide_ref, 0, jnp.dot(act, second_ref[...], preferred_element_type=F32))
    send_ref[...] = wide_ref[...].astype(BF)


def expert_late_kernel(
    pairs_ref, first_ref, second_ref, send_ref, slot_ref, mixed_ref, act_ref, grad_ref, wide_ref
):
    chunk = pairs_ref.shape[1] // 2
    wide_ref[...] = pairs_ref[...].astype(F32)
    slots = wide_rows(wide_ref, 0, chunk).astype(BF)
    mixed = wide_rows(wide_ref, chunk, chunk).astype(BF)
    slot_ref[...] = slots
    mixed_ref[...] = mixed
    value, slope = gelu_parts(jnp.dot(slots, first_ref[...], preferred_element_type=F32))
    act = value.astype(BF)
    act_ref[...] = act
    grad = (dot_dims(mixed, second_ref[...], 1, 1) * slope).astype(BF)
    grad_ref[...] = grad
    put_rows(wide_ref, 0, jnp.dot(act, second_ref[...], preferred_element_type=F32))
    put_rows(wide_ref, chunk, dot_dims(grad, first_ref[...], 1, 1))
    send_ref[...] = wide_ref[...].astype(BF)


def expert_back_kernel(
    mixed_in_ref, slope_ref, first_ref, second_ref, send_ref, mixed_ref, grad_ref, wide_ref
):
    wide_ref[...] = mixed_in_ref[...].astype(F32)
    mixed = wide_rows(wide_ref, 0, mixed_in_ref.shape[1]).astype(BF)
    mixed_ref[...] = mixed
    grad = (dot_dims(mixed, second_ref[...], 1, 1) * slope_ref[...]).astype(BF)
    grad_ref[...] = grad
    put_rows(wide_ref, 0, dot_dims(grad, first_ref[...], 1, 1))
    send_ref[...] = wide_ref[...].astype(BF)


def back_body(
    out_row, grad_row, in_ref, hidden_ref, inverse_ref, logits_ref, prob_ref, rows_ref,
    up_ref, columns_ref, aux_ref, hold_ref, pull_ref, mean_ref, put_grads,
):
    gain = aux_ref[:1]
    scale = aux_ref[1:2, :1]
    length = rows_ref[0:1]
    combine = rows_ref[1:2]
    spread = rows_ref[2:3]
    grad_rows = first_rows([grad_row])
    dcombine = dot_dims(first_rows([out_row]), up_ref[...], 1, 1)[:1]
    dspread = dot_dims(grad_rows, hidden_ref[...], 1, 1)[:1].astype(BF).astype(F32)
    first_term = spread * (dspread - jnp.sum(dspread * spread, axis=1, keepdims=True))
    mixed = combine * dcombine
    prob = prob_ref[...]
    top = lax.broadcasted_iota(jnp.int32, prob.shape, 0) == 0
    dlogits = jnp.where(top, mixed + first_term, 0.0) - prob * mixed
    dproduct = dlogits * scale * length
    pull = jnp.sum(dlogits * logits_ref[...], axis=0, keepdims=True) * length * length
    pull_ref[...] = to_column(pull)
    dproduct_bf = dproduct.astype(BF)
    hold_ref[...] = dot_dims(dproduct_bf, columns_ref[...], 0, 0) + dot_dims(
        first_rows([spread]), grad_rows, 0, 0
    )
    router = jnp.dot(dproduct_bf, hidden_ref[...], preferred_element_type=F32)

    def product_rows(index, total):
        window = pl.ds(index * STEP, STEP)
        dhidden = hold_ref[window, :] - hidden_ref[window, :].astype(F32) * pull_ref[window, :1]
        hold_ref[window, :] = dhidden
        product = dhidden * (in_ref[window, :].astype(F32) * inverse_ref[window, :1])
        mean_ref[window, :] = lane_sums(product * gain)
        return total + product[:8] + product[8:]

    gain_sum = lax.fori_loop(
        0, in_ref.shape[0] // STEP, product_rows, jnp.zeros((8, in_ref.shape[1]), F32)
    )
    mean = jnp.sum(mean_ref[...], axis=1, keepdims=True) * (1.0 / in_ref.shape[1])
    mean_ref[...] = jnp.broadcast_to(mean * inverse_ref[...], mean_ref.shape)

    def grad_rows_pass(window):
        inverse = inverse_ref[window, :1]
        through = hold_ref[window, :] * gain
        wide = in_ref[window, :].astype(F32)
        dinput = inverse * (through - wide * mean_ref[window, :1])
        put_grads(window, (up_ref[window, :].astype(F32) + dinput).astype(BF))

    passes(in_ref, grad_rows_pass)
    return router, gain_sum


def back_late_kernel(
    flags_ref, sums_ref, in_ref, hidden_ref, inverse_ref, logits_ref, prob_ref, rows_ref,
    up_ref, columns_ref, aux_ref, before_ref, slot_ref, mixed_ref, act_ref, grad_ref, cotangent_ref,
    send_ref, pack_ref, next_ref,
    own_ref, hold_ref, pull_ref, mean_ref, own_sem,
):
    last = flags_ref[1] != 0

    @pl.when(last)
    def _():
        pltpu.make_async_copy(cotangent_ref.at[0, 0], own_ref, own_sem).start()

    tokens, width = in_ref.shape
    chunk = sums_ref.shape[1] // 2
    total = summed(sums_ref)
    out_row = to_row(total[:chunk])
    grad_row = to_row(total[chunk:])

    @pl.when(last)
    def _():
        end_copy(cotangent_ref.at[0, 0], own_ref, own_sem)

    def put_grads(window, value):
        pack_ref[window, :] = value
        next_ref[window, :] = jnp.where(last, own_ref[window, :], value)

    router, gain_sum = back_body(
        out_row, grad_row, in_ref, hidden_ref, inverse_ref, logits_ref, prob_ref, rows_ref,
        up_ref, columns_ref, aux_ref, hold_ref, pull_ref, mean_ref, put_grads,
    )
    mixed = to_chunk(mix_rows(before_ref[1:2], next_ref[...])).astype(BF)
    send_ref[...] = jnp.broadcast_to(mixed[None], send_ref.shape)
    slots = router.shape[0]
    peers = slot_ref.shape[0]
    pack_ref[tokens : tokens + slots] = router.astype(BF)
    gain_row = jnp.sum(gain_sum, axis=0, keepdims=True)
    place = tokens + slots
    pack_ref[place : place + STEP] = first_rows([*two_parts(gain_row), out_row, grad_row])
    place += STEP
    pack_ref[place : place + peers] = slot_ref[...]
    pack_ref[place + peers : place + 2 * peers] = mixed_ref[...]
    place += 2 * peers
    hidden_units = act_ref.shape[1]
    pack_ref[place : place + peers, :hidden_units] = act_ref[...]
    pack_ref[place : place + peers, hidden_units : 2 * hidden_units] = grad_ref[...]
    rest = jnp.zeros((peers, width - 2 * hidden_units), BF)
    pack_ref[place : place + peers, 2 * hidden_units :] = rest


def back_early_kernel(
    sums_ref, out_ref, in_ref, hidden_ref, inverse_ref, logits_ref, prob_ref, rows_ref,
    up_ref, columns_ref, aux_ref, back_ref,
    grads_ref, outs_ref, send_ref, extra_ref, hold_ref, pull_ref, mean_ref, wide_ref, extra_sem,
):
    tokens = in_ref.shape[0]
    extra = back_ref.at[pl.ds(tokens, extra_ref.shape[0])]
    pltpu.make_async_copy(extra, extra_ref, extra_sem).start()
    chunk = sums_ref.shape[1]
    total = summed(sums_ref)
    outs_ref[...] = total

    def put_grads(window, value):
        grads_ref[window, :] = value

    router, gain_sum = back_body(
        to_row(out_ref[...]), to_row(total), in_ref, hidden_ref, inverse_ref, logits_ref, prob_ref,
        rows_ref, up_ref, columns_ref, aux_ref, hold_ref, pull_ref, mean_ref, put_grads,
    )
    end_copy(extra, extra_ref, extra_sem)
    slots = router.shape[0]
    router = router + extra_ref[:slots].astype(F32)
    peers = send_ref.shape[0]
    count = slots // peers
    for k in range(count):
        put_rows(wide_ref, k * chunk, router[k * peers : (k + 1) * peers])
    late = extra_ref[slots:].astype(F32)
    gain_row = jnp.sum(gain_sum, axis=0, keepdims=True) + late[:1] + late[1:2]
    wide_ref[:, count * chunk :, :] = jnp.broadcast_to(
        to_chunk(gain_row)[None], (peers, chunk, LANES)
    )
    send_ref[...] = wide_ref[...].astype(BF)


def final_kernel(chunks_ref, weights_ref, router_ref, gain_ref):
    weights, inverse = scaled_weights(weights_ref)
    total = jnp.sum(chunks_ref[...].astype(F32), axis=0)
    count = weights.shape[0]
    chunk = weights.shape[1] // LANES
    rows = [to_row(total[k * chunk : (k + 1) * chunk]) for k in range(count)]
    pulled = jnp.concatenate(rows, axis=0)
    dots = jnp.sum(pulled * weights, axis=1, keepdims=True)
    router_ref[...] = (inverse * (pulled - weights * (dots * inverse * inverse))).astype(BF)
    gain_ref[...] = to_row(total[count * chunk :])


def shards(
    tokens,
    cotangent,
    inflow,
    backflow,
    norm_gain,
    slot_scale,
    router_weight,
    expert_in,
    expert_back,
):
    section_index = lax.axis_index("section")
    end = lax.axis_size("section") - 1
    flags = jnp.stack([section_index == 0, section_index == end, section_index == end - 1])
    flags = flags.astype(jnp.int32)
    group = lax.axis_size(DP)
    patches = tokens.shape[2]
    width = tokens.shape[3]
    chunk = width // LANES
    local = router_weight.shape[2]
    slots = local * group
    hidden_units = expert_in.shape[2]
    first_weight = expert_in[0]
    second_weight = expert_back[0]
    weights = router_weight[0].T
    token_block = ((patches, width), BF)
    column = ((patches, LANES), F32)
    table = ((slots, patches), F32)
    rows = ((8, patches), F32)
    single = ((group, chunk, LANES), BF)
    double = ((group, 2 * chunk, LANES), BF)
    every_slot = ((group, width), BF)
    every_hidden = ((group, hidden_units), BF)
    copy_sem = pltpu.SemaphoreType.DMA

    columns_block = run(
        columns_kernel, [((group, local * chunk, LANES), BF)], [], 1000000, 1, weights
    )[0]
    aux = jnp.concatenate(
        [norm_gain, jnp.broadcast_to(slot_scale[:, None], (1, width)), jnp.zeros((6, width), F32)]
    )
    start_in, hidden_early, inverse_early, length_early = run(
        norm_kernel,
        [token_block + ("far",), token_block + ("far",), column, rows],
        [token_block, token_block, column, copy_sem, copy_sem, copy_sem],
        30000000,
        2,
        flags,
        aux,
        tokens,
        inflow,
    )
    ahead = lax.optimization_barrier(
        (length_early, expert_in[0], expert_back[0], backflow[0, 0], aux)
    )
    length_early = ahead[0]
    first_next, second_next, up_next, aux_next = [section_ring(item, -1) for item in ahead[1:]]
    send, columns, logits_early, prob_early, rows_early, base = run(
        early_kernel,
        [single, ((slots, width), BF), table, table, rows, token_block],
        [token_block, ((group, local * chunk, LANES), F32), copy_sem, copy_sem],
        300000000,
        4,
        flags,
        exchange(columns_block, DP),
        length_early,
        aux,
        hidden_early,
        start_in,
        tokens,
    )
    columns_next = section_ring(columns, -1)
    part, slot_early, act_early, slope_early = run(
        expert_early_kernel,
        [single, every_slot, every_hidden, ((group, hidden_units), F32)],
        [((group, chunk, LANES), F32)],
        70000000,
        3,
        exchange(send, DP),
        first_weight,
        second_weight,
    )
    (
        send, late_in, hidden_late, inverse_late, logits_late, prob_late, rows_late, late_up,
        out_early,
    ) = run(
        late_kernel,
        [
            double, token_block, token_block, column, table, table, rows, token_block,
            ((chunk, LANES), F32),
        ],
        [column, column, copy_sem],
        400000000,
        6,
        flags,
        exchange(part, DP),
        rows_early,
        base,
        columns_next,
        aux_next,
        up_next,
        cotangent,
    )
    parts, slot_late, mixed_late, act_late, pre_grad_late = run(
        expert_late_kernel,
        [double, every_slot, every_slot, every_hidden, every_hidden],
        [((group, 2 * chunk, LANES), F32)],
        140000000,
        3,
        exchange(send, DP),
        first_next,
        second_next,
    )
    back_scratch = [((patches, width), F32), column, column]
    pack_rows = patches + slots + STEP + 3 * group
    send, pack, early_up = run(
        back_late_kernel,
        [single, ((pack_rows, width), BF), token_block],
        [token_block] + back_scratch + [copy_sem],
        600000000,
        16,
        flags,
        exchange(parts, DP),
        late_in,
        hidden_late,
        inverse_late,
        logits_late,
        prob_late,
        rows_late,
        late_up,
        columns_next,
        aux_next,
        rows_early,
        slot_late,
        mixed_late,
        act_late,
        pre_grad_late,
        cotangent,
    )
    back = section_ring(pack, 1)
    part, mixed_early_all, pre_grad_early = run(
        expert_back_kernel,
        [single, every_slot, every_hidden],
        [((group, chunk, LANES), F32)],
        70000000,
        4,
        exchange(send, DP),
        slope_early,
        first_weight,
        second_weight,
    )
    last_rows = (local + 1) * chunk
    grads_early, outs_early, finals = run(
        back_early_kernel,
        [token_block, ((chunk, LANES), F32), ((group, last_rows, LANES), BF)],
        [((slots + STEP, width), BF)]
        + back_scratch
        + [((group, last_rows, LANES), F32), copy_sem],
        600000000,
        11,
        exchange(part, DP),
        out_early,
        start_in,
        hidden_early,
        inverse_early,
        logits_early,
        prob_early,
        rows_early,
        early_up,
        columns,
        aux,
        back,
    )
    router_grad, gain_total = run(
        final_kernel,
        [((local, width), BF), ((1, width), F32)],
        [],
        1000000,
        2,
        exchange(finals, DP),
        weights,
    )

    place = patches + slots
    grads_late = back[:patches]
    out_late = back[place + 2 : place + 3]
    slot_grad_late = back[place + 3 : place + 4]
    place += STEP
    slot_late = back[place : place + group]
    mixed_late = back[place + group : place + 2 * group]
    place += 2 * group
    act_late = back[place:, :hidden_units]
    pre_grad_late = back[place:, hidden_units : 2 * hidden_units]
    first_grad = dot_dims(
        jnp.concatenate([slot_early, slot_late], axis=0),
        jnp.concatenate([pre_grad_early, pre_grad_late], axis=0),
        0,
        0,
    )
    second_grad = dot_dims(
        jnp.concatenate([act_early, act_late], axis=0),
        jnp.concatenate([mixed_early_all, mixed_late], axis=0),
        0,
        0,
    )
    slot_out = jnp.stack([out_early.reshape(1, width).astype(BF), out_late])
    slot_grad = jnp.stack([outs_early.reshape(1, width).astype(BF), slot_grad_late])
    return (
        jnp.stack([grads_early, grads_late])[None, :, None],
        slot_out[None],
        slot_grad[None],
        first_grad.astype(BF)[None],
        second_grad.astype(BF)[None],
        router_grad.T[None],
        gain_total,
    )


def solution(mesh):
    fine = Mesh(mesh.devices.reshape(mesh.shape["section"], 2, 4, 4), AXES)
    in_specs = (
        P(None, DP, None, None),
        P(None, DP, None, None),
        P("section", DP, None, None),
        P("section", DP, None, None),
        P("section", None),
        P("section"),
        P("section", None, DP),
        P("section", None, DP),
        P("section", DP, None),
    )
    out_specs = (
        P("section", None, DP, None, None),
        P("section", None, DP, None),
        P("section", None, DP, None),
        P("section", None, DP),
        P("section", DP, None),
        P("section", None, DP),
        P("section", None),
    )
    return jax.shard_map(shards, mesh=fine, in_specs=in_specs, out_specs=out_specs, check_vma=False)
```

```python
import jax
import jax.numpy as jnp
from jax import lax
from jax.experimental import pallas as pl
from jax.experimental.pallas import tpu as pltpu
from jax.sharding import Mesh
from jax.sharding import PartitionSpec as P

EPSILON = 1e-06
BF = jnp.bfloat16
F32 = jnp.float32
AXES = ("section", "zh", "y", "x")
DP = ("zh", "y", "x")
LANES = 128
STEP = 16
VMEM_BYTES = 24 * 1024 * 1024
VMEM_MOST = 58 * 1024 * 1024


def dot_dims(left_side, right_side, left_dim, right_dim):
    return lax.dot_general(
        left_side,
        right_side,
        (((left_dim,), (right_dim,)), ((), ())),
        preferred_element_type=F32,
    )


def exchange(chunks, axes):
    return lax.all_to_all(chunks, axes, 0, 0, tiled=True)


def section_shift(block, distance):
    sections = lax.axis_size("section")
    route = [(i, i + distance) for i in range(sections) if 0 <= i + distance < sections]
    return lax.ppermute(block, "section", route)


def section_ring(block, distance):
    sections = lax.axis_size("section")
    return lax.ppermute(block, "section", [(i, (i + distance) % sections) for i in range(sections)])


def run(body, outs, scratch, flops, near, *operands, vmem=VMEM_BYTES):
    def place(index, item):
        if item.ndim == 1:
            return pltpu.SMEM
        return pltpu.VMEM if index < near else pl.ANY

    return pl.pallas_call(
        body,
        out_shape=[jax.ShapeDtypeStruct(item[0], item[1]) for item in outs],
        in_specs=[
            pl.BlockSpec(memory_space=place(index, item)) for index, item in enumerate(operands)
        ],
        out_specs=[
            pl.BlockSpec(memory_space=pltpu.VMEM if len(item) == 2 else pl.ANY) for item in outs
        ],
        scratch_shapes=[
            pltpu.VMEM(*item) if isinstance(item, tuple) else item for item in scratch
        ],
        compiler_params=pltpu.CompilerParams(vmem_limit_bytes=vmem),
        cost_estimate=pl.CostEstimate(flops=flops, bytes_accessed=4000000, transcendentals=0),
    )(*operands)


def to_chunk(row):
    count = row.shape[1] // LANES
    return jnp.concatenate([row[:, k * LANES : (k + 1) * LANES] for k in range(count)], axis=0)


def to_row(chunk):
    return jnp.concatenate([chunk[k : k + 1, :] for k in range(chunk.shape[0])], axis=1)


def to_column(row):
    return jnp.transpose(jnp.broadcast_to(row, (LANES, row.shape[1])))


def stack_rows(rows, count, kind):
    filler = jnp.zeros((count - len(rows), rows[0].shape[1]), F32)
    return jnp.concatenate(list(rows) + [filler], axis=0).astype(kind)


def first_rows(rows):
    return stack_rows(rows, STEP, BF)


def wide_rows(ref, offset, count):
    return jnp.concatenate([ref[:, offset + k, :] for k in range(count)], axis=1)


def put_rows(ref, offset, value):
    for k in range(value.shape[1] // LANES):
        ref[:, offset + k, :] = value[:, k * LANES : (k + 1) * LANES]


def two_parts(row):
    high = row.astype(BF).astype(F32)
    return high, row - high


def lane_sums(value):
    parts = [value[:, k * LANES : (k + 1) * LANES] for k in range(value.shape[1] // LANES)]
    while len(parts) > 1:
        parts = [x + y for x, y in zip(parts[::2], parts[1::2])]
    return parts[0]


def summed(chunks_ref):
    return jnp.sum(chunks_ref[...].astype(F32), axis=0).astype(BF).astype(F32)


def passes(ref, body):
    @pl.loop(0, ref.shape[0] // STEP, unroll=8)
    def _(index):
        body(pl.ds(index * STEP, STEP))


def begin_copy(flag, yes, no, target, sem):
    @pl.when(flag != 0)
    def _():
        pltpu.make_async_copy(yes, target, sem).start()

    @pl.when(flag == 0)
    def _():
        pltpu.make_async_copy(no, target, sem).start()


def end_copy(source, target, sem):
    pltpu.make_async_copy(source, target, sem).wait()


def scaled_weights(weights_ref):
    weights = weights_ref[...].astype(F32)
    total = jnp.sum(weights * weights, axis=1, keepdims=True)
    return weights, lax.rsqrt(total + EPSILON)


def columns_kernel(weights_ref, send_ref):
    weights, inverse = scaled_weights(weights_ref)
    columns = weights * inverse
    rows = [to_chunk(columns[k : k + 1]) for k in range(columns.shape[0])]
    block = jnp.concatenate(rows, axis=0).astype(BF)
    send_ref[...] = jnp.broadcast_to(block[None], send_ref.shape)


def norm_passes(in_ref, gain, hidden_ref, inverse_ref, sums_ref):
    rate = 1.0 / in_ref.shape[1]
    inverse = lax.rsqrt(jnp.sum(sums_ref[...], axis=1, keepdims=True) * rate + EPSILON)
    inverse_ref[...] = jnp.broadcast_to(inverse, inverse_ref.shape)

    def scale_rows(window):
        wide = in_ref[window, :].astype(F32)
        hidden = (wide * inverse_ref[window, :1] * gain).astype(BF)
        hidden_ref[window, :] = hidden
        hidden_f = hidden.astype(F32)
        sums_ref[window, :] = lane_sums(hidden_f * hidden_f)

    passes(in_ref, scale_rows)
    total = jnp.sum(jnp.transpose(sums_ref[...]), axis=0, keepdims=True)
    return lax.rsqrt(total + EPSILON)


def slot_front(scale, columns_ref, hidden_ref, length, logits_ref, prob_ref, rows_ref):
    product = dot_dims(columns_ref[...], hidden_ref[...], 1, 1)
    logits = scale * product * length
    expo = jnp.exp(logits)
    first = expo[:1]
    norm = jnp.sum(expo, axis=0, keepdims=True)
    combine = first / norm
    spread = first / jnp.sum(first, axis=1, keepdims=True)
    logits_ref[...] = logits
    prob_ref[...] = expo / norm
    rows_ref[...] = stack_rows([length, combine, spread], 8, F32)
    slot = jnp.dot(first_rows([spread]), hidden_ref[...], preferred_element_type=F32)
    return combine, slot[:1]


def mix_rows(combine, upstream):
    mixed = jnp.dot(first_rows(two_parts(combine)), upstream, preferred_element_type=F32)
    return mixed[:1] + mixed[1:2]


def norm_kernel(
    flags_ref, gain_ref, tokens_ref, inflow_ref,
    start_ref, hidden_out, inverse_ref, length_ref,
    in_ref, hidden_ref, sums_ref, in_sem, out_sem, hidden_sem,
):
    begin_copy(flags_ref[0], tokens_ref.at[0, 0], inflow_ref.at[0, 0], in_ref, in_sem)
    end_copy(inflow_ref.at[0, 0], in_ref, in_sem)
    pltpu.make_async_copy(in_ref, start_ref, out_sem).start()

    def square_rows(window):
        wide = in_ref[window, :].astype(F32)
        sums_ref[window, :] = lane_sums(wide * wide)

    passes(in_ref, square_rows)
    length = norm_passes(in_ref, gain_ref[...], hidden_ref, inverse_ref, sums_ref)
    length_ref[...] = jnp.broadcast_to(length, length_ref.shape)
    pltpu.make_async_copy(hidden_ref, hidden_out, hidden_sem).start()
    end_copy(in_ref, start_ref, out_sem)
    end_copy(hidden_ref, hidden_out, hidden_sem)


def early_kernel(
    scale_ref, chunks_ref, length_ref, hidden_in,
    send_ref, columns_ref, logits_ref, prob_ref, rows_ref,
    hidden_ref, wide_ref, hidden_sem,
):
    pltpu.make_async_copy(hidden_in, hidden_ref, hidden_sem).start()
    peers = chunks_ref.shape[0]
    chunk = hidden_ref.shape[1] // LANES
    wide_ref[...] = chunks_ref[...].astype(F32)
    for k in range(chunks_ref.shape[1] // chunk):
        columns_ref[k * peers : (k + 1) * peers] = wide_rows(wide_ref, k * chunk, chunk).astype(BF)
    end_copy(hidden_in, hidden_ref, hidden_sem)
    _, slot = slot_front(
        scale_ref[0], columns_ref, hidden_ref, length_ref[:1], logits_ref, prob_ref, rows_ref
    )
    send_ref[...] = jnp.broadcast_to(to_chunk(slot).astype(BF)[None], send_ref.shape)


def join_rows(parts, out_ref):
    count = sum(part.shape[0] for part in parts)
    filler = jnp.zeros((out_ref.shape[0] - count, LANES), F32)
    out_ref[...] = jnp.concatenate([*parts, filler], axis=0)


def pack_kernel(sums_ref, rows_ref, out_ref):
    join_rows([summed(sums_ref), to_chunk(rows_ref[1:2])], out_ref)


def late_kernel(
    scale_ref, flags_ref, base_ref, moved_ref, columns_ref, gain_ref, cotangent_ref, backflow_ref,
    send_ref, in_ref, hidden_ref, inverse_ref, logits_ref, prob_ref, rows_ref, up_ref,
    sums_ref, comb_ref, up_sem,
):
    begin_copy(flags_ref[1], cotangent_ref.at[1, 0], backflow_ref.at[0, 0], up_ref, up_sem)
    chunk = gain_ref.shape[1] // LANES
    out_row = to_row(moved_ref[:chunk])
    before = to_row(moved_ref[chunk : chunk + 2])
    comb_ref[...] = to_column(jnp.where(flags_ref[0] != 0, jnp.zeros_like(before), before))

    def add_rows(window):
        base = base_ref[window, :].astype(F32)
        value = (base + comb_ref[window, :1] * out_row).astype(BF)
        in_ref[window, :] = value
        wide = value.astype(F32)
        sums_ref[window, :] = lane_sums(wide * wide)

    passes(in_ref, add_rows)
    length = norm_passes(in_ref, gain_ref[...], hidden_ref, inverse_ref, sums_ref)
    combine, slot = slot_front(
        scale_ref[0], columns_ref, hidden_ref, length, logits_ref, prob_ref, rows_ref
    )
    end_copy(backflow_ref.at[0, 0], up_ref, up_sem)
    mixed = mix_rows(combine, up_ref[...])
    both = jnp.concatenate([to_chunk(slot), to_chunk(mixed)], axis=0).astype(BF)
    send_ref[...] = jnp.broadcast_to(both[None], send_ref.shape)


def gelu_parts(value):
    rate = 0.7978845608028654
    cube = 0.044715
    bent = jnp.tanh(rate * (value + cube * value * value * value))
    half = 0.5 * (1.0 + bent)
    slope = half + 0.5 * value * (1.0 - bent * bent) * rate * (1.0 + 3.0 * cube * value * value)
    return value * half, slope


def expert_early_kernel(
    slots_ref, first_ref, second_ref, send_ref, slot_ref, act_ref, slope_ref, wide_ref
):
    wide_ref[...] = slots_ref[...].astype(F32)
    slots = wide_rows(wide_ref, 0, slots_ref.shape[1]).astype(BF)
    slot_ref[...] = slots
    value, slope = gelu_parts(jnp.dot(slots, first_ref[...], preferred_element_type=F32))
    act = value.astype(BF)
    act_ref[...] = act
    slope_ref[...] = slope
    put_rows(wide_ref, 0, jnp.dot(act, second_ref[...], preferred_element_type=F32))
    send_ref[...] = wide_ref[...].astype(BF)


def expert_late_kernel(
    pairs_ref, first_ref, second_ref, send_ref, slot_ref, mixed_ref, act_ref, grad_ref, wide_ref
):
    chunk = pairs_ref.shape[1] // 2
    wide_ref[...] = pairs_ref[...].astype(F32)
    slots = wide_rows(wide_ref, 0, chunk).astype(BF)
    mixed = wide_rows(wide_ref, chunk, chunk).astype(BF)
    slot_ref[...] = slots
    mixed_ref[...] = mixed
    value, slope = gelu_parts(jnp.dot(slots, first_ref[...], preferred_element_type=F32))
    act = value.astype(BF)
    act_ref[...] = act
    grad = (dot_dims(mixed, second_ref[...], 1, 1) * slope).astype(BF)
    grad_ref[...] = grad
    put_rows(wide_ref, 0, jnp.dot(act, second_ref[...], preferred_element_type=F32))
    put_rows(wide_ref, chunk, dot_dims(grad, first_ref[...], 1, 1))
    send_ref[...] = wide_ref[...].astype(BF)


def expert_back_kernel(
    mixed_in_ref, slope_ref, first_ref, second_ref, send_ref, mixed_ref, grad_ref, wide_ref
):
    wide_ref[...] = mixed_in_ref[...].astype(F32)
    mixed = wide_rows(wide_ref, 0, mixed_in_ref.shape[1]).astype(BF)
    mixed_ref[...] = mixed
    grad = (dot_dims(mixed, second_ref[...], 1, 1) * slope_ref[...]).astype(BF)
    grad_ref[...] = grad
    put_rows(wide_ref, 0, dot_dims(grad, first_ref[...], 1, 1))
    send_ref[...] = wide_ref[...].astype(BF)


def spread_kernel(flags_ref, moved_ref, own_ref, send_ref, kept_ref):
    block = jnp.where(flags_ref[1] != 0, own_ref[...], moved_ref[...])
    kept_ref[...] = block
    send_ref[...] = jnp.broadcast_to(block[: send_ref.shape[1]].astype(BF)[None], send_ref.shape)


def row_dots(pairs):
    def body(window):
        for ref, row, sums_ref in pairs:
            sums_ref[window, :] = lane_sums(ref[window, :].astype(F32) * row)

    passes(pairs[0][0], body)
    return [jnp.sum(jnp.transpose(sums_ref[...]), axis=0, keepdims=True) for _, _, sums_ref in pairs]


def back_body(
    scale, dcombine, dspread, grad_row, in_ref, hidden_ref, inverse_ref, logits_ref, prob_ref, rows_ref,
    columns_ref, gain_ref, hold_ref, pull_ref, mean_ref, put_grads,
):
    gain = gain_ref[...]
    length = rows_ref[0:1]
    combine = rows_ref[1:2]
    spread = rows_ref[2:3]
    grad_rows = first_rows([grad_row])
    dspread = dspread.astype(BF).astype(F32)
    first_term = spread * (dspread - jnp.sum(dspread * spread, axis=1, keepdims=True))
    mixed = combine * dcombine
    prob = prob_ref[...]
    top = lax.broadcasted_iota(jnp.int32, prob.shape, 0) == 0
    dlogits = jnp.where(top, mixed + first_term, 0.0) - prob * mixed
    dproduct = dlogits * scale * length
    pull = jnp.sum(dlogits * logits_ref[...], axis=0, keepdims=True) * length * length
    pull_ref[...] = to_column(pull)
    dproduct_bf = dproduct.astype(BF)
    hold_ref[...] = dot_dims(dproduct_bf, columns_ref[...], 0, 0) + dot_dims(
        first_rows([spread]), grad_rows, 0, 0
    )
    router = jnp.dot(dproduct_bf, hidden_ref[...], preferred_element_type=F32)

    def product_rows(index, total):
        window = pl.ds(index * STEP, STEP)
        dhidden = hold_ref[window, :] - hidden_ref[window, :].astype(F32) * pull_ref[window, :1]
        hold_ref[window, :] = dhidden
        product = dhidden * (in_ref[window, :].astype(F32) * inverse_ref[window, :1])
        mean_ref[window, :] = lane_sums(product * gain)
        return total + product[:8] + product[8:]

    gain_sum = lax.fori_loop(
        0, in_ref.shape[0] // STEP, product_rows, jnp.zeros((8, in_ref.shape[1]), F32), unroll=4
    )
    mean = jnp.sum(mean_ref[...], axis=1, keepdims=True) * (1.0 / in_ref.shape[1])
    mean_ref[...] = jnp.broadcast_to(mean * inverse_ref[...], mean_ref.shape)

    def grad_rows_pass(window):
        inverse = inverse_ref[window, :1]
        through = hold_ref[window, :] * gain
        wide = in_ref[window, :].astype(F32)
        dinput = inverse * (through - wide * mean_ref[window, :1])
        put_grads(window, dinput)

    passes(in_ref, grad_rows_pass)
    return router, gain_sum


def back_late_kernel(
    scale_ref, flags_ref, sums_ref, in_ref, hidden_ref, inverse_ref, logits_ref, prob_ref,
    rows_ref, up_ref, columns_ref, gain_ref, moved_ref, rows_own_ref, packed_ref, cotangent_ref,
    grads_ref, moved_out, own_out, outs_ref, router_ref, gain_out,
    own_ref, hold_ref, pull_ref, mean_ref, own_sem,
):
    last = flags_ref[1] != 0

    @pl.when(last)
    def _():
        pltpu.make_async_copy(cotangent_ref.at[0, 0], own_ref, own_sem).start()

    chunk = sums_ref.shape[1] // 2
    total = summed(sums_ref)
    outs_ref[...] = total

    def put_grads(window, dinput):
        grads_ref[window, :] = (up_ref[window, :].astype(F32) + dinput).astype(BF)

    grad_row = to_row(total[chunk:])
    dcombine, dspread = row_dots(
        [(up_ref, to_row(total[:chunk]), pull_ref), (hidden_ref, grad_row, mean_ref)]
    )
    router, gain_sum = back_body(
        scale_ref[0], dcombine, dspread, grad_row, in_ref, hidden_ref, inverse_ref, logits_ref,
        prob_ref, rows_ref, columns_ref, gain_ref, hold_ref, pull_ref, mean_ref, put_grads,
    )

    def message(combine, out_row, ref, out):
        mixed = to_chunk(mix_rows(combine, ref[...]).astype(BF).astype(F32))
        join_rows([mixed, to_chunk(row_dots([(ref, out_row, mean_ref)])[0])], out)

    combine = to_row(moved_ref[chunk : chunk + 2])
    message(combine, to_row(moved_ref[:chunk]), grads_ref, moved_out)
    router_ref[...] = router
    gain_out[...] = gain_sum
    own_out[...] = jnp.zeros_like(own_out)

    @pl.when(last)
    def _():
        end_copy(cotangent_ref.at[0, 0], own_ref, own_sem)
        message(rows_own_ref[1:2], to_row(packed_ref[:chunk]), own_ref, own_out)


def back_early_kernel(
    scale_ref, sums_ref, kept_ref, in_ref, hidden_ref, inverse_ref, logits_ref, prob_ref,
    rows_ref, columns_ref, gain_ref, router_in_ref, gain_in_ref,
    dinput_ref, outs_ref, send_ref, hold_ref, pull_ref, mean_ref, wide_ref,
):
    chunk = sums_ref.shape[1]
    total = summed(sums_ref)
    outs_ref[...] = total

    def put_grads(window, dinput):
        dinput_ref[window, :] = dinput.astype(BF)

    grad_row = to_row(total)
    (dspread,) = row_dots([(hidden_ref, grad_row, mean_ref)])
    router, gain_sum = back_body(
        scale_ref[0], to_row(kept_ref[chunk : chunk + 2]), dspread, grad_row, in_ref, hidden_ref,
        inverse_ref, logits_ref, prob_ref, rows_ref, columns_ref, gain_ref, hold_ref, pull_ref,
        mean_ref, put_grads,
    )
    router = router + router_in_ref[...]
    peers = send_ref.shape[0]
    count = router.shape[0] // peers
    for k in range(count):
        put_rows(wide_ref, k * chunk, router[k * peers : (k + 1) * peers])
    send_ref[:, : count * chunk, :] = wide_ref[...].astype(BF)
    gain_row = jnp.sum(gain_sum + gain_in_ref[...], axis=0, keepdims=True)
    send_ref[:, count * chunk :, :] = jnp.broadcast_to(
        to_chunk(gain_row).astype(BF)[None], (peers, chunk, LANES)
    )


def final_kernel(chunks_ref, weights_ref, router_ref, gain_ref):
    weights, inverse = scaled_weights(weights_ref)
    total = jnp.sum(chunks_ref[...].astype(F32), axis=0)
    count = weights.shape[0]
    chunk = weights.shape[1] // LANES
    rows = [to_row(total[k * chunk : (k + 1) * chunk]) for k in range(count)]
    pulled = jnp.concatenate(rows, axis=0)
    dots = jnp.sum(pulled * weights, axis=1, keepdims=True)
    router_ref[...] = (inverse * (pulled - weights * (dots * inverse * inverse))).astype(BF)
    gain_ref[...] = to_row(total[count * chunk :])


def shards(
    tokens,
    cotangent,
    inflow,
    backflow,
    norm_gain,
    slot_scale,
    router_weight,
    expert_in,
    expert_back,
):
    section_index = lax.axis_index("section")
    is_first = section_index == 0
    is_last = section_index == lax.axis_size("section") - 1
    flags = jnp.stack([is_first, is_last]).astype(jnp.int32)
    group = lax.axis_size(DP)
    patches = tokens.shape[2]
    width = tokens.shape[3]
    chunk = width // LANES
    local = router_weight.shape[2]
    slots = local * group
    hidden_units = expert_in.shape[2]
    first_weight = expert_in[0]
    second_weight = expert_back[0]
    weights = router_weight[0].T
    token_block = ((patches, width), BF)
    column = ((patches, LANES), F32)
    table = ((slots, patches), F32)
    rows = ((8, patches), F32)
    single = ((group, chunk, LANES), BF)
    double = ((group, 2 * chunk, LANES), BF)
    every_slot = ((group, width), BF)
    every_hidden = ((group, hidden_units), BF)
    copy_sem = pltpu.SemaphoreType.DMA

    columns_block = run(
        columns_kernel, [((group, local * chunk, LANES), BF)], [], 1000000, 1, weights
    )[0]
    start_in, hidden_early, inverse_early, length_early = run(
        norm_kernel,
        [token_block + ("far",), token_block + ("far",), column, rows],
        [token_block, token_block, column, copy_sem, copy_sem, copy_sem],
        30000000,
        2,
        flags,
        norm_gain,
        tokens,
        inflow,
        vmem=VMEM_MOST,
    )
    sent_in = section_shift(start_in, 1)
    send, columns, logits_early, prob_early, rows_early = run(
        early_kernel,
        [single, ((slots, width), BF), table, table, rows],
        [token_block, ((group, local * chunk, LANES), F32), copy_sem],
        300000000,
        3,
        slot_scale,
        exchange(columns_block, DP),
        length_early,
        hidden_early,
    )
    part, slot_early, act_early, slope_early = run(
        expert_early_kernel,
        [single, every_slot, every_hidden, ((group, hidden_units), F32)],
        [((group, chunk, LANES), F32)],
        70000000,
        3,
        exchange(send, DP),
        first_weight,
        second_weight,
    )
    packed = run(
        pack_kernel, [((chunk + 8, LANES), F32)], [], 1000000, 2, exchange(part, DP), rows_early
    )[0]
    moved = section_ring(packed, 1)

    base = jnp.where(is_first, tokens[1, 0], sent_in)
    (
        send, late_in, hidden_late, inverse_late, logits_late, prob_late, rows_late, late_up,
    ) = run(
        late_kernel,
        [double, token_block, token_block, column, table, table, rows, token_block],
        [column, column, copy_sem],
        400000000,
        6,
        slot_scale,
        flags,
        base,
        moved,
        columns,
        norm_gain,
        cotangent,
        backflow,
    )
    parts, slot_late, mixed_late, act_late, pre_grad_late = run(
        expert_late_kernel,
        [double, every_slot, every_slot, every_hidden, every_hidden],
        [((group, 2 * chunk, LANES), F32)],
        140000000,
        3,
        exchange(send, DP),
        first_weight,
        second_weight,
    )
    back_scratch = [((patches, width), F32), column, column]
    message = ((chunk + 8, LANES), F32)
    grads_late, moved_back, own_back, outs_late, router_late, gain_late = run(
        back_late_kernel,
        [
            token_block, message, message, ((2 * chunk, LANES), F32), ((slots, width), F32),
            ((8, width), F32),
        ],
        [token_block] + back_scratch + [copy_sem],
        600000000,
        15,
        slot_scale,
        flags,
        exchange(parts, DP),
        late_in,
        hidden_late,
        inverse_late,
        logits_late,
        prob_late,
        rows_late,
        late_up,
        columns,
        norm_gain,
        moved,
        rows_early,
        packed,
        cotangent,
    )
    send, kept = run(
        spread_kernel, [single, message], [], 1000000, 3, flags, section_ring(moved_back, -1), own_back
    )
    part, mixed_early_all, pre_grad_early = run(
        expert_back_kernel,
        [single, every_slot, every_hidden],
        [((group, chunk, LANES), F32)],
        70000000,
        4,
        exchange(send, DP),
        slope_early,
        first_weight,
        second_weight,
    )
    last_rows = (local + 1) * chunk
    slot_sums, held_grads = lax.optimization_barrier((exchange(part, DP), grads_late))
    sent_grads = section_shift(held_grads, -1)
    dinput, outs_early, finals = run(
        back_early_kernel,
        [token_block, ((chunk, LANES), F32), ((group, last_rows, LANES), BF)],
        back_scratch + [((group, local * chunk, LANES), F32)],
        600000000,
        13,
        slot_scale,
        slot_sums,
        kept,
        start_in,
        hidden_early,
        inverse_early,
        logits_early,
        prob_early,
        rows_early,
        columns,
        norm_gain,
        router_late,
        gain_late,
    )
    router_grad, gain_total = run(
        final_kernel,
        [((local, width), BF), ((1, width), F32)],
        [],
        1000000,
        2,
        exchange(finals, DP),
        weights,
    )

    (
        dinput, outs_early, outs_late, packed, slot_early, slot_late, pre_grad_early, pre_grad_late,
        act_early, act_late, mixed_early_all, mixed_late,
    ) = lax.optimization_barrier(
        (
            dinput, outs_early, outs_late, packed, slot_early, slot_late, pre_grad_early,
            pre_grad_late, act_early, act_late, mixed_early_all, mixed_late,
        )
    )
    early_up = jnp.where(is_last, cotangent[0, 0], sent_grads).astype(F32)
    grads_early = (early_up + dinput.astype(F32)).astype(BF)
    first_grad = dot_dims(
        jnp.concatenate([slot_early, slot_late], axis=0),
        jnp.concatenate([pre_grad_early, pre_grad_late], axis=0),
        0,
        0,
    )
    second_grad = dot_dims(
        jnp.concatenate([act_early, act_late], axis=0),
        jnp.concatenate([mixed_early_all, mixed_late], axis=0),
        0,
        0,
    )
    slot_out = jnp.stack([packed[:chunk].reshape(1, width), outs_late[:chunk].reshape(1, width)])
    slot_grad = jnp.stack([outs_early.reshape(1, width), outs_late[chunk:].reshape(1, width)])
    return (
        jnp.stack([grads_early, grads_late])[None, :, None],
        slot_out.astype(BF)[None],
        slot_grad.astype(BF)[None],
        first_grad.astype(BF)[None],
        second_grad.astype(BF)[None],
        router_grad.T[None],
        gain_total,
    )


def solution(mesh):
    fine = Mesh(mesh.devices.reshape(mesh.shape["section"], 2, 4, 4), AXES)
    in_specs = (
        P(None, DP, None, None),
        P(None, DP, None, None),
        P("section", DP, None, None),
        P("section", DP, None, None),
        P("section", None),
        P("section"),
        P("section", None, DP),
        P("section", None, DP),
        P("section", DP, None),
    )
    out_specs = (
        P("section", None, DP, None, None),
        P("section", None, DP, None),
        P("section", None, DP, None),
        P("section", None, DP),
        P("section", DP, None),
        P("section", None, DP),
        P("section", None),
    )
    return jax.shard_map(shards, mesh=fine, in_specs=in_specs, out_specs=out_specs, check_vma=False)
```

```python
import jax
import jax.numpy as jnp
from jax import lax
from jax.experimental import pallas as pl
from jax.experimental.pallas import tpu as pltpu
from jax.sharding import Mesh
from jax.sharding import PartitionSpec as P

EPSILON = 1e-06
BF = jnp.bfloat16
F32 = jnp.float32
AXES = ("section", "zh", "y", "x")
DP = ("zh", "y", "x")
PLANE = ("y", "x")
LANES = 128
STEP = 16
VMEM_BYTES = 24 * 1024 * 1024
VMEM_NORM = VMEM_BYTES


def dot_dims(left_side, right_side, left_dim, right_dim):
    return lax.dot_general(
        left_side,
        right_side,
        (((left_dim,), (right_dim,)), ((), ())),
        preferred_element_type=F32,
    )


def exchange(chunks, axes):
    return lax.all_to_all(chunks, axes, 0, 0, tiled=True)


def section_shift(block, distance):
    sections = lax.axis_size("section")
    route = [(i, i + distance) for i in range(sections) if 0 <= i + distance < sections]
    return lax.ppermute(block, "section", route)


def other_half(block):
    return lax.ppermute(block, "zh", [(0, 1), (1, 0)])


def section_ring(block, distance):
    sections = lax.axis_size("section")
    return lax.ppermute(block, "section", [(i, (i + distance) % sections) for i in range(sections)])


def run(body, outs, scratch, flops, near, *operands, vmem=VMEM_BYTES):
    def place(index, item):
        if item.ndim == 1:
            return pltpu.SMEM
        return pltpu.VMEM if index < near else pl.ANY

    return pl.pallas_call(
        body,
        out_shape=[jax.ShapeDtypeStruct(item[0], item[1]) for item in outs],
        in_specs=[
            pl.BlockSpec(memory_space=place(index, item)) for index, item in enumerate(operands)
        ],
        out_specs=[
            pl.BlockSpec(memory_space=pltpu.VMEM if len(item) == 2 else pl.ANY) for item in outs
        ],
        scratch_shapes=[
            pltpu.VMEM(*item) if isinstance(item, tuple) else item for item in scratch
        ],
        compiler_params=pltpu.CompilerParams(vmem_limit_bytes=vmem),
        cost_estimate=pl.CostEstimate(flops=flops, bytes_accessed=4000000, transcendentals=0),
    )(*operands)


def to_chunk(row):
    count = row.shape[1] // LANES
    return jnp.concatenate([row[:, k * LANES : (k + 1) * LANES] for k in range(count)], axis=0)


def to_row(chunk):
    return jnp.concatenate([chunk[k : k + 1, :] for k in range(chunk.shape[0])], axis=1)


def to_column(row):
    return jnp.transpose(jnp.broadcast_to(row, (LANES, row.shape[1])))


def stack_rows(rows, count, kind):
    filler = jnp.zeros((count - len(rows), rows[0].shape[1]), F32)
    return jnp.concatenate(list(rows) + [filler], axis=0).astype(kind)


def first_rows(rows):
    return stack_rows(rows, STEP, BF)


def wide_rows(ref, offset, count):
    return jnp.concatenate([ref[:, offset + k, :] for k in range(count)], axis=1)


def put_rows(ref, offset, value):
    for k in range(value.shape[1] // LANES):
        ref[:, offset + k, :] = value[:, k * LANES : (k + 1) * LANES]


def two_parts(row):
    high = row.astype(BF).astype(F32)
    return high, row - high


def lane_sums(value):
    parts = [value[:, k * LANES : (k + 1) * LANES] for k in range(value.shape[1] // LANES)]
    while len(parts) > 1:
        parts = [x + y for x, y in zip(parts[::2], parts[1::2])]
    return parts[0]


def summed(chunks_ref):
    return jnp.sum(chunks_ref[...].astype(F32), axis=0).astype(BF).astype(F32)


def passes(ref, body):
    @pl.loop(0, ref.shape[0] // STEP, unroll=8)
    def _(index):
        body(pl.ds(index * STEP, STEP))


def begin_copy(flag, yes, no, target, sem):
    @pl.when(flag != 0)
    def _():
        pltpu.make_async_copy(yes, target, sem).start()

    @pl.when(flag == 0)
    def _():
        pltpu.make_async_copy(no, target, sem).start()


def end_copy(source, target, sem):
    pltpu.make_async_copy(source, target, sem).wait()


def scaled_weights(weights_ref):
    weights = weights_ref[...].astype(F32)
    total = jnp.sum(weights * weights, axis=1, keepdims=True)
    return weights, lax.rsqrt(total + EPSILON)


def columns_kernel(weights_ref, send_ref):
    weights, inverse = scaled_weights(weights_ref)
    columns = weights * inverse
    rows = [to_chunk(columns[k : k + 1]) for k in range(columns.shape[0])]
    send_ref[...] = jnp.concatenate(rows, axis=0).astype(BF)


def order_kernel(flags_ref, own_ref, other_ref, send_ref):
    own = own_ref[...].astype(F32)
    other = other_ref[...].astype(F32)
    upper = flags_ref[2] != 0
    pair = [jnp.where(upper, other, own), jnp.where(upper, own, other)]
    block = jnp.concatenate(pair, axis=0).astype(BF)
    send_ref[...] = jnp.broadcast_to(block[None], send_ref.shape)


def norm_passes(in_ref, gain, hidden_ref, inverse_ref, sums_ref):
    rate = 1.0 / in_ref.shape[1]
    inverse = lax.rsqrt(jnp.sum(sums_ref[...], axis=1, keepdims=True) * rate + EPSILON)
    inverse_ref[...] = jnp.broadcast_to(inverse, inverse_ref.shape)

    def scale_rows(window):
        wide = in_ref[window, :].astype(F32)
        hidden = (wide * inverse_ref[window, :1] * gain).astype(BF)
        hidden_ref[window, :] = hidden
        hidden_f = hidden.astype(F32)
        sums_ref[window, :] = lane_sums(hidden_f * hidden_f)

    passes(in_ref, scale_rows)
    total = jnp.sum(jnp.transpose(sums_ref[...]), axis=0, keepdims=True)
    return lax.rsqrt(total + EPSILON)


def slot_front(scaled, columns_ref, hidden_ref, length, logits_ref, prob_ref, rows_ref):
    product = dot_dims(columns_ref[...], hidden_ref[...], 1, 1)
    logits = product * scaled
    expo = jnp.exp(logits)
    first = expo[:1]
    norm = jnp.sum(expo, axis=0, keepdims=True)
    combine = first / norm
    spread = first / jnp.sum(first, axis=1, keepdims=True)
    logits_ref[...] = logits
    prob_ref[...] = expo / norm
    rows_ref[...] = stack_rows([length, combine, spread], 8, F32)
    slot = jnp.dot(first_rows([spread]), hidden_ref[...], preferred_element_type=F32)
    return combine, slot[:1]


def mix_rows(combine, upstream):
    mixed = jnp.dot(first_rows(two_parts(combine)), upstream, preferred_element_type=F32)
    return mixed[:1] + mixed[1:2]


def norm_kernel(
    scale_ref, flags_ref, gain_ref, tokens_ref, inflow_ref,
    in_ref, hidden_ref, inverse_ref, length_ref, sums_ref, in_sem,
):
    begin_copy(flags_ref[0], tokens_ref.at[0, 0], inflow_ref.at[0, 0], in_ref, in_sem)
    end_copy(inflow_ref.at[0, 0], in_ref, in_sem)

    def square_rows(window):
        wide = in_ref[window, :].astype(F32)
        sums_ref[window, :] = lane_sums(wide * wide)

    passes(in_ref, square_rows)
    length = norm_passes(in_ref, gain_ref[...], hidden_ref, inverse_ref, sums_ref)
    length_ref[...] = stack_rows([length, length * scale_ref[0]], 8, F32)


def early_kernel(
    chunks_ref, length_ref, hidden_ref,
    send_ref, columns_ref, logits_ref, prob_ref, rows_ref, wide_ref,
):
    peers = chunks_ref.shape[0]
    chunk = hidden_ref.shape[1] // LANES
    wide_ref[...] = chunks_ref[...].astype(F32)
    local = chunks_ref.shape[1] // (2 * chunk)
    for k in range(local):
        for z in range(2):
            place = (2 * k + z) * peers
            values = wide_rows(wide_ref, (z * local + k) * chunk, chunk)
            columns_ref[place : place + peers] = values.astype(BF)
    _, slot = slot_front(
        length_ref[1:2], columns_ref, hidden_ref, length_ref[:1], logits_ref, prob_ref, rows_ref
    )
    send_ref[...] = jnp.broadcast_to(to_chunk(slot).astype(BF)[None], send_ref.shape)


def join_rows(parts, out_ref):
    count = sum(part.shape[0] for part in parts)
    filler = jnp.zeros((out_ref.shape[0] - count, LANES), F32)
    out_ref[...] = jnp.concatenate([*parts, filler], axis=0)


def pack_kernel(sums_ref, rows_ref, out_ref):
    join_rows([summed(sums_ref), to_chunk(rows_ref[1:2])], out_ref)


def late_kernel(
    scale_ref, flags_ref, base_ref, moved_ref, columns_ref, gain_ref, cotangent_ref, backflow_ref,
    send_ref, in_ref, hidden_ref, inverse_ref, logits_ref, prob_ref, rows_ref, up_ref,
    sums_ref, comb_ref, up_sem,
):
    begin_copy(flags_ref[1], cotangent_ref.at[1, 0], backflow_ref.at[0, 0], up_ref, up_sem)
    chunk = gain_ref.shape[1] // LANES
    out_row = to_row(moved_ref[:chunk])
    before = to_row(moved_ref[chunk : chunk + 2])
    comb_ref[...] = to_column(jnp.where(flags_ref[0] != 0, jnp.zeros_like(before), before))

    def add_rows(window):
        base = base_ref[window, :].astype(F32)
        value = (base + comb_ref[window, :1] * out_row).astype(BF)
        in_ref[window, :] = value
        wide = value.astype(F32)
        sums_ref[window, :] = lane_sums(wide * wide)

    passes(in_ref, add_rows)
    length = norm_passes(in_ref, gain_ref[...], hidden_ref, inverse_ref, sums_ref)
    combine, slot = slot_front(
        scale_ref[0] * length, columns_ref, hidden_ref, length, logits_ref, prob_ref, rows_ref
    )
    end_copy(backflow_ref.at[0, 0], up_ref, up_sem)
    mixed = mix_rows(combine, up_ref[...])
    both = jnp.concatenate([to_chunk(slot), to_chunk(mixed)], axis=0).astype(BF)
    send_ref[...] = jnp.broadcast_to(both[None], send_ref.shape)


def gelu_parts(value):
    rate = 0.7978845608028654
    cube = 0.044715
    bent = jnp.tanh(rate * (value + cube * value * value * value))
    half = 0.5 * (1.0 + bent)
    slope = half + 0.5 * value * (1.0 - bent * bent) * rate * (1.0 + 3.0 * cube * value * value)
    return value * half, slope


def expert_early_kernel(
    slots_ref, first_ref, second_ref, send_ref, slot_ref, act_ref, slope_ref, wide_ref
):
    wide_ref[...] = slots_ref[...].astype(F32)
    slots = wide_rows(wide_ref, 0, slots_ref.shape[1]).astype(BF)
    slot_ref[...] = slots
    value, slope = gelu_parts(jnp.dot(slots, first_ref[...], preferred_element_type=F32))
    act = value.astype(BF)
    act_ref[...] = act
    slope_ref[...] = slope
    put_rows(wide_ref, 0, jnp.dot(act, second_ref[...], preferred_element_type=F32))
    send_ref[...] = wide_ref[...].astype(BF)


def expert_late_kernel(
    pairs_ref, first_ref, second_ref, send_ref, slot_ref, mixed_ref, act_ref, grad_ref, wide_ref
):
    chunk = pairs_ref.shape[1] // 2
    wide_ref[...] = pairs_ref[...].astype(F32)
    slots = wide_rows(wide_ref, 0, chunk).astype(BF)
    mixed = wide_rows(wide_ref, chunk, chunk).astype(BF)
    slot_ref[...] = slots
    mixed_ref[...] = mixed
    value, slope = gelu_parts(jnp.dot(slots, first_ref[...], preferred_element_type=F32))
    act = value.astype(BF)
    act_ref[...] = act
    grad = (dot_dims(mixed, second_ref[...], 1, 1) * slope).astype(BF)
    grad_ref[...] = grad
    put_rows(wide_ref, 0, jnp.dot(act, second_ref[...], preferred_element_type=F32))
    put_rows(wide_ref, chunk, dot_dims(grad, first_ref[...], 1, 1))
    send_ref[...] = wide_ref[...].astype(BF)


def expert_back_kernel(
    mixed_in_ref, slope_ref, first_ref, second_ref, send_ref, mixed_ref, grad_ref, wide_ref
):
    wide_ref[...] = mixed_in_ref[...].astype(F32)
    mixed = wide_rows(wide_ref, 0, mixed_in_ref.shape[1]).astype(BF)
    mixed_ref[...] = mixed
    grad = (dot_dims(mixed, second_ref[...], 1, 1) * slope_ref[...]).astype(BF)
    grad_ref[...] = grad
    put_rows(wide_ref, 0, dot_dims(grad, first_ref[...], 1, 1))
    send_ref[...] = wide_ref[...].astype(BF)


def spread_kernel(flags_ref, moved_ref, own_ref, send_ref, kept_ref):
    block = jnp.where(flags_ref[1] != 0, own_ref[...], moved_ref[...])
    kept_ref[...] = block
    send_ref[...] = jnp.broadcast_to(block[: send_ref.shape[1]].astype(BF)[None], send_ref.shape)


def row_dots(pairs):
    def body(window):
        for ref, row, sums_ref in pairs:
            sums_ref[window, :] = lane_sums(ref[window, :].astype(F32) * row)

    passes(pairs[0][0], body)
    return [jnp.sum(jnp.transpose(sums_ref[...]), axis=0, keepdims=True) for _, _, sums_ref in pairs]


def back_body(
    scale, dcombine, dspread, grad_row, in_ref, hidden_ref, inverse_ref, logits_ref, prob_ref, rows_ref,
    columns_ref, gain_ref, hold_ref, pull_ref, mean_ref, put_grads,
):
    gain = gain_ref[...]
    length = rows_ref[0:1]
    combine = rows_ref[1:2]
    spread = rows_ref[2:3]
    grad_rows = first_rows([grad_row])
    dspread = dspread.astype(BF).astype(F32)
    first_term = spread * (dspread - jnp.sum(dspread * spread, axis=1, keepdims=True))
    mixed = combine * dcombine
    prob = prob_ref[...]
    top = lax.broadcasted_iota(jnp.int32, prob.shape, 0) == 0
    dlogits = jnp.where(top, mixed + first_term, 0.0) - prob * mixed
    dproduct = dlogits * scale * length
    pull = jnp.sum(dlogits * logits_ref[...], axis=0, keepdims=True) * length * length
    pull_ref[...] = to_column(pull)
    dproduct_bf = dproduct.astype(BF)
    hold_ref[...] = dot_dims(dproduct_bf, columns_ref[...], 0, 0) + dot_dims(
        first_rows([spread]), grad_rows, 0, 0
    )
    router = jnp.dot(dproduct_bf, hidden_ref[...], preferred_element_type=F32)

    def product_rows(index, total):
        window = pl.ds(index * STEP, STEP)
        dhidden = hold_ref[window, :] - hidden_ref[window, :].astype(F32) * pull_ref[window, :1]
        hold_ref[window, :] = dhidden
        product = dhidden * (in_ref[window, :].astype(F32) * inverse_ref[window, :1])
        mean_ref[window, :] = lane_sums(product * gain)
        return total + product[:8] + product[8:]

    gain_sum = lax.fori_loop(
        0, in_ref.shape[0] // STEP, product_rows, jnp.zeros((8, in_ref.shape[1]), F32), unroll=4
    )
    mean = jnp.sum(mean_ref[...], axis=1, keepdims=True) * (1.0 / in_ref.shape[1])
    mean_ref[...] = jnp.broadcast_to(mean * inverse_ref[...], mean_ref.shape)

    def grad_rows_pass(window):
        inverse = inverse_ref[window, :1]
        through = hold_ref[window, :] * gain
        wide = in_ref[window, :].astype(F32)
        dinput = inverse * (through - wide * mean_ref[window, :1])
        put_grads(window, dinput)

    passes(in_ref, grad_rows_pass)
    return router, gain_sum


def back_late_kernel(
    scale_ref, flags_ref, sums_ref, in_ref, hidden_ref, inverse_ref, logits_ref, prob_ref,
    rows_ref, up_ref, columns_ref, gain_ref, moved_ref, rows_own_ref, packed_ref, cotangent_ref,
    grads_ref, moved_out, own_out, outs_ref, router_ref, gain_out,
    own_ref, hold_ref, pull_ref, mean_ref, own_sem,
):
    last = flags_ref[1] != 0

    @pl.when(last)
    def _():
        pltpu.make_async_copy(cotangent_ref.at[0, 0], own_ref, own_sem).start()

    chunk = sums_ref.shape[1] // 2
    total = summed(sums_ref)
    outs_ref[...] = total

    def put_grads(window, dinput):
        grads_ref[window, :] = (up_ref[window, :].astype(F32) + dinput).astype(BF)

    grad_row = to_row(total[chunk:])
    dcombine, dspread = row_dots(
        [(up_ref, to_row(total[:chunk]), pull_ref), (hidden_ref, grad_row, mean_ref)]
    )
    router, gain_sum = back_body(
        scale_ref[0], dcombine, dspread, grad_row, in_ref, hidden_ref, inverse_ref, logits_ref,
        prob_ref, rows_ref, columns_ref, gain_ref, hold_ref, pull_ref, mean_ref, put_grads,
    )

    def message(combine, out_row, ref, out):
        mixed = to_chunk(mix_rows(combine, ref[...]).astype(BF).astype(F32))
        join_rows([mixed, to_chunk(row_dots([(ref, out_row, mean_ref)])[0])], out)

    combine = to_row(moved_ref[chunk : chunk + 2])
    message(combine, to_row(moved_ref[:chunk]), grads_ref, moved_out)
    router_ref[...] = router
    gain_out[...] = gain_sum
    own_out[...] = jnp.zeros_like(own_out)

    @pl.when(last)
    def _():
        end_copy(cotangent_ref.at[0, 0], own_ref, own_sem)
        message(rows_own_ref[1:2], to_row(packed_ref[:chunk]), own_ref, own_out)


def back_early_kernel(
    scale_ref, sums_ref, kept_ref, in_ref, hidden_ref, inverse_ref, logits_ref, prob_ref,
    rows_ref, columns_ref, gain_ref, router_in_ref, gain_in_ref,
    dinput_ref, outs_ref, send_ref, hold_ref, pull_ref, mean_ref, wide_ref,
):
    chunk = sums_ref.shape[1]
    total = summed(sums_ref)
    outs_ref[...] = total

    def put_grads(window, dinput):
        dinput_ref[window, :] = dinput.astype(BF)

    grad_row = to_row(total)
    (dspread,) = row_dots([(hidden_ref, grad_row, mean_ref)])
    router, gain_sum = back_body(
        scale_ref[0], to_row(kept_ref[chunk : chunk + 2]), dspread, grad_row, in_ref, hidden_ref,
        inverse_ref, logits_ref, prob_ref, rows_ref, columns_ref, gain_ref, hold_ref, pull_ref,
        mean_ref, put_grads,
    )
    router = router + router_in_ref[...]
    peers = send_ref.shape[0]
    count = router.shape[0] // peers
    for k in range(count):
        put_rows(wide_ref, k * chunk, router[k * peers : (k + 1) * peers])
    send_ref[:, : count * chunk, :] = wide_ref[...].astype(BF)
    gain_row = jnp.sum(gain_sum + gain_in_ref[...], axis=0, keepdims=True)
    send_ref[:, count * chunk :, :] = jnp.broadcast_to(
        to_chunk(gain_row).astype(BF)[None], (peers, chunk, LANES)
    )


def final_kernel(
    chunks_ref, weights_ref, packed_ref, outs_late_ref, outs_early_ref,
    router_ref, gain_ref, slot_out_ref, slot_grad_ref,
):
    weights, inverse = scaled_weights(weights_ref)
    total = jnp.sum(chunks_ref[...].astype(F32), axis=0)
    count = weights.shape[0]
    chunk = weights.shape[1] // LANES
    rows = [to_row(total[k * chunk : (k + 1) * chunk]) for k in range(count)]
    pulled = jnp.concatenate(rows, axis=0)
    dots = jnp.sum(pulled * weights, axis=1, keepdims=True)
    router_ref[...] = (inverse * (pulled - weights * (dots * inverse * inverse))).astype(BF)
    gain_ref[...] = to_row(total[count * chunk :])
    late = outs_late_ref[...]
    outs = [to_row(packed_ref[:chunk]), to_row(late[:chunk])]
    grads = [to_row(outs_early_ref[...]), to_row(late[chunk:])]
    slot_out_ref[...] = jnp.concatenate(outs, axis=0).astype(BF)
    slot_grad_ref[...] = jnp.concatenate(grads, axis=0).astype(BF)


def shards(
    tokens,
    cotangent,
    inflow,
    backflow,
    norm_gain,
    slot_scale,
    router_weight,
    expert_in,
    expert_back,
):
    section_index = lax.axis_index("section")
    is_first = section_index == 0
    is_last = section_index == lax.axis_size("section") - 1
    flags = jnp.stack([is_first, is_last, lax.axis_index("zh") == 1]).astype(jnp.int32)
    group = lax.axis_size(DP)
    patches = tokens.shape[2]
    width = tokens.shape[3]
    chunk = width // LANES
    local = router_weight.shape[2]
    slots = local * group
    hidden_units = expert_in.shape[2]
    first_weight = expert_in[0]
    second_weight = expert_back[0]
    weights = router_weight[0].T
    token_block = ((patches, width), BF)
    column = ((patches, LANES), F32)
    table = ((slots, patches), F32)
    rows = ((8, patches), F32)
    single = ((group, chunk, LANES), BF)
    double = ((group, 2 * chunk, LANES), BF)
    every_slot = ((group, width), BF)
    every_hidden = ((group, hidden_units), BF)
    copy_sem = pltpu.SemaphoreType.DMA

    plane = group // 2
    block = run(columns_kernel, [((local * chunk, LANES), BF)], [], 1000000, 1, weights)[0]
    start_in, hidden_early, inverse_early, length_early = run(
        norm_kernel,
        [token_block, token_block, column, rows],
        [column, copy_sem],
        30000000,
        3,
        slot_scale,
        flags,
        norm_gain,
        tokens,
        inflow,
        vmem=VMEM_NORM,
    )
    other, length_early = lax.optimization_barrier((other_half(block), length_early))
    send = run(
        order_kernel,
        [((plane, 2 * local * chunk, LANES), BF)],
        [],
        1000000,
        3,
        flags,
        block,
        other,
    )[0]
    sent_in = section_ring(start_in, 1)
    send, columns, logits_early, prob_early, rows_early = run(
        early_kernel,
        [single, ((slots, width), BF), table, table, rows],
        [((plane, 2 * local * chunk, LANES), F32)],
        300000000,
        3,
        exchange(send, PLANE),
        length_early,
        hidden_early,
    )
    part, slot_early, act_early, slope_early = run(
        expert_early_kernel,
        [single, every_slot, every_hidden, ((group, hidden_units), F32)],
        [((group, chunk, LANES), F32)],
        70000000,
        3,
        exchange(send, DP),
        first_weight,
        second_weight,
    )
    packed = run(
        pack_kernel, [((chunk + 8, LANES), F32)], [], 1000000, 2, exchange(part, DP), rows_early
    )[0]
    moved = section_ring(packed, 1)

    base = jnp.where(is_first, tokens[1, 0], sent_in)
    (
        send, late_in, hidden_late, inverse_late, logits_late, prob_late, rows_late, late_up,
    ) = run(
        late_kernel,
        [double, token_block, token_block, column, table, table, rows, token_block],
        [column, column, copy_sem],
        400000000,
        6,
        slot_scale,
        flags,
        base,
        moved,
        columns,
        norm_gain,
        cotangent,
        backflow,
    )
    parts, slot_late, mixed_late, act_late, pre_grad_late = run(
        expert_late_kernel,
        [double, every_slot, every_slot, every_hidden, every_hidden],
        [((group, 2 * chunk, LANES), F32)],
        140000000,
        3,
        exchange(send, DP),
        first_weight,
        second_weight,
    )
    back_scratch = [((patches, width), F32), column, column]
    message = ((chunk + 8, LANES), F32)
    grads_late, moved_back, own_back, outs_late, router_late, gain_late = run(
        back_late_kernel,
        [
            token_block, message, message, ((2 * chunk, LANES), F32), ((slots, width), F32),
            ((8, width), F32),
        ],
        [token_block] + back_scratch + [copy_sem],
        600000000,
        15,
        slot_scale,
        flags,
        exchange(parts, DP),
        late_in,
        hidden_late,
        inverse_late,
        logits_late,
        prob_late,
        rows_late,
        late_up,
        columns,
        norm_gain,
        moved,
        rows_early,
        packed,
        cotangent,
    )
    send, kept = run(
        spread_kernel, [single, message], [], 1000000, 3, flags, section_ring(moved_back, -1), own_back
    )
    part, mixed_early_all, pre_grad_early = run(
        expert_back_kernel,
        [single, every_slot, every_hidden],
        [((group, chunk, LANES), F32)],
        70000000,
        4,
        exchange(send, DP),
        slope_early,
        first_weight,
        second_weight,
    )
    last_rows = (local + 1) * chunk
    slot_sums, held_grads = lax.optimization_barrier((exchange(part, DP), grads_late))
    sent_grads = section_ring(held_grads, -1)
    dinput, outs_early, finals = run(
        back_early_kernel,
        [token_block, ((chunk, LANES), F32), ((group, last_rows, LANES), BF)],
        back_scratch + [((group, local * chunk, LANES), F32)],
        600000000,
        13,
        slot_scale,
        slot_sums,
        kept,
        start_in,
        hidden_early,
        inverse_early,
        logits_early,
        prob_early,
        rows_early,
        columns,
        norm_gain,
        router_late,
        gain_late,
    )
    router_grad, gain_total, slot_out, slot_grad = run(
        final_kernel,
        [((local, width), BF), ((1, width), F32), ((2, width), BF), ((2, width), BF)],
        [],
        1000000,
        5,
        exchange(finals, DP),
        weights,
        packed,
        outs_late,
        outs_early,
    )

    (
        dinput, slot_early, slot_late, pre_grad_early, pre_grad_late, act_early, act_late,
        mixed_early_all, mixed_late, grads_late,
    ) = lax.optimization_barrier(
        (
            dinput, slot_early, slot_late, pre_grad_early, pre_grad_late, act_early, act_late,
            mixed_early_all, mixed_late, grads_late,
        )
    )
    early_up = jnp.where(is_last, cotangent[0, 0], sent_grads).astype(F32)
    grads_early = (early_up + dinput.astype(F32)).astype(BF)
    first_grad = dot_dims(
        jnp.concatenate([slot_early, slot_late], axis=0),
        jnp.concatenate([pre_grad_early, pre_grad_late], axis=0),
        0,
        0,
    )
    second_grad = dot_dims(
        jnp.concatenate([act_early, act_late], axis=0),
        jnp.concatenate([mixed_early_all, mixed_late], axis=0),
        0,
        0,
    )
    return (
        jnp.stack([grads_early, grads_late])[None, :, None],
        slot_out[None, :, None],
        slot_grad[None, :, None],
        first_grad.astype(BF)[None],
        second_grad.astype(BF)[None],
        router_grad.T[None],
        gain_total,
    )


def solution(mesh):
    fine = Mesh(mesh.devices.reshape(mesh.shape["section"], 2, 4, 4), AXES)
    in_specs = (
        P(None, DP, None, None),
        P(None, DP, None, None),
        P("section", DP, None, None),
        P("section", DP, None, None),
        P("section", None),
        P("section"),
        P("section", None, DP),
        P("section", None, DP),
        P("section", DP, None),
    )
    out_specs = (
        P("section", None, DP, None, None),
        P("section", None, DP, None),
        P("section", None, DP, None),
        P("section", None, DP),
        P("section", DP, None),
        P("section", None, DP),
        P("section", None),
    )
    return jax.shard_map(shards, mesh=fine, in_specs=in_specs, out_specs=out_specs, check_vma=False)
```

```python
import jax
import jax.numpy as jnp
from jax import lax
from jax.experimental import pallas as pl
from jax.experimental.pallas import tpu as pltpu
from jax.sharding import Mesh
from jax.sharding import PartitionSpec as P

EPSILON = 1e-06
BF = jnp.bfloat16
F32 = jnp.float32
AXES = ("section", "zh", "y", "x")
DP = ("zh", "y", "x")
PLANE = ("y", "x")
LANES = 128
STEP = 16
VMEM_BYTES = 24 * 1024 * 1024


def dot_dims(left_side, right_side, left_dim, right_dim):
    return lax.dot_general(
        left_side,
        right_side,
        (((left_dim,), (right_dim,)), ((), ())),
        preferred_element_type=F32,
    )


def exchange(chunks, axes):
    return lax.all_to_all(chunks, axes, 0, 0, tiled=True)


def section_shift(block, distance):
    sections = lax.axis_size("section")
    route = [(i, i + distance) for i in range(sections) if 0 <= i + distance < sections]
    return lax.ppermute(block, "section", route)


def other_half(block):
    return lax.ppermute(block, "zh", [(0, 1), (1, 0)])


def section_ring(block, distance):
    sections = lax.axis_size("section")
    return lax.ppermute(block, "section", [(i, (i + distance) % sections) for i in range(sections)])


def run(body, outs, scratch, flops, near, *operands, vmem=VMEM_BYTES):
    def place(index, item):
        if item.ndim == 1:
            return pltpu.SMEM
        return pltpu.VMEM if index < near else pl.ANY

    return pl.pallas_call(
        body,
        out_shape=[jax.ShapeDtypeStruct(item[0], item[1]) for item in outs],
        in_specs=[
            pl.BlockSpec(memory_space=place(index, item)) for index, item in enumerate(operands)
        ],
        out_specs=[
            pl.BlockSpec(memory_space=pltpu.VMEM if len(item) == 2 else pl.ANY) for item in outs
        ],
        scratch_shapes=[
            pltpu.VMEM(*item) if isinstance(item, tuple) else item for item in scratch
        ],
        compiler_params=pltpu.CompilerParams(vmem_limit_bytes=vmem),
        cost_estimate=pl.CostEstimate(flops=flops, bytes_accessed=4000000, transcendentals=0),
    )(*operands)


def to_chunk(row):
    count = row.shape[1] // LANES
    return jnp.concatenate([row[:, k * LANES : (k + 1) * LANES] for k in range(count)], axis=0)


def to_row(chunk):
    return jnp.concatenate([chunk[k : k + 1, :] for k in range(chunk.shape[0])], axis=1)


def to_column(row):
    return jnp.transpose(jnp.broadcast_to(row, (LANES, row.shape[1])))


def stack_rows(rows, count, kind):
    filler = jnp.zeros((count - len(rows), rows[0].shape[1]), F32)
    return jnp.concatenate(list(rows) + [filler], axis=0).astype(kind)


def first_rows(rows):
    return stack_rows(rows, STEP, BF)


def wide_rows(ref, offset, count):
    return jnp.concatenate([ref[:, offset + k, :] for k in range(count)], axis=1)


def put_rows(ref, offset, value):
    for k in range(value.shape[1] // LANES):
        ref[:, offset + k, :] = value[:, k * LANES : (k + 1) * LANES]


def two_parts(row):
    high = row.astype(BF).astype(F32)
    return high, row - high


def lane_sums(value):
    parts = [value[:, k * LANES : (k + 1) * LANES] for k in range(value.shape[1] // LANES)]
    while len(parts) > 1:
        parts = [x + y for x, y in zip(parts[::2], parts[1::2])]
    return parts[0]


def summed(chunks_ref):
    return jnp.sum(chunks_ref[...].astype(F32), axis=0).astype(BF).astype(F32)


def passes(ref, body):
    @pl.loop(0, ref.shape[0] // STEP, unroll=8)
    def _(index):
        body(pl.ds(index * STEP, STEP))


def begin_copy(flag, yes, no, target, sem):
    @pl.when(flag != 0)
    def _():
        pltpu.make_async_copy(yes, target, sem).start()

    @pl.when(flag == 0)
    def _():
        pltpu.make_async_copy(no, target, sem).start()


def end_copy(source, target, sem):
    pltpu.make_async_copy(source, target, sem).wait()


def scaled_weights(weights_ref):
    weights = weights_ref[...].astype(F32)
    total = jnp.sum(weights * weights, axis=1, keepdims=True)
    return weights, lax.rsqrt(total + EPSILON)


def columns_kernel(weights_ref, send_ref):
    weights, inverse = scaled_weights(weights_ref)
    columns = weights * inverse
    rows = [to_chunk(columns[k : k + 1]) for k in range(columns.shape[0])]
    send_ref[...] = jnp.concatenate(rows, axis=0).astype(BF)


def order_kernel(flags_ref, own_ref, other_ref, send_ref):
    own = own_ref[...].astype(F32)
    other = other_ref[...].astype(F32)
    upper = flags_ref[2] != 0
    pair = [jnp.where(upper, other, own), jnp.where(upper, own, other)]
    block = jnp.concatenate(pair, axis=0).astype(BF)
    send_ref[...] = jnp.broadcast_to(block[None], send_ref.shape)


def norm_passes(in_ref, gain, hidden_ref, inverse_ref, sums_ref):
    rate = 1.0 / in_ref.shape[1]
    inverse = lax.rsqrt(jnp.sum(sums_ref[...], axis=1, keepdims=True) * rate + EPSILON)
    inverse_ref[...] = jnp.broadcast_to(inverse, inverse_ref.shape)

    def scale_rows(window):
        wide = in_ref[window, :].astype(F32)
        hidden = (wide * inverse_ref[window, :1] * gain).astype(BF)
        hidden_ref[window, :] = hidden
        hidden_f = hidden.astype(F32)
        sums_ref[window, :] = lane_sums(hidden_f * hidden_f)

    passes(in_ref, scale_rows)
    total = jnp.sum(jnp.transpose(sums_ref[...]), axis=0, keepdims=True)
    return lax.rsqrt(total + EPSILON)


def slot_front(scaled, columns_ref, hidden_ref, length, logits_ref, prob_ref, rows_ref):
    product = dot_dims(columns_ref[...], hidden_ref[...], 1, 1)
    logits = product * scaled
    expo = jnp.exp(logits)
    first = expo[:1]
    norm = jnp.sum(expo, axis=0, keepdims=True)
    combine = first / norm
    spread = first / jnp.sum(first, axis=1, keepdims=True)
    logits_ref[...] = logits
    prob_ref[...] = expo / norm
    rows_ref[...] = stack_rows([length, combine, spread], 8, F32)
    slot = jnp.dot(first_rows([spread]), hidden_ref[...], preferred_element_type=F32)
    return combine, slot[:1]


def mix_rows(combine, upstream):
    mixed = jnp.dot(first_rows(two_parts(combine)), upstream, preferred_element_type=F32)
    return mixed[:1] + mixed[1:2]


def norm_kernel(
    scale_ref, gain_ref, in_ref, hidden_ref, inverse_ref, length_ref, sums_ref
):
    def square_rows(window):
        wide = in_ref[window, :].astype(F32)
        sums_ref[window, :] = lane_sums(wide * wide)

    passes(in_ref, square_rows)
    length = norm_passes(in_ref, gain_ref[...], hidden_ref, inverse_ref, sums_ref)
    length_ref[...] = stack_rows([length, length * scale_ref[0]], 8, F32)


def early_kernel(
    chunks_ref, length_ref, hidden_ref,
    send_ref, columns_ref, logits_ref, prob_ref, rows_ref, wide_ref,
):
    peers = chunks_ref.shape[0]
    chunk = hidden_ref.shape[1] // LANES
    wide_ref[...] = chunks_ref[...].astype(F32)
    local = chunks_ref.shape[1] // (2 * chunk)
    for k in range(local):
        for z in range(2):
            place = (2 * k + z) * peers
            values = wide_rows(wide_ref, (z * local + k) * chunk, chunk)
            columns_ref[place : place + peers] = values.astype(BF)
    _, slot = slot_front(
        length_ref[1:2], columns_ref, hidden_ref, length_ref[:1], logits_ref, prob_ref, rows_ref
    )
    send_ref[...] = jnp.broadcast_to(to_chunk(slot).astype(BF)[None], send_ref.shape)


def join_rows(parts, out_ref):
    count = sum(part.shape[0] for part in parts)
    filler = jnp.zeros((out_ref.shape[0] - count, LANES), F32)
    out_ref[...] = jnp.concatenate([*parts, filler], axis=0)


def pack_kernel(sums_ref, rows_ref, out_ref):
    join_rows([summed(sums_ref), to_chunk(rows_ref[1:2])], out_ref)


def late_kernel(
    scale_ref, flags_ref, base_ref, moved_ref, columns_ref, gain_ref, cotangent_ref, backflow_ref,
    send_ref, in_ref, hidden_ref, inverse_ref, logits_ref, prob_ref, rows_ref, up_ref,
    sums_ref, comb_ref, up_sem,
):
    begin_copy(flags_ref[1], cotangent_ref.at[1, 0], backflow_ref.at[0, 0], up_ref, up_sem)
    chunk = gain_ref.shape[1] // LANES
    out_row = to_row(moved_ref[:chunk])
    before = to_row(moved_ref[chunk : chunk + 2])
    comb_ref[...] = to_column(jnp.where(flags_ref[0] != 0, jnp.zeros_like(before), before))

    def add_rows(window):
        base = base_ref[window, :].astype(F32)
        value = (base + comb_ref[window, :1] * out_row).astype(BF)
        in_ref[window, :] = value
        wide = value.astype(F32)
        sums_ref[window, :] = lane_sums(wide * wide)

    passes(in_ref, add_rows)
    length = norm_passes(in_ref, gain_ref[...], hidden_ref, inverse_ref, sums_ref)
    combine, slot = slot_front(
        scale_ref[0] * length, columns_ref, hidden_ref, length, logits_ref, prob_ref, rows_ref
    )
    end_copy(backflow_ref.at[0, 0], up_ref, up_sem)
    mixed = mix_rows(combine, up_ref[...])
    both = jnp.concatenate([to_chunk(slot), to_chunk(mixed)], axis=0).astype(BF)
    send_ref[...] = jnp.broadcast_to(both[None], send_ref.shape)


def gelu_parts(value):
    rate = 0.7978845608028654
    cube = 0.044715
    bent = jnp.tanh(rate * (value + cube * value * value * value))
    half = 0.5 * (1.0 + bent)
    slope = half + 0.5 * value * (1.0 - bent * bent) * rate * (1.0 + 3.0 * cube * value * value)
    return value * half, slope


def expert_early_kernel(
    slots_ref, first_ref, second_ref, send_ref, slot_ref, act_ref, slope_ref, wide_ref
):
    wide_ref[...] = slots_ref[...].astype(F32)
    slots = wide_rows(wide_ref, 0, slots_ref.shape[1]).astype(BF)
    slot_ref[...] = slots
    value, slope = gelu_parts(jnp.dot(slots, first_ref[...], preferred_element_type=F32))
    act = value.astype(BF)
    act_ref[...] = act
    slope_ref[...] = slope
    put_rows(wide_ref, 0, jnp.dot(act, second_ref[...], preferred_element_type=F32))
    send_ref[...] = wide_ref[...].astype(BF)


def expert_late_kernel(
    pairs_ref, first_ref, second_ref, send_ref, slot_ref, mixed_ref, act_ref, grad_ref, wide_ref
):
    chunk = pairs_ref.shape[1] // 2
    wide_ref[...] = pairs_ref[...].astype(F32)
    slots = wide_rows(wide_ref, 0, chunk).astype(BF)
    mixed = wide_rows(wide_ref, chunk, chunk).astype(BF)
    slot_ref[...] = slots
    mixed_ref[...] = mixed
    value, slope = gelu_parts(jnp.dot(slots, first_ref[...], preferred_element_type=F32))
    act = value.astype(BF)
    act_ref[...] = act
    grad = (dot_dims(mixed, second_ref[...], 1, 1) * slope).astype(BF)
    grad_ref[...] = grad
    put_rows(wide_ref, 0, jnp.dot(act, second_ref[...], preferred_element_type=F32))
    put_rows(wide_ref, chunk, dot_dims(grad, first_ref[...], 1, 1))
    send_ref[...] = wide_ref[...].astype(BF)


def expert_back_kernel(
    mixed_in_ref, slope_ref, first_ref, second_ref, send_ref, mixed_ref, grad_ref, wide_ref
):
    wide_ref[...] = mixed_in_ref[...].astype(F32)
    mixed = wide_rows(wide_ref, 0, mixed_in_ref.shape[1]).astype(BF)
    mixed_ref[...] = mixed
    grad = (dot_dims(mixed, second_ref[...], 1, 1) * slope_ref[...]).astype(BF)
    grad_ref[...] = grad
    put_rows(wide_ref, 0, dot_dims(grad, first_ref[...], 1, 1))
    send_ref[...] = wide_ref[...].astype(BF)


def spread_kernel(flags_ref, moved_ref, own_ref, send_ref, kept_ref):
    block = jnp.where(flags_ref[1] != 0, own_ref[...], moved_ref[...])
    kept_ref[...] = block
    send_ref[...] = jnp.broadcast_to(block[: send_ref.shape[1]].astype(BF)[None], send_ref.shape)


def row_dots(pairs):
    def body(window):
        for ref, row, sums_ref in pairs:
            sums_ref[window, :] = lane_sums(ref[window, :].astype(F32) * row)

    passes(pairs[0][0], body)
    return [jnp.sum(jnp.transpose(sums_ref[...]), axis=0, keepdims=True) for _, _, sums_ref in pairs]


def back_body(
    scale, dcombine, dspread, grad_row, in_ref, hidden_ref, inverse_ref, logits_ref, prob_ref, rows_ref,
    columns_ref, gain_ref, hold_ref, pull_ref, mean_ref, put_grads,
):
    gain = gain_ref[...]
    length = rows_ref[0:1]
    combine = rows_ref[1:2]
    spread = rows_ref[2:3]
    grad_rows = first_rows([grad_row])
    dspread = dspread.astype(BF).astype(F32)
    first_term = spread * (dspread - jnp.sum(dspread * spread, axis=1, keepdims=True))
    mixed = combine * dcombine
    prob = prob_ref[...]
    top = lax.broadcasted_iota(jnp.int32, prob.shape, 0) == 0
    dlogits = jnp.where(top, mixed + first_term, 0.0) - prob * mixed
    dproduct = dlogits * scale * length
    pull = jnp.sum(dlogits * logits_ref[...], axis=0, keepdims=True) * length * length
    pull_ref[...] = to_column(pull)
    dproduct_bf = dproduct.astype(BF)
    hold_ref[...] = dot_dims(
        jnp.concatenate([dproduct_bf, first_rows([spread])], axis=0),
        jnp.concatenate([columns_ref[...], grad_rows], axis=0),
        0,
        0,
    )
    router = jnp.dot(dproduct_bf, hidden_ref[...], preferred_element_type=F32)

    def product_rows(index, total):
        window = pl.ds(index * STEP, STEP)
        dhidden = hold_ref[window, :] - hidden_ref[window, :].astype(F32) * pull_ref[window, :1]
        hold_ref[window, :] = dhidden
        product = dhidden * (in_ref[window, :].astype(F32) * inverse_ref[window, :1])
        mean_ref[window, :] = lane_sums(product * gain)
        return total + product[:8] + product[8:]

    gain_sum = lax.fori_loop(
        0, in_ref.shape[0] // STEP, product_rows, jnp.zeros((8, in_ref.shape[1]), F32), unroll=4
    )
    mean = jnp.sum(mean_ref[...], axis=1, keepdims=True) * (1.0 / in_ref.shape[1])
    mean_ref[...] = jnp.broadcast_to(mean * inverse_ref[...], mean_ref.shape)

    def grad_rows_pass(window):
        inverse = inverse_ref[window, :1]
        through = hold_ref[window, :] * gain
        wide = in_ref[window, :].astype(F32)
        dinput = inverse * (through - wide * mean_ref[window, :1])
        put_grads(window, dinput)

    passes(in_ref, grad_rows_pass)
    return router, gain_sum


def back_late_kernel(
    scale_ref, flags_ref, sums_ref, in_ref, hidden_ref, inverse_ref, logits_ref, prob_ref,
    rows_ref, up_ref, columns_ref, gain_ref, moved_ref, rows_own_ref, packed_ref, cotangent_ref,
    grads_out, moved_out, own_out, outs_ref, router_ref, gain_out,
    own_ref, grads_ref, hold_ref, pull_ref, mean_ref, own_sem, grads_sem,
):
    last = flags_ref[1] != 0

    @pl.when(last)
    def _():
        pltpu.make_async_copy(cotangent_ref.at[0, 0], own_ref, own_sem).start()

    chunk = sums_ref.shape[1] // 2
    total = summed(sums_ref)
    outs_ref[...] = total

    def put_grads(window, dinput):
        grads_ref[window, :] = (up_ref[window, :].astype(F32) + dinput).astype(BF)

    grad_row = to_row(total[chunk:])
    dcombine, dspread = row_dots(
        [(up_ref, to_row(total[:chunk]), pull_ref), (hidden_ref, grad_row, mean_ref)]
    )
    router, gain_sum = back_body(
        scale_ref[0], dcombine, dspread, grad_row, in_ref, hidden_ref, inverse_ref, logits_ref,
        prob_ref, rows_ref, columns_ref, gain_ref, hold_ref, pull_ref, mean_ref, put_grads,
    )

    leave = pltpu.make_async_copy(grads_ref, grads_out, grads_sem)
    leave.start()

    def message(combine, out_row, ref, out):
        mixed = to_chunk(mix_rows(combine, ref[...]).astype(BF).astype(F32))
        join_rows([mixed, to_chunk(row_dots([(ref, out_row, mean_ref)])[0])], out)

    combine = to_row(moved_ref[chunk : chunk + 2])
    message(combine, to_row(moved_ref[:chunk]), grads_ref, moved_out)
    router_ref[...] = router
    gain_out[...] = gain_sum
    own_out[...] = jnp.zeros_like(own_out)

    @pl.when(last)
    def _():
        end_copy(cotangent_ref.at[0, 0], own_ref, own_sem)
        message(rows_own_ref[1:2], to_row(packed_ref[:chunk]), own_ref, own_out)

    leave.wait()


def back_early_kernel(
    scale_ref, sums_ref, kept_ref, in_ref, hidden_ref, inverse_ref, logits_ref, prob_ref,
    rows_ref, columns_ref, gain_ref, router_in_ref, gain_in_ref,
    dinput_ref, outs_ref, send_ref, hold_ref, pull_ref, mean_ref, wide_ref,
):
    chunk = sums_ref.shape[1]
    total = summed(sums_ref)
    outs_ref[...] = total

    def put_grads(window, dinput):
        dinput_ref[window, :] = dinput.astype(BF)

    grad_row = to_row(total)
    (dspread,) = row_dots([(hidden_ref, grad_row, mean_ref)])
    router, gain_sum = back_body(
        scale_ref[0], to_row(kept_ref[chunk : chunk + 2]), dspread, grad_row, in_ref, hidden_ref,
        inverse_ref, logits_ref, prob_ref, rows_ref, columns_ref, gain_ref, hold_ref, pull_ref,
        mean_ref, put_grads,
    )
    router = router + router_in_ref[...]
    peers = send_ref.shape[0]
    count = router.shape[0] // peers
    for k in range(count):
        place = (k % 2) * (count // 2) + k // 2
        put_rows(wide_ref, place * chunk, router[k * peers : (k + 1) * peers])
    send_ref[:, : count * chunk, :] = wide_ref[...].astype(BF)
    gain_row = jnp.sum(gain_sum + gain_in_ref[...], axis=0, keepdims=True)
    send_ref[:, count * chunk :, :] = jnp.broadcast_to(
        to_chunk(gain_row).astype(BF)[None], (peers, chunk, LANES)
    )


def plane_kernel(flags_ref, chunks_ref, kept_ref, given_ref):
    total = jnp.sum(chunks_ref[...].astype(F32), axis=0)
    count = chunks_ref.shape[1] - kept_ref.shape[0]
    low, high, gain = total[:count], total[count : 2 * count], total[2 * count :]
    upper = flags_ref[2] != 0
    kept_ref[...] = jnp.concatenate([jnp.where(upper, high, low), gain], axis=0)
    given_ref[...] = jnp.concatenate([jnp.where(upper, low, high), gain], axis=0)


def final_kernel(
    kept_ref, taken_ref, weights_ref, packed_ref, outs_late_ref, outs_early_ref,
    router_ref, gain_ref, slot_out_ref, slot_grad_ref,
):
    weights, inverse = scaled_weights(weights_ref)
    total = kept_ref[...] + taken_ref[...]
    count = weights.shape[0]
    chunk = weights.shape[1] // LANES
    rows = [to_row(total[k * chunk : (k + 1) * chunk]) for k in range(count)]
    pulled = jnp.concatenate(rows, axis=0)
    dots = jnp.sum(pulled * weights, axis=1, keepdims=True)
    router_ref[...] = (inverse * (pulled - weights * (dots * inverse * inverse))).astype(BF)
    gain_ref[...] = to_row(total[count * chunk :])
    late = outs_late_ref[...]
    outs = [to_row(packed_ref[:chunk]), to_row(late[:chunk])]
    grads = [to_row(outs_early_ref[...]), to_row(late[chunk:])]
    slot_out_ref[...] = jnp.concatenate(outs, axis=0).astype(BF)
    slot_grad_ref[...] = jnp.concatenate(grads, axis=0).astype(BF)


def shards(
    tokens,
    cotangent,
    inflow,
    backflow,
    norm_gain,
    slot_scale,
    router_weight,
    expert_in,
    expert_back,
):
    section_index = lax.axis_index("section")
    is_first = section_index == 0
    is_last = section_index == lax.axis_size("section") - 1
    flags = jnp.stack([is_first, is_last, lax.axis_index("zh") == 1]).astype(jnp.int32)
    group = lax.axis_size(DP)
    patches = tokens.shape[2]
    width = tokens.shape[3]
    chunk = width // LANES
    local = router_weight.shape[2]
    slots = local * group
    hidden_units = expert_in.shape[2]
    first_weight = expert_in[0]
    second_weight = expert_back[0]
    weights = router_weight[0].T
    token_block = ((patches, width), BF)
    column = ((patches, LANES), F32)
    table = ((slots, patches), F32)
    rows = ((8, patches), F32)
    single = ((group, chunk, LANES), BF)
    double = ((group, 2 * chunk, LANES), BF)
    every_slot = ((group, width), BF)
    every_hidden = ((group, hidden_units), BF)
    copy_sem = pltpu.SemaphoreType.DMA

    plane = group // 2
    block = run(columns_kernel, [((local * chunk, LANES), BF)], [], 1000000, 1, weights)[0]
    start_in = jnp.where(is_first, tokens[0, 0], inflow[0, 0])
    hidden_early, inverse_early, length_early = run(
        norm_kernel,
        [token_block, column, rows],
        [column],
        30000000,
        3,
        slot_scale,
        norm_gain,
        start_in,
    )
    other, length_early = lax.optimization_barrier((other_half(block), length_early))
    send = run(
        order_kernel,
        [((plane, 2 * local * chunk, LANES), BF)],
        [],
        1000000,
        3,
        flags,
        block,
        other,
    )[0]
    sent_in = section_ring(start_in, 1)
    send, columns, logits_early, prob_early, rows_early = run(
        early_kernel,
        [single, ((slots, width), BF), table, table, rows],
        [((plane, 2 * local * chunk, LANES), F32)],
        300000000,
        3,
        exchange(send, PLANE),
        length_early,
        hidden_early,
    )
    part, slot_early, act_early, slope_early = run(
        expert_early_kernel,
        [single, every_slot, every_hidden, ((group, hidden_units), F32)],
        [((group, chunk, LANES), F32)],
        70000000,
        3,
        exchange(send, DP),
        first_weight,
        second_weight,
    )
    packed = run(
        pack_kernel, [((chunk + 8, LANES), F32)], [], 1000000, 2, exchange(part, DP), rows_early
    )[0]
    moved = section_ring(packed, 1)

    base = jnp.where(is_first, tokens[1, 0], sent_in)
    (
        send, late_in, hidden_late, inverse_late, logits_late, prob_late, rows_late, late_up,
    ) = run(
        late_kernel,
        [double, token_block, token_block, column, table, table, rows, token_block],
        [column, column, copy_sem],
        400000000,
        6,
        slot_scale,
        flags,
        base,
        moved,
        columns,
        norm_gain,
        cotangent,
        backflow,
    )
    parts, slot_late, mixed_late, act_late, pre_grad_late = run(
        expert_late_kernel,
        [double, every_slot, every_slot, every_hidden, every_hidden],
        [((group, 2 * chunk, LANES), F32)],
        140000000,
        3,
        exchange(send, DP),
        first_weight,
        second_weight,
    )
    back_scratch = [((patches, width), F32), column, column]
    message = ((chunk + 8, LANES), F32)
    grads_late, moved_back, own_back, outs_late, router_late, gain_late = run(
        back_late_kernel,
        [
            token_block + ("far",), message, message, ((2 * chunk, LANES), F32),
            ((slots, width), F32), ((8, width), F32),
        ],
        [token_block, token_block] + back_scratch + [copy_sem, copy_sem],
        600000000,
        15,
        slot_scale,
        flags,
        exchange(parts, DP),
        late_in,
        hidden_late,
        inverse_late,
        logits_late,
        prob_late,
        rows_late,
        late_up,
        columns,
        norm_gain,
        moved,
        rows_early,
        packed,
        cotangent,
    )
    send, kept = run(
        spread_kernel, [single, message], [], 1000000, 3, flags, section_ring(moved_back, -1), own_back
    )
    part, mixed_early_all, pre_grad_early = run(
        expert_back_kernel,
        [single, every_slot, every_hidden],
        [((group, chunk, LANES), F32)],
        70000000,
        4,
        exchange(send, DP),
        slope_early,
        first_weight,
        second_weight,
    )
    last_rows = (2 * local + 1) * chunk
    slot_sums, held_grads = lax.optimization_barrier((exchange(part, DP), grads_late))
    sent_grads = section_ring(held_grads, -1)
    dinput, outs_early, finals = run(
        back_early_kernel,
        [token_block, ((chunk, LANES), F32), ((plane, last_rows, LANES), BF)],
        back_scratch + [((plane, 2 * local * chunk, LANES), F32)],
        600000000,
        13,
        slot_scale,
        slot_sums,
        kept,
        start_in,
        hidden_early,
        inverse_early,
        logits_early,
        prob_early,
        rows_early,
        columns,
        norm_gain,
        router_late,
        gain_late,
    )
    half_rows = (((local + 1) * chunk, LANES), F32)
    kept_sums, given_sums = run(
        plane_kernel, [half_rows, half_rows], [], 1000000, 2, flags, exchange(finals, PLANE)
    )
    (
        given_sums, dinput, slot_early, slot_late, pre_grad_early, pre_grad_late, act_early, act_late,
        mixed_early_all, mixed_late, grads_late,
    ) = lax.optimization_barrier(
        (
            given_sums, dinput, slot_early, slot_late, pre_grad_early, pre_grad_late, act_early, act_late,
            mixed_early_all, mixed_late, grads_late,
        )
    )
    early_up = jnp.where(is_last, cotangent[0, 0], sent_grads).astype(F32)
    grads_early = (early_up + dinput.astype(F32)).astype(BF)
    first_grad = dot_dims(
        jnp.concatenate([slot_early, slot_late], axis=0),
        jnp.concatenate([pre_grad_early, pre_grad_late], axis=0),
        0,
        0,
    )
    second_grad = dot_dims(
        jnp.concatenate([act_early, act_late], axis=0),
        jnp.concatenate([mixed_early_all, mixed_late], axis=0),
        0,
        0,
    )
    taken_sums, section_grads, first_grad, second_grad = lax.optimization_barrier(
        (
            other_half(given_sums), jnp.stack([grads_early, grads_late]), first_grad.astype(BF),
            second_grad.astype(BF),
        )
    )
    router_grad, gain_total, slot_out, slot_grad = run(
        final_kernel,
        [((local, width), BF), ((1, width), F32), ((2, width), BF), ((2, width), BF)],
        [],
        1000000,
        6,
        kept_sums,
        taken_sums,
        weights,
        packed,
        outs_late,
        outs_early,
    )

    return (
        section_grads[None, :, None],
        slot_out[None, :, None],
        slot_grad[None, :, None],
        first_grad[None],
        second_grad[None],
        router_grad.T[None],
        gain_total,
    )


def solution(mesh):
    fine = Mesh(mesh.devices.reshape(mesh.shape["section"], 2, 4, 4), AXES)
    in_specs = (
        P(None, DP, None, None),
        P(None, DP, None, None),
        P("section", DP, None, None),
        P("section", DP, None, None),
        P("section", None),
        P("section"),
        P("section", None, DP),
        P("section", None, DP),
        P("section", DP, None),
    )
    out_specs = (
        P("section", None, DP, None, None),
        P("section", None, DP, None),
        P("section", None, DP, None),
        P("section", None, DP),
        P("section", DP, None),
        P("section", None, DP),
        P("section", None),
    )
    return jax.shard_map(shards, mesh=fine, in_specs=in_specs, out_specs=out_specs, check_vma=False)
```

```python
import jax
import jax.numpy as jnp
from jax import lax
from jax.experimental import pallas as pl
from jax.experimental.pallas import tpu as pltpu
from jax.sharding import Mesh
from jax.sharding import PartitionSpec as P

EPSILON = 1e-06
BF = jnp.bfloat16
F32 = jnp.float32
AXES = ("section", "zh", "y", "x")
DP = ("zh", "y", "x")
PLANE = ("y", "x")
LANES = 128
STEP = 16
VMEM_BYTES = 24 * 1024 * 1024


def dot_dims(left_side, right_side, left_dim, right_dim):
    return lax.dot_general(
        left_side,
        right_side,
        (((left_dim,), (right_dim,)), ((), ())),
        preferred_element_type=F32,
    )


def exchange(chunks, axes):
    return lax.all_to_all(chunks, axes, 0, 0, tiled=True)


def section_shift(block, distance):
    sections = lax.axis_size("section")
    route = [(i, i + distance) for i in range(sections) if 0 <= i + distance < sections]
    return lax.ppermute(block, "section", route)


def other_half(block):
    return lax.ppermute(block, "zh", [(0, 1), (1, 0)])


def section_ring(block, distance):
    sections = lax.axis_size("section")
    return lax.ppermute(block, "section", [(i, (i + distance) % sections) for i in range(sections)])


def run(body, outs, scratch, flops, near, *operands, vmem=VMEM_BYTES):
    def place(index, item):
        if item.ndim == 1:
            return pltpu.SMEM
        return pltpu.VMEM if index < near else pl.ANY

    return pl.pallas_call(
        body,
        out_shape=[jax.ShapeDtypeStruct(item[0], item[1]) for item in outs],
        in_specs=[
            pl.BlockSpec(memory_space=place(index, item)) for index, item in enumerate(operands)
        ],
        out_specs=[
            pl.BlockSpec(memory_space=pltpu.VMEM if len(item) == 2 else pl.ANY) for item in outs
        ],
        scratch_shapes=[
            pltpu.VMEM(*item) if isinstance(item, tuple) else item for item in scratch
        ],
        compiler_params=pltpu.CompilerParams(vmem_limit_bytes=vmem),
        cost_estimate=pl.CostEstimate(flops=flops, bytes_accessed=4000000, transcendentals=0),
    )(*operands)


def to_chunk(row):
    count = row.shape[1] // LANES
    return jnp.concatenate([row[:, k * LANES : (k + 1) * LANES] for k in range(count)], axis=0)


def to_row(chunk):
    return jnp.concatenate([chunk[k : k + 1, :] for k in range(chunk.shape[0])], axis=1)


def to_column(row):
    return jnp.transpose(jnp.broadcast_to(row, (LANES, row.shape[1])))


def stack_rows(rows, count, kind):
    filler = jnp.zeros((count - len(rows), rows[0].shape[1]), F32)
    return jnp.concatenate(list(rows) + [filler], axis=0).astype(kind)


def first_rows(rows):
    return stack_rows(rows, STEP, BF)


def wide_rows(ref, offset, count):
    return jnp.concatenate([ref[:, offset + k, :] for k in range(count)], axis=1)


def put_rows(ref, offset, value):
    for k in range(value.shape[1] // LANES):
        ref[:, offset + k, :] = value[:, k * LANES : (k + 1) * LANES]


def two_parts(row):
    high = row.astype(BF).astype(F32)
    return high, row - high


def lane_sums(value):
    parts = [value[:, k * LANES : (k + 1) * LANES] for k in range(value.shape[1] // LANES)]
    while len(parts) > 1:
        parts = [x + y for x, y in zip(parts[::2], parts[1::2])]
    return parts[0]


def summed(chunks_ref):
    return jnp.sum(chunks_ref[...].astype(F32), axis=0).astype(BF).astype(F32)


def passes(ref, body):
    @pl.loop(0, ref.shape[0] // STEP, unroll=16)
    def _(index):
        body(pl.ds(index * STEP, STEP))


def begin_copy(flag, yes, no, target, sem):
    @pl.when(flag != 0)
    def _():
        pltpu.make_async_copy(yes, target, sem).start()

    @pl.when(flag == 0)
    def _():
        pltpu.make_async_copy(no, target, sem).start()


def end_copy(source, target, sem):
    pltpu.make_async_copy(source, target, sem).wait()


def scaled_weights(weights_ref):
    weights = weights_ref[...].astype(F32)
    total = jnp.sum(weights * weights, axis=1, keepdims=True)
    return weights, lax.rsqrt(total + EPSILON)


def columns_kernel(weights_ref, send_ref):
    weights, inverse = scaled_weights(weights_ref)
    columns = weights * inverse
    rows = [to_chunk(columns[k : k + 1]) for k in range(columns.shape[0])]
    send_ref[...] = jnp.concatenate(rows, axis=0).astype(BF)


def order_kernel(flags_ref, own_ref, other_ref, send_ref):
    own = own_ref[...].astype(F32)
    other = other_ref[...].astype(F32)
    upper = flags_ref[2] != 0
    pair = [jnp.where(upper, other, own), jnp.where(upper, own, other)]
    block = jnp.concatenate(pair, axis=0).astype(BF)
    send_ref[...] = jnp.broadcast_to(block[None], send_ref.shape)


def norm_passes(in_ref, gain, hidden_ref, inverse_ref, sums_ref):
    rate = 1.0 / in_ref.shape[1]
    inverse = lax.rsqrt(jnp.sum(sums_ref[...], axis=1, keepdims=True) * rate + EPSILON)
    inverse_ref[...] = jnp.broadcast_to(inverse, inverse_ref.shape)

    def scale_rows(window):
        wide = in_ref[window, :].astype(F32)
        hidden = (wide * inverse_ref[window, :1] * gain).astype(BF)
        hidden_ref[window, :] = hidden
        hidden_f = hidden.astype(F32)
        sums_ref[window, :] = lane_sums(hidden_f * hidden_f)

    passes(in_ref, scale_rows)
    total = jnp.sum(jnp.transpose(sums_ref[...]), axis=0, keepdims=True)
    return lax.rsqrt(total + EPSILON)


def slot_front(scaled, columns_ref, hidden_ref, length, logits_ref, prob_ref, rows_ref):
    product = dot_dims(columns_ref[...], hidden_ref[...], 1, 1)
    logits = product * scaled
    expo = jnp.exp(logits)
    first = expo[:1]
    norm = jnp.sum(expo, axis=0, keepdims=True)
    combine = first / norm
    spread = first / jnp.sum(first, axis=1, keepdims=True)
    logits_ref[...] = logits
    prob_ref[...] = expo / norm
    rows_ref[...] = stack_rows([length, combine, spread], 8, F32)
    slot = jnp.dot(first_rows([spread]), hidden_ref[...], preferred_element_type=F32)
    return combine, slot[:1]


def mix_rows(combine, upstream):
    mixed = jnp.dot(first_rows(two_parts(combine)), upstream, preferred_element_type=F32)
    return mixed[:1] + mixed[1:2]


def norm_kernel(
    scale_ref, gain_ref, in_ref, hidden_ref, inverse_ref, length_ref, sums_ref
):
    def square_rows(window):
        wide = in_ref[window, :].astype(F32)
        sums_ref[window, :] = lane_sums(wide * wide)

    passes(in_ref, square_rows)
    length = norm_passes(in_ref, gain_ref[...], hidden_ref, inverse_ref, sums_ref)
    length_ref[...] = stack_rows([length, length * scale_ref[0]], 8, F32)


def early_kernel(
    chunks_ref, length_ref, hidden_ref,
    send_ref, columns_ref, logits_ref, prob_ref, rows_ref, wide_ref,
):
    peers = chunks_ref.shape[0]
    chunk = hidden_ref.shape[1] // LANES
    wide_ref[...] = chunks_ref[...].astype(F32)
    local = chunks_ref.shape[1] // (2 * chunk)
    for k in range(local):
        for z in range(2):
            place = (2 * k + z) * peers
            values = wide_rows(wide_ref, (z * local + k) * chunk, chunk)
            columns_ref[place : place + peers] = values.astype(BF)
    _, slot = slot_front(
        length_ref[1:2], columns_ref, hidden_ref, length_ref[:1], logits_ref, prob_ref, rows_ref
    )
    send_ref[...] = jnp.broadcast_to(to_chunk(slot).astype(BF)[None], send_ref.shape)


def join_rows(parts, out_ref):
    count = sum(part.shape[0] for part in parts)
    filler = jnp.zeros((out_ref.shape[0] - count, LANES), F32)
    out_ref[...] = jnp.concatenate([*parts, filler], axis=0)


def pack_kernel(sums_ref, rows_ref, out_ref):
    join_rows([summed(sums_ref), to_chunk(rows_ref[1:2])], out_ref)


def late_kernel(
    scale_ref, flags_ref, base_ref, moved_ref, columns_ref, gain_ref, cotangent_ref, backflow_ref,
    send_ref, in_ref, hidden_ref, inverse_ref, logits_ref, prob_ref, rows_ref, up_ref,
    sums_ref, comb_ref, up_sem,
):
    begin_copy(flags_ref[1], cotangent_ref.at[1, 0], backflow_ref.at[0, 0], up_ref, up_sem)
    chunk = gain_ref.shape[1] // LANES
    out_row = to_row(moved_ref[:chunk])
    before = to_row(moved_ref[chunk : chunk + 2])
    comb_ref[...] = to_column(jnp.where(flags_ref[0] != 0, jnp.zeros_like(before), before))

    def add_rows(window):
        base = base_ref[window, :].astype(F32)
        value = (base + comb_ref[window, :1] * out_row).astype(BF)
        in_ref[window, :] = value
        wide = value.astype(F32)
        sums_ref[window, :] = lane_sums(wide * wide)

    passes(in_ref, add_rows)
    length = norm_passes(in_ref, gain_ref[...], hidden_ref, inverse_ref, sums_ref)
    combine, slot = slot_front(
        scale_ref[0] * length, columns_ref, hidden_ref, length, logits_ref, prob_ref, rows_ref
    )
    end_copy(backflow_ref.at[0, 0], up_ref, up_sem)
    mixed = mix_rows(combine, up_ref[...])
    both = jnp.concatenate([to_chunk(slot), to_chunk(mixed)], axis=0).astype(BF)
    send_ref[...] = jnp.broadcast_to(both[None], send_ref.shape)


def gelu_parts(value):
    rate = 0.7978845608028654
    cube = 0.044715
    bent = jnp.tanh(rate * (value + cube * value * value * value))
    half = 0.5 * (1.0 + bent)
    slope = half + 0.5 * value * (1.0 - bent * bent) * rate * (1.0 + 3.0 * cube * value * value)
    return value * half, slope


def expert_early_kernel(
    slots_ref, first_ref, second_ref, send_ref, slot_ref, act_ref, slope_ref, wide_ref
):
    wide_ref[...] = slots_ref[...].astype(F32)
    slots = wide_rows(wide_ref, 0, slots_ref.shape[1]).astype(BF)
    slot_ref[...] = slots
    value, slope = gelu_parts(jnp.dot(slots, first_ref[...], preferred_element_type=F32))
    act = value.astype(BF)
    act_ref[...] = act
    slope_ref[...] = slope
    put_rows(wide_ref, 0, jnp.dot(act, second_ref[...], preferred_element_type=F32))
    send_ref[...] = wide_ref[...].astype(BF)


def expert_late_kernel(
    pairs_ref, first_ref, second_ref, send_ref, slot_ref, mixed_ref, act_ref, grad_ref, wide_ref
):
    chunk = pairs_ref.shape[1] // 2
    wide_ref[...] = pairs_ref[...].astype(F32)
    slots = wide_rows(wide_ref, 0, chunk).astype(BF)
    mixed = wide_rows(wide_ref, chunk, chunk).astype(BF)
    slot_ref[...] = slots
    mixed_ref[...] = mixed
    value, slope = gelu_parts(jnp.dot(slots, first_ref[...], preferred_element_type=F32))
    act = value.astype(BF)
    act_ref[...] = act
    grad = (dot_dims(mixed, second_ref[...], 1, 1) * slope).astype(BF)
    grad_ref[...] = grad
    put_rows(wide_ref, 0, jnp.dot(act, second_ref[...], preferred_element_type=F32))
    put_rows(wide_ref, chunk, dot_dims(grad, first_ref[...], 1, 1))
    send_ref[...] = wide_ref[...].astype(BF)


def expert_back_kernel(
    mixed_in_ref, slope_ref, first_ref, second_ref, send_ref, mixed_ref, grad_ref, wide_ref
):
    wide_ref[...] = mixed_in_ref[...].astype(F32)
    mixed = wide_rows(wide_ref, 0, mixed_in_ref.shape[1]).astype(BF)
    mixed_ref[...] = mixed
    grad = (dot_dims(mixed, second_ref[...], 1, 1) * slope_ref[...]).astype(BF)
    grad_ref[...] = grad
    put_rows(wide_ref, 0, dot_dims(grad, first_ref[...], 1, 1))
    send_ref[...] = wide_ref[...].astype(BF)


def spread_kernel(flags_ref, moved_ref, own_ref, send_ref, kept_ref):
    block = jnp.where(flags_ref[1] != 0, own_ref[...], moved_ref[...])
    kept_ref[...] = block
    send_ref[...] = jnp.broadcast_to(block[: send_ref.shape[1]].astype(BF)[None], send_ref.shape)


def row_dots(pairs):
    def body(window):
        for ref, row, sums_ref in pairs:
            sums_ref[window, :] = lane_sums(ref[window, :].astype(F32) * row)

    passes(pairs[0][0], body)
    return [jnp.sum(jnp.transpose(sums_ref[...]), axis=0, keepdims=True) for _, _, sums_ref in pairs]


def back_body(
    scale, dcombine, dspread, grad_row, in_ref, hidden_ref, inverse_ref, logits_ref, prob_ref, rows_ref,
    columns_ref, gain_ref, hold_ref, pull_ref, mean_ref, put_grads,
):
    gain = gain_ref[...]
    length = rows_ref[0:1]
    combine = rows_ref[1:2]
    spread = rows_ref[2:3]
    grad_rows = first_rows([grad_row])
    dspread = dspread.astype(BF).astype(F32)
    first_term = spread * (dspread - jnp.sum(dspread * spread, axis=1, keepdims=True))
    mixed = combine * dcombine
    prob = prob_ref[...]
    top = lax.broadcasted_iota(jnp.int32, prob.shape, 0) == 0
    dlogits = jnp.where(top, mixed + first_term, 0.0) - prob * mixed
    dproduct = dlogits * scale * length
    pull = jnp.sum(dlogits * logits_ref[...], axis=0, keepdims=True) * length * length
    pull_ref[...] = to_column(pull)
    dproduct_bf = dproduct.astype(BF)
    hold_ref[...] = dot_dims(
        jnp.concatenate([dproduct_bf, first_rows([spread])], axis=0),
        jnp.concatenate([columns_ref[...], grad_rows], axis=0),
        0,
        0,
    )
    router = jnp.dot(dproduct_bf, hidden_ref[...], preferred_element_type=F32)

    def product_rows(index, total):
        window = pl.ds(index * STEP, STEP)
        dhidden = hold_ref[window, :] - hidden_ref[window, :].astype(F32) * pull_ref[window, :1]
        hold_ref[window, :] = dhidden
        product = dhidden * (in_ref[window, :].astype(F32) * inverse_ref[window, :1])
        mean_ref[window, :] = lane_sums(product * gain)
        return total + product[:8] + product[8:]

    gain_sum = lax.fori_loop(
        0, in_ref.shape[0] // STEP, product_rows, jnp.zeros((8, in_ref.shape[1]), F32), unroll=8
    )
    mean = jnp.sum(mean_ref[...], axis=1, keepdims=True) * (1.0 / in_ref.shape[1])
    mean_ref[...] = jnp.broadcast_to(mean * inverse_ref[...], mean_ref.shape)

    def grad_rows_pass(window):
        inverse = inverse_ref[window, :1]
        through = hold_ref[window, :] * gain
        wide = in_ref[window, :].astype(F32)
        dinput = inverse * (through - wide * mean_ref[window, :1])
        put_grads(window, dinput)

    passes(in_ref, grad_rows_pass)
    return router, gain_sum


def back_late_kernel(
    scale_ref, flags_ref, sums_ref, in_ref, hidden_ref, inverse_ref, logits_ref, prob_ref,
    rows_ref, up_ref, columns_ref, gain_ref, moved_ref, rows_own_ref, packed_ref, cotangent_ref,
    grads_out, moved_out, own_out, outs_ref, router_ref, gain_out,
    own_ref, grads_ref, hold_ref, pull_ref, mean_ref, own_sem, grads_sem,
):
    last = flags_ref[1] != 0

    @pl.when(last)
    def _():
        pltpu.make_async_copy(cotangent_ref.at[0, 0], own_ref, own_sem).start()

    chunk = sums_ref.shape[1] // 2
    total = summed(sums_ref)
    outs_ref[...] = total

    def put_grads(window, dinput):
        grads_ref[window, :] = (up_ref[window, :].astype(F32) + dinput).astype(BF)

    grad_row = to_row(total[chunk:])
    dcombine, dspread = row_dots(
        [(up_ref, to_row(total[:chunk]), pull_ref), (hidden_ref, grad_row, mean_ref)]
    )
    router, gain_sum = back_body(
        scale_ref[0], dcombine, dspread, grad_row, in_ref, hidden_ref, inverse_ref, logits_ref,
        prob_ref, rows_ref, columns_ref, gain_ref, hold_ref, pull_ref, mean_ref, put_grads,
    )

    leave = pltpu.make_async_copy(grads_ref, grads_out, grads_sem)
    leave.start()

    def message(combine, out_row, ref, out):
        mixed = to_chunk(mix_rows(combine, ref[...]).astype(BF).astype(F32))
        join_rows([mixed, to_chunk(row_dots([(ref, out_row, mean_ref)])[0])], out)

    combine = to_row(moved_ref[chunk : chunk + 2])
    message(combine, to_row(moved_ref[:chunk]), grads_ref, moved_out)
    router_ref[...] = router
    gain_out[...] = gain_sum
    own_out[...] = jnp.zeros_like(own_out)

    @pl.when(last)
    def _():
        end_copy(cotangent_ref.at[0, 0], own_ref, own_sem)
        message(rows_own_ref[1:2], to_row(packed_ref[:chunk]), own_ref, own_out)

    leave.wait()


def back_early_kernel(
    scale_ref, sums_ref, kept_ref, in_ref, hidden_ref, inverse_ref, logits_ref, prob_ref,
    rows_ref, columns_ref, gain_ref, router_in_ref, gain_in_ref,
    dinput_ref, outs_ref, send_ref, hold_ref, pull_ref, mean_ref, wide_ref,
):
    chunk = sums_ref.shape[1]
    total = summed(sums_ref)
    outs_ref[...] = total

    def put_grads(window, dinput):
        dinput_ref[window, :] = dinput.astype(BF)

    grad_row = to_row(total)
    (dspread,) = row_dots([(hidden_ref, grad_row, mean_ref)])
    router, gain_sum = back_body(
        scale_ref[0], to_row(kept_ref[chunk : chunk + 2]), dspread, grad_row, in_ref, hidden_ref,
        inverse_ref, logits_ref, prob_ref, rows_ref, columns_ref, gain_ref, hold_ref, pull_ref,
        mean_ref, put_grads,
    )
    router = router + router_in_ref[...]
    peers = send_ref.shape[0]
    count = router.shape[0] // peers
    for k in range(count):
        place = (k % 2) * (count // 2) + k // 2
        put_rows(wide_ref, place * chunk, router[k * peers : (k + 1) * peers])
    send_ref[:, : count * chunk, :] = wide_ref[...].astype(BF)
    gain_row = jnp.sum(gain_sum + gain_in_ref[...], axis=0, keepdims=True)
    send_ref[:, count * chunk :, :] = jnp.broadcast_to(
        to_chunk(gain_row).astype(BF)[None], (peers, chunk, LANES)
    )


def plane_kernel(flags_ref, chunks_ref, kept_ref, given_ref):
    total = jnp.sum(chunks_ref[...].astype(F32), axis=0)
    count = chunks_ref.shape[1] - kept_ref.shape[0]
    low, high, gain = total[:count], total[count : 2 * count], total[2 * count :]
    upper = flags_ref[2] != 0
    kept_ref[...] = jnp.concatenate([jnp.where(upper, high, low), gain], axis=0)
    given_ref[...] = jnp.concatenate([jnp.where(upper, low, high), gain], axis=0)


def final_kernel(
    kept_ref, taken_ref, weights_ref, packed_ref, outs_late_ref, outs_early_ref,
    router_ref, gain_ref, slot_out_ref, slot_grad_ref,
):
    weights, inverse = scaled_weights(weights_ref)
    total = kept_ref[...] + taken_ref[...]
    count = weights.shape[0]
    chunk = weights.shape[1] // LANES
    rows = [to_row(total[k * chunk : (k + 1) * chunk]) for k in range(count)]
    pulled = jnp.concatenate(rows, axis=0)
    dots = jnp.sum(pulled * weights, axis=1, keepdims=True)
    router_ref[...] = (inverse * (pulled - weights * (dots * inverse * inverse))).astype(BF)
    gain_ref[...] = to_row(total[count * chunk :])
    late = outs_late_ref[...]
    outs = [to_row(packed_ref[:chunk]), to_row(late[:chunk])]
    grads = [to_row(outs_early_ref[...]), to_row(late[chunk:])]
    slot_out_ref[...] = jnp.concatenate(outs, axis=0).astype(BF)
    slot_grad_ref[...] = jnp.concatenate(grads, axis=0).astype(BF)


def shards(
    tokens,
    cotangent,
    inflow,
    backflow,
    norm_gain,
    slot_scale,
    router_weight,
    expert_in,
    expert_back,
):
    section_index = lax.axis_index("section")
    is_first = section_index == 0
    is_last = section_index == lax.axis_size("section") - 1
    flags = jnp.stack([is_first, is_last, lax.axis_index("zh") == 1]).astype(jnp.int32)
    group = lax.axis_size(DP)
    patches = tokens.shape[2]
    width = tokens.shape[3]
    chunk = width // LANES
    local = router_weight.shape[2]
    slots = local * group
    hidden_units = expert_in.shape[2]
    first_weight = expert_in[0]
    second_weight = expert_back[0]
    weights = router_weight[0].T
    token_block = ((patches, width), BF)
    column = ((patches, LANES), F32)
    table = ((slots, patches), F32)
    rows = ((8, patches), F32)
    single = ((group, chunk, LANES), BF)
    double = ((group, 2 * chunk, LANES), BF)
    every_slot = ((group, width), BF)
    every_hidden = ((group, hidden_units), BF)
    copy_sem = pltpu.SemaphoreType.DMA

    plane = group // 2
    block = run(columns_kernel, [((local * chunk, LANES), BF)], [], 1000000, 1, weights)[0]
    start_in = jnp.where(is_first, tokens[0, 0], inflow[0, 0])
    hidden_early, inverse_early, length_early = run(
        norm_kernel,
        [token_block, column, rows],
        [column],
        30000000,
        3,
        slot_scale,
        norm_gain,
        start_in,
    )
    other, length_early = lax.optimization_barrier((other_half(block), length_early))
    send = run(
        order_kernel,
        [((plane, 2 * local * chunk, LANES), BF)],
        [],
        1000000,
        3,
        flags,
        block,
        other,
    )[0]
    sent_in = section_ring(start_in, 1)
    send, columns, logits_early, prob_early, rows_early = run(
        early_kernel,
        [single, ((slots, width), BF), table, table, rows],
        [((plane, 2 * local * chunk, LANES), F32)],
        300000000,
        3,
        exchange(send, PLANE),
        length_early,
        hidden_early,
    )
    part, slot_early, act_early, slope_early = run(
        expert_early_kernel,
        [single, every_slot, every_hidden, ((group, hidden_units), F32)],
        [((group, chunk, LANES), F32)],
        70000000,
        3,
        exchange(send, DP),
        first_weight,
        second_weight,
    )
    packed = run(
        pack_kernel, [((chunk + 8, LANES), F32)], [], 1000000, 2, exchange(part, DP), rows_early
    )[0]
    moved = section_shift(packed, 1)

    base = jnp.where(is_first, tokens[1, 0], sent_in)
    (
        send, late_in, hidden_late, inverse_late, logits_late, prob_late, rows_late, late_up,
    ) = run(
        late_kernel,
        [double, token_block, token_block, column, table, table, rows, token_block],
        [column, column, copy_sem],
        400000000,
        6,
        slot_scale,
        flags,
        base,
        moved,
        columns,
        norm_gain,
        cotangent,
        backflow,
    )
    parts, slot_late, mixed_late, act_late, pre_grad_late = run(
        expert_late_kernel,
        [double, every_slot, every_slot, every_hidden, every_hidden],
        [((group, 2 * chunk, LANES), F32)],
        140000000,
        3,
        exchange(send, DP),
        first_weight,
        second_weight,
    )
    back_scratch = [((patches, width), F32), column, column]
    message = ((chunk + 8, LANES), F32)
    grads_late, moved_back, own_back, outs_late, router_late, gain_late = run(
        back_late_kernel,
        [
            token_block + ("far",), message, message, ((2 * chunk, LANES), F32),
            ((slots, width), F32), ((8, width), F32),
        ],
        [token_block, token_block] + back_scratch + [copy_sem, copy_sem],
        600000000,
        15,
        slot_scale,
        flags,
        exchange(parts, DP),
        late_in,
        hidden_late,
        inverse_late,
        logits_late,
        prob_late,
        rows_late,
        late_up,
        columns,
        norm_gain,
        moved,
        rows_early,
        packed,
        cotangent,
    )
    send, kept = run(
        spread_kernel, [single, message], [], 1000000, 3, flags, section_ring(moved_back, -1), own_back
    )
    part, mixed_early_all, pre_grad_early = run(
        expert_back_kernel,
        [single, every_slot, every_hidden],
        [((group, chunk, LANES), F32)],
        70000000,
        4,
        exchange(send, DP),
        slope_early,
        first_weight,
        second_weight,
    )
    last_rows = (2 * local + 1) * chunk
    slot_sums, held_grads = lax.optimization_barrier((exchange(part, DP), grads_late))
    sent_grads = section_ring(held_grads, -1)
    dinput, outs_early, finals = run(
        back_early_kernel,
        [token_block, ((chunk, LANES), F32), ((plane, last_rows, LANES), BF)],
        back_scratch + [((plane, 2 * local * chunk, LANES), F32)],
        600000000,
        13,
        slot_scale,
        slot_sums,
        kept,
        start_in,
        hidden_early,
        inverse_early,
        logits_early,
        prob_early,
        rows_early,
        columns,
        norm_gain,
        router_late,
        gain_late,
    )
    half_rows = (((local + 1) * chunk, LANES), F32)
    kept_sums, given_sums = run(
        plane_kernel, [half_rows, half_rows], [], 1000000, 2, flags, exchange(finals, PLANE)
    )
    (
        given_sums, dinput, slot_early, slot_late, pre_grad_early, pre_grad_late, act_early, act_late,
        mixed_early_all, mixed_late, grads_late,
    ) = lax.optimization_barrier(
        (
            given_sums, dinput, slot_early, slot_late, pre_grad_early, pre_grad_late, act_early, act_late,
            mixed_early_all, mixed_late, grads_late,
        )
    )
    early_up = jnp.where(is_last, cotangent[0, 0], sent_grads).astype(F32)
    grads_early = (early_up + dinput.astype(F32)).astype(BF)
    first_grad = dot_dims(
        jnp.concatenate([slot_early, slot_late], axis=0),
        jnp.concatenate([pre_grad_early, pre_grad_late], axis=0),
        0,
        0,
    )
    second_grad = dot_dims(
        jnp.concatenate([act_early, act_late], axis=0),
        jnp.concatenate([mixed_early_all, mixed_late], axis=0),
        0,
        0,
    )
    taken_sums, section_grads, first_grad, second_grad = lax.optimization_barrier(
        (
            other_half(given_sums), jnp.stack([grads_early, grads_late]), first_grad.astype(BF),
            second_grad.astype(BF),
        )
    )
    router_grad, gain_total, slot_out, slot_grad = run(
        final_kernel,
        [((local, width), BF), ((1, width), F32), ((2, width), BF), ((2, width), BF)],
        [],
        1000000,
        6,
        kept_sums,
        taken_sums,
        weights,
        packed,
        outs_late,
        outs_early,
    )

    return (
        section_grads[None, :, None],
        slot_out[None, :, None],
        slot_grad[None, :, None],
        first_grad[None],
        second_grad[None],
        router_grad.T[None],
        gain_total,
    )


def solution(mesh):
    fine = Mesh(mesh.devices.reshape(mesh.shape["section"], 2, 4, 4), AXES)
    in_specs = (
        P(None, DP, None, None),
        P(None, DP, None, None),
        P("section", DP, None, None),
        P("section", DP, None, None),
        P("section", None),
        P("section"),
        P("section", None, DP),
        P("section", None, DP),
        P("section", DP, None),
    )
    out_specs = (
        P("section", None, DP, None, None),
        P("section", None, DP, None),
        P("section", None, DP, None),
        P("section", None, DP),
        P("section", DP, None),
        P("section", None, DP),
        P("section", None),
    )
    return jax.shard_map(shards, mesh=fine, in_specs=in_specs, out_specs=out_specs, check_vma=False)
```

```python
import jax
import jax.numpy as jnp
from jax import lax
from jax.experimental import pallas as pl
from jax.experimental.pallas import tpu as pltpu
from jax.sharding import Mesh
from jax.sharding import PartitionSpec as P

EPSILON = 1e-06
BF = jnp.bfloat16
F32 = jnp.float32
AXES = ("section", "zh", "y", "x")
DP = ("zh", "y", "x")
PLANE = ("y", "x")
LANES = 128
STEP = 16
VMEM_BYTES = 24 * 1024 * 1024


def dot_dims(left_side, right_side, left_dim, right_dim):
    return lax.dot_general(
        left_side,
        right_side,
        (((left_dim,), (right_dim,)), ((), ())),
        preferred_element_type=F32,
    )


def exchange(chunks, axes):
    return lax.all_to_all(chunks, axes, 0, 0, tiled=True)


def section_shift(block, distance):
    sections = lax.axis_size("section")
    route = [(i, i + distance) for i in range(sections) if 0 <= i + distance < sections]
    return lax.ppermute(block, "section", route)


def other_half(block):
    return lax.ppermute(block, "zh", [(0, 1), (1, 0)])


def section_ring(block, distance):
    sections = lax.axis_size("section")
    return lax.ppermute(block, "section", [(i, (i + distance) % sections) for i in range(sections)])


def run(body, outs, scratch, flops, near, *operands, vmem=VMEM_BYTES):
    def place(index, item):
        if item.ndim == 1:
            return pltpu.SMEM
        return pltpu.VMEM if index < near else pl.ANY

    return pl.pallas_call(
        body,
        out_shape=[jax.ShapeDtypeStruct(item[0], item[1]) for item in outs],
        in_specs=[
            pl.BlockSpec(memory_space=place(index, item)) for index, item in enumerate(operands)
        ],
        out_specs=[
            pl.BlockSpec(memory_space=pltpu.VMEM if len(item) == 2 else pl.ANY) for item in outs
        ],
        scratch_shapes=[
            pltpu.VMEM(*item) if isinstance(item, tuple) else item for item in scratch
        ],
        compiler_params=pltpu.CompilerParams(vmem_limit_bytes=vmem),
        cost_estimate=pl.CostEstimate(flops=flops, bytes_accessed=4000000, transcendentals=0),
    )(*operands)


def to_chunk(row):
    count = row.shape[1] // LANES
    return jnp.concatenate([row[:, k * LANES : (k + 1) * LANES] for k in range(count)], axis=0)


def to_row(chunk):
    return jnp.concatenate([chunk[k : k + 1, :] for k in range(chunk.shape[0])], axis=1)


def to_column(row):
    return jnp.transpose(jnp.broadcast_to(row, (LANES, row.shape[1])))


def stack_rows(rows, count, kind):
    filler = jnp.zeros((count - len(rows), rows[0].shape[1]), F32)
    return jnp.concatenate(list(rows) + [filler], axis=0).astype(kind)


def first_rows(rows):
    return stack_rows(rows, STEP, BF)


def wide_rows(ref, offset, count):
    return jnp.concatenate([ref[:, offset + k, :] for k in range(count)], axis=1)


def put_rows(ref, offset, value):
    for k in range(value.shape[1] // LANES):
        ref[:, offset + k, :] = value[:, k * LANES : (k + 1) * LANES]


def two_parts(row):
    high = row.astype(BF).astype(F32)
    return high, row - high


def lane_sums(value):
    parts = [value[:, k * LANES : (k + 1) * LANES] for k in range(value.shape[1] // LANES)]
    while len(parts) > 1:
        parts = [x + y for x, y in zip(parts[::2], parts[1::2])]
    return parts[0]


def summed(chunks_ref):
    return jnp.sum(chunks_ref[...].astype(F32), axis=0).astype(BF).astype(F32)


def passes(ref, body):
    @pl.loop(0, ref.shape[0] // STEP, unroll=16)
    def _(index):
        body(pl.ds(index * STEP, STEP))


def begin_copy(flag, yes, no, target, sem):
    @pl.when(flag != 0)
    def _():
        pltpu.make_async_copy(yes, target, sem).start()

    @pl.when(flag == 0)
    def _():
        pltpu.make_async_copy(no, target, sem).start()


def end_copy(source, target, sem):
    pltpu.make_async_copy(source, target, sem).wait()


def scaled_weights(weights_ref):
    weights = weights_ref[...].astype(F32)
    total = jnp.sum(weights * weights, axis=1, keepdims=True)
    return weights, lax.rsqrt(total + EPSILON)


def columns_kernel(weights_ref, send_ref):
    weights, inverse = scaled_weights(weights_ref)
    columns = weights * inverse
    rows = [to_chunk(columns[k : k + 1]) for k in range(columns.shape[0])]
    send_ref[...] = jnp.concatenate(rows, axis=0).astype(BF)


def order_kernel(flags_ref, own_ref, other_ref, send_ref):
    own = own_ref[...].astype(F32)
    other = other_ref[...].astype(F32)
    upper = flags_ref[2] != 0
    pair = [jnp.where(upper, other, own), jnp.where(upper, own, other)]
    block = jnp.concatenate(pair, axis=0).astype(BF)
    send_ref[...] = jnp.broadcast_to(block[None], send_ref.shape)


def norm_passes(in_ref, gain, hidden_ref, inverse_ref, sums_ref):
    rate = 1.0 / in_ref.shape[1]
    inverse = lax.rsqrt(jnp.sum(sums_ref[...], axis=1, keepdims=True) * rate + EPSILON)
    inverse_ref[...] = jnp.broadcast_to(inverse, inverse_ref.shape)

    def scale_rows(window):
        wide = in_ref[window, :].astype(F32)
        hidden = (wide * inverse_ref[window, :1] * gain).astype(BF)
        hidden_ref[window, :] = hidden
        hidden_f = hidden.astype(F32)
        sums_ref[window, :] = lane_sums(hidden_f * hidden_f)

    passes(in_ref, scale_rows)
    total = jnp.sum(jnp.transpose(sums_ref[...]), axis=0, keepdims=True)
    return lax.rsqrt(total + EPSILON)


def slot_front(scaled, columns_ref, hidden_ref, length, logits_ref, prob_ref, rows_ref):
    product = dot_dims(columns_ref[...], hidden_ref[...], 1, 1)
    logits = product * scaled
    expo = jnp.exp(logits)
    first = expo[:1]
    norm = jnp.sum(expo, axis=0, keepdims=True)
    combine = first / norm
    spread = first / jnp.sum(first, axis=1, keepdims=True)
    logits_ref[...] = logits
    prob_ref[...] = expo / norm
    rows_ref[...] = stack_rows([length, combine, spread], 8, F32)
    slot = jnp.dot(first_rows([spread]), hidden_ref[...], preferred_element_type=F32)
    return combine, slot[:1]


def mix_rows(combine, upstream):
    mixed = jnp.dot(first_rows(two_parts(combine)), upstream, preferred_element_type=F32)
    return mixed[:1] + mixed[1:2]


def norm_kernel(
    scale_ref, gain_ref, in_ref, hidden_ref, inverse_ref, length_ref, sums_ref
):
    def square_rows(window):
        wide = in_ref[window, :].astype(F32)
        sums_ref[window, :] = lane_sums(wide * wide)

    passes(in_ref, square_rows)
    length = norm_passes(in_ref, gain_ref[...], hidden_ref, inverse_ref, sums_ref)
    length_ref[...] = stack_rows([length, length * scale_ref[0]], 8, F32)


def early_kernel(
    chunks_ref, length_ref, hidden_ref,
    send_ref, columns_ref, logits_ref, prob_ref, rows_ref, wide_ref,
):
    peers = chunks_ref.shape[0]
    chunk = hidden_ref.shape[1] // LANES
    wide_ref[...] = chunks_ref[...].astype(F32)
    local = chunks_ref.shape[1] // (2 * chunk)
    for k in range(local):
        for z in range(2):
            place = (2 * k + z) * peers
            values = wide_rows(wide_ref, (z * local + k) * chunk, chunk)
            columns_ref[place : place + peers] = values.astype(BF)
    _, slot = slot_front(
        length_ref[1:2], columns_ref, hidden_ref, length_ref[:1], logits_ref, prob_ref, rows_ref
    )
    send_ref[...] = jnp.broadcast_to(to_chunk(slot).astype(BF)[None], send_ref.shape)


def join_rows(parts, out_ref):
    count = sum(part.shape[0] for part in parts)
    filler = jnp.zeros((out_ref.shape[0] - count, LANES), F32)
    out_ref[...] = jnp.concatenate([*parts, filler], axis=0)


def pack_kernel(sums_ref, rows_ref, out_ref):
    join_rows([summed(sums_ref), to_chunk(rows_ref[1:2])], out_ref)


def late_kernel(
    scale_ref, flags_ref, base_ref, moved_ref, columns_ref, gain_ref, cotangent_ref, backflow_ref,
    send_ref, in_ref, hidden_ref, inverse_ref, logits_ref, prob_ref, rows_ref, up_ref,
    sums_ref, comb_ref, up_sem,
):
    begin_copy(flags_ref[1], cotangent_ref.at[1, 0], backflow_ref.at[0, 0], up_ref, up_sem)
    chunk = gain_ref.shape[1] // LANES
    out_row = to_row(moved_ref[:chunk])
    before = to_row(moved_ref[chunk : chunk + 2])
    comb_ref[...] = to_column(jnp.where(flags_ref[0] != 0, jnp.zeros_like(before), before))

    def add_rows(window):
        base = base_ref[window, :].astype(F32)
        value = (base + comb_ref[window, :1] * out_row).astype(BF)
        in_ref[window, :] = value
        wide = value.astype(F32)
        sums_ref[window, :] = lane_sums(wide * wide)

    passes(in_ref, add_rows)
    length = norm_passes(in_ref, gain_ref[...], hidden_ref, inverse_ref, sums_ref)
    combine, slot = slot_front(
        scale_ref[0] * length, columns_ref, hidden_ref, length, logits_ref, prob_ref, rows_ref
    )
    end_copy(backflow_ref.at[0, 0], up_ref, up_sem)
    mixed = mix_rows(combine, up_ref[...])
    both = jnp.concatenate([to_chunk(slot), to_chunk(mixed)], axis=0).astype(BF)
    send_ref[...] = jnp.broadcast_to(both[None], send_ref.shape)


def gelu_parts(value):
    rate = 0.7978845608028654
    cube = 0.044715
    bent = jnp.tanh(rate * (value + cube * value * value * value))
    half = 0.5 * (1.0 + bent)
    slope = half + 0.5 * value * (1.0 - bent * bent) * rate * (1.0 + 3.0 * cube * value * value)
    return value * half, slope


def expert_early_kernel(
    slots_ref, first_ref, second_ref, send_ref, slot_ref, act_ref, slope_ref, wide_ref
):
    wide_ref[...] = slots_ref[...].astype(F32)
    slots = wide_rows(wide_ref, 0, slots_ref.shape[1]).astype(BF)
    slot_ref[...] = slots
    value, slope = gelu_parts(jnp.dot(slots, first_ref[...], preferred_element_type=F32))
    act = value.astype(BF)
    act_ref[...] = act
    slope_ref[...] = slope
    put_rows(wide_ref, 0, jnp.dot(act, second_ref[...], preferred_element_type=F32))
    send_ref[...] = wide_ref[...].astype(BF)


def expert_late_kernel(
    pairs_ref, first_ref, second_ref, send_ref, slot_ref, mixed_ref, act_ref, grad_ref, wide_ref
):
    chunk = pairs_ref.shape[1] // 2
    wide_ref[...] = pairs_ref[...].astype(F32)
    slots = wide_rows(wide_ref, 0, chunk).astype(BF)
    mixed = wide_rows(wide_ref, chunk, chunk).astype(BF)
    slot_ref[...] = slots
    mixed_ref[...] = mixed
    value, slope = gelu_parts(jnp.dot(slots, first_ref[...], preferred_element_type=F32))
    act = value.astype(BF)
    act_ref[...] = act
    grad = (dot_dims(mixed, second_ref[...], 1, 1) * slope).astype(BF)
    grad_ref[...] = grad
    put_rows(wide_ref, 0, jnp.dot(act, second_ref[...], preferred_element_type=F32))
    put_rows(wide_ref, chunk, dot_dims(grad, first_ref[...], 1, 1))
    send_ref[...] = wide_ref[...].astype(BF)


def expert_back_kernel(
    mixed_in_ref, slope_ref, first_ref, second_ref, send_ref, mixed_ref, grad_ref, wide_ref
):
    wide_ref[...] = mixed_in_ref[...].astype(F32)
    mixed = wide_rows(wide_ref, 0, mixed_in_ref.shape[1]).astype(BF)
    mixed_ref[...] = mixed
    grad = (dot_dims(mixed, second_ref[...], 1, 1) * slope_ref[...]).astype(BF)
    grad_ref[...] = grad
    put_rows(wide_ref, 0, dot_dims(grad, first_ref[...], 1, 1))
    send_ref[...] = wide_ref[...].astype(BF)


def spread_kernel(flags_ref, moved_ref, own_ref, send_ref, kept_ref):
    block = jnp.where(flags_ref[1] != 0, own_ref[...], moved_ref[...])
    kept_ref[...] = block
    send_ref[...] = jnp.broadcast_to(block[: send_ref.shape[1]].astype(BF)[None], send_ref.shape)


def row_dots(pairs):
    def body(window):
        for ref, row, sums_ref in pairs:
            sums_ref[window, :] = lane_sums(ref[window, :].astype(F32) * row)

    passes(pairs[0][0], body)
    return [jnp.sum(jnp.transpose(sums_ref[...]), axis=0, keepdims=True) for _, _, sums_ref in pairs]


def back_body(
    scale, dcombine, dspread, grad_row, in_ref, hidden_ref, inverse_ref, logits_ref, prob_ref, rows_ref,
    columns_ref, gain_ref, hold_ref, pull_ref, mean_ref, put_grads,
):
    gain = gain_ref[...]
    length = rows_ref[0:1]
    combine = rows_ref[1:2]
    spread = rows_ref[2:3]
    grad_rows = first_rows([grad_row])
    dspread = dspread.astype(BF).astype(F32)
    first_term = spread * (dspread - jnp.sum(dspread * spread, axis=1, keepdims=True))
    mixed = combine * dcombine
    prob = prob_ref[...]
    top = lax.broadcasted_iota(jnp.int32, prob.shape, 0) == 0
    dlogits = jnp.where(top, mixed + first_term, 0.0) - prob * mixed
    dproduct = dlogits * scale * length
    pull = jnp.sum(dlogits * logits_ref[...], axis=0, keepdims=True) * length * length
    pull_ref[...] = to_column(pull)
    dproduct_bf = dproduct.astype(BF)
    hold_ref[...] = dot_dims(
        jnp.concatenate([dproduct_bf, first_rows([spread])], axis=0),
        jnp.concatenate([columns_ref[...], grad_rows], axis=0),
        0,
        0,
    )
    router = jnp.dot(dproduct_bf, hidden_ref[...], preferred_element_type=F32)

    def product_rows(index, total):
        window = pl.ds(index * STEP, STEP)
        dhidden = hold_ref[window, :] - hidden_ref[window, :].astype(F32) * pull_ref[window, :1]
        hold_ref[window, :] = dhidden
        product = dhidden * (in_ref[window, :].astype(F32) * inverse_ref[window, :1])
        mean_ref[window, :] = lane_sums(product * gain)
        return total + product[:8] + product[8:]

    gain_sum = lax.fori_loop(
        0, in_ref.shape[0] // STEP, product_rows, jnp.zeros((8, in_ref.shape[1]), F32), unroll=8
    )
    mean = jnp.sum(mean_ref[...], axis=1, keepdims=True) * (1.0 / in_ref.shape[1])
    mean_ref[...] = jnp.broadcast_to(mean * inverse_ref[...], mean_ref.shape)

    def grad_rows_pass(window):
        inverse = inverse_ref[window, :1]
        through = hold_ref[window, :] * gain
        wide = in_ref[window, :].astype(F32)
        dinput = inverse * (through - wide * mean_ref[window, :1])
        put_grads(window, dinput)

    passes(in_ref, grad_rows_pass)
    return router, gain_sum


def back_late_kernel(
    scale_ref, flags_ref, sums_ref, in_ref, hidden_ref, inverse_ref, logits_ref, prob_ref,
    rows_ref, up_ref, columns_ref, gain_ref, moved_ref, rows_own_ref, packed_ref, cotangent_ref,
    grads_out, moved_out, own_out, outs_ref, router_ref, gain_out,
    own_ref, grads_ref, hold_ref, pull_ref, mean_ref, own_sem, grads_sem,
):
    last = flags_ref[1] != 0

    @pl.when(last)
    def _():
        pltpu.make_async_copy(cotangent_ref.at[0, 0], own_ref, own_sem).start()

    chunk = sums_ref.shape[1] // 2
    total = summed(sums_ref)
    outs_ref[...] = total

    def put_grads(window, dinput):
        grads_ref[window, :] = (up_ref[window, :].astype(F32) + dinput).astype(BF)

    grad_row = to_row(total[chunk:])
    dcombine, dspread = row_dots(
        [(up_ref, to_row(total[:chunk]), pull_ref), (hidden_ref, grad_row, mean_ref)]
    )
    router, gain_sum = back_body(
        scale_ref[0], dcombine, dspread, grad_row, in_ref, hidden_ref, inverse_ref, logits_ref,
        prob_ref, rows_ref, columns_ref, gain_ref, hold_ref, pull_ref, mean_ref, put_grads,
    )

    leave = pltpu.make_async_copy(grads_ref, grads_out, grads_sem)
    leave.start()

    def message(combine, out_row, ref, out):
        mixed = to_chunk(mix_rows(combine, ref[...]).astype(BF).astype(F32))
        join_rows([mixed, to_chunk(row_dots([(ref, out_row, mean_ref)])[0])], out)

    combine = to_row(moved_ref[chunk : chunk + 2])
    message(combine, to_row(moved_ref[:chunk]), grads_ref, moved_out)
    router_ref[...] = router
    gain_out[...] = gain_sum
    own_out[...] = jnp.zeros_like(own_out)

    @pl.when(last)
    def _():
        end_copy(cotangent_ref.at[0, 0], own_ref, own_sem)
        message(rows_own_ref[1:2], to_row(packed_ref[:chunk]), own_ref, own_out)

    leave.wait()


def back_early_kernel(
    scale_ref, sums_ref, kept_ref, in_ref, hidden_ref, inverse_ref, logits_ref, prob_ref,
    rows_ref, columns_ref, gain_ref, router_in_ref, gain_in_ref,
    dinput_ref, outs_ref, send_ref, hold_ref, pull_ref, mean_ref, wide_ref,
):
    chunk = sums_ref.shape[1]
    total = summed(sums_ref)
    outs_ref[...] = total

    def put_grads(window, dinput):
        dinput_ref[window, :] = dinput.astype(BF)

    grad_row = to_row(total)
    (dspread,) = row_dots([(hidden_ref, grad_row, mean_ref)])
    router, gain_sum = back_body(
        scale_ref[0], to_row(kept_ref[chunk : chunk + 2]), dspread, grad_row, in_ref, hidden_ref,
        inverse_ref, logits_ref, prob_ref, rows_ref, columns_ref, gain_ref, hold_ref, pull_ref,
        mean_ref, put_grads,
    )
    router = router + router_in_ref[...]
    peers = send_ref.shape[0]
    count = router.shape[0] // peers
    for k in range(count):
        place = (k % 2) * (count // 2) + k // 2
        put_rows(wide_ref, place * chunk, router[k * peers : (k + 1) * peers])
    send_ref[:, : count * chunk, :] = wide_ref[...].astype(BF)
    gain_row = jnp.sum(gain_sum + gain_in_ref[...], axis=0, keepdims=True)
    send_ref[:, count * chunk :, :] = jnp.broadcast_to(
        to_chunk(gain_row).astype(BF)[None], (peers, chunk, LANES)
    )


def plane_kernel(flags_ref, chunks_ref, kept_ref, given_ref):
    total = jnp.sum(chunks_ref[...].astype(F32), axis=0)
    count = chunks_ref.shape[1] - kept_ref.shape[0]
    low, high, gain = total[:count], total[count : 2 * count], total[2 * count :]
    upper = flags_ref[2] != 0
    kept_ref[...] = jnp.concatenate([jnp.where(upper, high, low), gain], axis=0)
    given = jnp.concatenate([jnp.where(upper, low, high), gain], axis=0)
    given_ref[...] = given.astype(BF)


def final_kernel(
    kept_ref, taken_ref, weights_ref, packed_ref, outs_late_ref, outs_early_ref,
    router_ref, gain_ref, slot_out_ref, slot_grad_ref,
):
    weights, inverse = scaled_weights(weights_ref)
    total = kept_ref[...] + taken_ref[...].astype(F32)
    count = weights.shape[0]
    chunk = weights.shape[1] // LANES
    rows = [to_row(total[k * chunk : (k + 1) * chunk]) for k in range(count)]
    pulled = jnp.concatenate(rows, axis=0)
    dots = jnp.sum(pulled * weights, axis=1, keepdims=True)
    router_ref[...] = (inverse * (pulled - weights * (dots * inverse * inverse))).astype(BF)
    gain_ref[...] = to_row(total[count * chunk :])
    late = outs_late_ref[...]
    outs = [to_row(packed_ref[:chunk]), to_row(late[:chunk])]
    grads = [to_row(outs_early_ref[...]), to_row(late[chunk:])]
    slot_out_ref[...] = jnp.concatenate(outs, axis=0).astype(BF)
    slot_grad_ref[...] = jnp.concatenate(grads, axis=0).astype(BF)


def shards(
    tokens,
    cotangent,
    inflow,
    backflow,
    norm_gain,
    slot_scale,
    router_weight,
    expert_in,
    expert_back,
):
    section_index = lax.axis_index("section")
    is_first = section_index == 0
    is_last = section_index == lax.axis_size("section") - 1
    flags = jnp.stack([is_first, is_last, lax.axis_index("zh") == 1]).astype(jnp.int32)
    group = lax.axis_size(DP)
    patches = tokens.shape[2]
    width = tokens.shape[3]
    chunk = width // LANES
    local = router_weight.shape[2]
    slots = local * group
    hidden_units = expert_in.shape[2]
    first_weight = expert_in[0]
    second_weight = expert_back[0]
    weights = router_weight[0].T
    token_block = ((patches, width), BF)
    column = ((patches, LANES), F32)
    table = ((slots, patches), F32)
    rows = ((8, patches), F32)
    single = ((group, chunk, LANES), BF)
    double = ((group, 2 * chunk, LANES), BF)
    every_slot = ((group, width), BF)
    every_hidden = ((group, hidden_units), BF)
    copy_sem = pltpu.SemaphoreType.DMA

    plane = group // 2
    block = run(columns_kernel, [((local * chunk, LANES), BF)], [], 1000000, 1, weights)[0]
    start_in = jnp.where(is_first, tokens[0, 0], inflow[0, 0])
    hidden_early, inverse_early, length_early = run(
        norm_kernel,
        [token_block, column, rows],
        [column],
        30000000,
        3,
        slot_scale,
        norm_gain,
        start_in,
    )
    other, length_early = lax.optimization_barrier((other_half(block), length_early))
    send = run(
        order_kernel,
        [((plane, 2 * local * chunk, LANES), BF)],
        [],
        1000000,
        3,
        flags,
        block,
        other,
    )[0]
    sent_in = section_ring(start_in, 1)
    send, columns, logits_early, prob_early, rows_early = run(
        early_kernel,
        [single, ((slots, width), BF), table, table, rows],
        [((plane, 2 * local * chunk, LANES), F32)],
        300000000,
        3,
        exchange(send, PLANE),
        length_early,
        hidden_early,
    )
    part, slot_early, act_early, slope_early = run(
        expert_early_kernel,
        [single, every_slot, every_hidden, ((group, hidden_units), F32)],
        [((group, chunk, LANES), F32)],
        70000000,
        3,
        exchange(send, DP),
        first_weight,
        second_weight,
    )
    packed = run(
        pack_kernel, [((chunk + 8, LANES), F32)], [], 1000000, 2, exchange(part, DP), rows_early
    )[0]
    moved = section_shift(packed, 1)

    base = jnp.where(is_first, tokens[1, 0], sent_in)
    (
        send, late_in, hidden_late, inverse_late, logits_late, prob_late, rows_late, late_up,
    ) = run(
        late_kernel,
        [double, token_block, token_block, column, table, table, rows, token_block],
        [column, column, copy_sem],
        400000000,
        6,
        slot_scale,
        flags,
        base,
        moved,
        columns,
        norm_gain,
        cotangent,
        backflow,
    )
    parts, slot_late, mixed_late, act_late, pre_grad_late = run(
        expert_late_kernel,
        [double, every_slot, every_slot, every_hidden, every_hidden],
        [((group, 2 * chunk, LANES), F32)],
        140000000,
        3,
        exchange(send, DP),
        first_weight,
        second_weight,
    )
    back_scratch = [((patches, width), F32), column, column]
    message = ((chunk + 8, LANES), F32)
    grads_late, moved_back, own_back, outs_late, router_late, gain_late = run(
        back_late_kernel,
        [
            token_block + ("far",), message, message, ((2 * chunk, LANES), F32),
            ((slots, width), F32), ((8, width), F32),
        ],
        [token_block, token_block] + back_scratch + [copy_sem, copy_sem],
        600000000,
        15,
        slot_scale,
        flags,
        exchange(parts, DP),
        late_in,
        hidden_late,
        inverse_late,
        logits_late,
        prob_late,
        rows_late,
        late_up,
        columns,
        norm_gain,
        moved,
        rows_early,
        packed,
        cotangent,
    )
    send, kept = run(
        spread_kernel, [single, message], [], 1000000, 3, flags, section_ring(moved_back, -1), own_back
    )
    part, mixed_early_all, pre_grad_early = run(
        expert_back_kernel,
        [single, every_slot, every_hidden],
        [((group, chunk, LANES), F32)],
        70000000,
        4,
        exchange(send, DP),
        slope_early,
        first_weight,
        second_weight,
    )
    last_rows = (2 * local + 1) * chunk
    slot_sums, held_grads = lax.optimization_barrier((exchange(part, DP), grads_late))
    sent_grads = section_ring(held_grads, -1)
    dinput, outs_early, finals = run(
        back_early_kernel,
        [token_block, ((chunk, LANES), F32), ((plane, last_rows, LANES), BF)],
        back_scratch + [((plane, 2 * local * chunk, LANES), F32)],
        600000000,
        13,
        slot_scale,
        slot_sums,
        kept,
        start_in,
        hidden_early,
        inverse_early,
        logits_early,
        prob_early,
        rows_early,
        columns,
        norm_gain,
        router_late,
        gain_late,
    )
    half_rows = (((local + 1) * chunk, LANES), F32)
    kept_sums, given_sums = run(
        plane_kernel, [half_rows, (half_rows[0], BF)], [], 1000000, 2, flags, exchange(finals, PLANE)
    )
    (
        given_sums, dinput, slot_early, slot_late, pre_grad_early, pre_grad_late, act_early, act_late,
        mixed_early_all, mixed_late, grads_late,
    ) = lax.optimization_barrier(
        (
            given_sums, dinput, slot_early, slot_late, pre_grad_early, pre_grad_late, act_early, act_late,
            mixed_early_all, mixed_late, grads_late,
        )
    )
    early_up = jnp.where(is_last, cotangent[0, 0], sent_grads).astype(F32)
    grads_early = (early_up + dinput.astype(F32)).astype(BF)
    first_grad = dot_dims(
        jnp.concatenate([slot_early, slot_late], axis=0),
        jnp.concatenate([pre_grad_early, pre_grad_late], axis=0),
        0,
        0,
    )
    second_grad = dot_dims(
        jnp.concatenate([act_early, act_late], axis=0),
        jnp.concatenate([mixed_early_all, mixed_late], axis=0),
        0,
        0,
    )
    taken_sums, section_grads, first_grad, second_grad = lax.optimization_barrier(
        (
            other_half(given_sums), jnp.stack([grads_early, grads_late]), first_grad.astype(BF),
            second_grad.astype(BF),
        )
    )
    router_grad, gain_total, slot_out, slot_grad = run(
        final_kernel,
        [((local, width), BF), ((1, width), F32), ((2, width), BF), ((2, width), BF)],
        [],
        1000000,
        6,
        kept_sums,
        taken_sums,
        weights,
        packed,
        outs_late,
        outs_early,
    )

    return (
        section_grads[None, :, None],
        slot_out[None, :, None],
        slot_grad[None, :, None],
        first_grad[None],
        second_grad[None],
        router_grad.T[None],
        gain_total,
    )


def solution(mesh):
    fine = Mesh(mesh.devices.reshape(mesh.shape["section"], 2, 4, 4), AXES)
    in_specs = (
        P(None, DP, None, None),
        P(None, DP, None, None),
        P("section", DP, None, None),
        P("section", DP, None, None),
        P("section", None),
        P("section"),
        P("section", None, DP),
        P("section", None, DP),
        P("section", DP, None),
    )
    out_specs = (
        P("section", None, DP, None, None),
        P("section", None, DP, None),
        P("section", None, DP, None),
        P("section", None, DP),
        P("section", DP, None),
        P("section", None, DP),
        P("section", None),
    )
    return jax.shard_map(shards, mesh=fine, in_specs=in_specs, out_specs=out_specs, check_vma=False)
```
